32 devices in a mesh: dp: 2 (over x), fsdp: 16 (over z, y, core).
Axes of the slice: x: 2, y: 2, z: 4, core: 2. Of those that a mesh axis runs over, the one named last changes fastest.
Arguments:
- source: bfloat16 [8192, 512], P(('dp', 'fsdp')), may hold values from -6 to 6
- first_in: bfloat16 [8192, 512], P(('dp', 'fsdp')), may hold values from -6 to 6
- second_in: bfloat16 [8192, 512], P(('dp', 'fsdp')), may hold values from -6 to 6
- cot_first: bfloat16 [8192, 512], P(('dp', 'fsdp')), may hold values from -6 to 6
- cot_second: bfloat16 [8192, 512], P(('dp', 'fsdp')), may hold values from -6 to 6
- src_lengths: int32 [32, 8], P(('dp', 'fsdp')), may hold values from 1 to 128, 256 in all within a row
- tgt_lengths: int32 [32, 8], P(('dp', 'fsdp')), may hold values from 1 to 128, 256 in all within a row
- enc_attn_in: bfloat16 [512, 1536], P('fsdp'), may hold values from -0.25 to 0.25
- enc_attn_out: bfloat16 [512, 512], P('fsdp'), may hold values from -0.75 to 0.75
- enc_ffn_in: bfloat16 [512, 2048], P('fsdp'), may hold values from -0.25 to 0.25
- enc_ffn_out: bfloat16 [2048, 512], P('fsdp'), may hold values from -0.125 to 0.125
- enc_gain: bfloat16 [2, 512], P(None, 'fsdp'), may hold values from 0.5 to 1.5
- enc_bias: bfloat16 [2, 512], P(None, 'fsdp'), may hold values from -3 to 3
- dec_self_in: bfloat16 [512, 1536], P('fsdp'), may hold values from -0.25 to 0.25
- dec_self_out: bfloat16 [512, 512], P('fsdp'), may hold values from -0.75 to 0.75
- dec_cross_q: bfloat16 [512, 512], P('fsdp'), may hold values from -0.25 to 0.25
- dec_cross_kv: bfloat16 [512, 1024], P('fsdp'), may hold values from -0.25 to 0.25
- dec_cross_out: bfloat16 [512, 512], P('fsdp'), may hold values from -0.75 to 0.75
- dec_ffn_in: bfloat16 [512, 2048], P('fsdp'), may hold values from -0.25 to 0.25
- dec_ffn_out: bfloat16 [2048, 512], P('fsdp'), may hold values from -0.125 to 0.125
- dec_gain: bfloat16 [3, 512], P(None, 'fsdp'), may hold values from 0.5 to 1.5
- dec_bias: bfloat16 [3, 512], P(None, 'fsdp'), may hold values from -3 to 3
Outputs:
- first_out: bfloat16 [8192, 512], P(('dp', 'fsdp'))
- second_out: bfloat16 [8192, 512], P(('dp', 'fsdp'))
- source_grad: float32 [8192, 512], P(('dp', 'fsdp'))
- first_grad: float32 [8192, 512], P(('dp', 'fsdp'))
- enc_attn_in_grad: float32 [512, 1536], P('fsdp')
- enc_attn_out_grad: float32 [512, 512], P('fsdp')
- enc_ffn_in_grad: float32 [512, 2048], P('fsdp')
- enc_ffn_out_grad: float32 [2048, 512], P('fsdp')
- enc_gain_grad: float32 [2, 512], P(None, 'fsdp')
- enc_bias_grad: float32 [2, 512], P(None, 'fsdp')
- dec_self_in_grad: float32 [512, 1536], P('fsdp')
- dec_self_out_grad: float32 [512, 512], P('fsdp')
- dec_cross_q_grad: float32 [512, 512], P('fsdp')
- dec_cross_kv_grad: float32 [512, 1024], P('fsdp')
- dec_cross_out_grad: float32 [512, 512], P('fsdp')
- dec_ffn_in_grad: float32 [512, 2048], P('fsdp')
- dec_ffn_out_grad: float32 [2048, 512], P('fsdp')
- dec_gain_grad: float32 [3, 512], P(None, 'fsdp')
- dec_bias_grad: float32 [3, 512], P(None, 'fsdp')
The draws below stay inside these ranges and needn't reach their ends.
Inputs may be any that keep to these rules, and one draw needn't show every extreme that they name: `src_lengths`: row r lists in order the lengths of the 8 source sentences that fill tokens r * 256 to (r + 1) * 256 - 1 of source; they sum to 256; sentence k of a row pairs with sentence k of the same row of tgt_lengths. `tgt_lengths`: row r lists in order the lengths of the 8 target sentences that fill tokens r * 256 to (r + 1) * 256 - 1 of first_in, second_in and the cotangents; they sum to 256.
All inputs are finite; a program needn't handle non-finite values.
Results may differ from the reference program's by a relative error of at most 0.029.
Values may be sent and summed in bfloat16 or wider, within the bound.
No kernel may reach another device: no remote copies, remote signals or barrier semaphores. Data moves between devices by JAX's collectives and lax.ppermute only.
A program may use at most 192 MiB of HBM per device.

```python
import math
import jax
import jax.numpy as jnp
import numpy as np
from jax import lax

D = 512
HEADS = 8
HEAD = 64
FF = 2048
TOK_DEV = 256
SENTS = 8
MOST = 128
GROUPS = 32
TOKENS = 8192


def level_of(key, shape, cuts, low, top_value):
    def one(dim, shards_of):
        draws = jax.random.uniform(jax.random.fold_in(jax.random.fold_in(key, 6), dim), (shards_of,), jnp.float32, low / len(cuts), top_value / len(cuts))
        return jnp.repeat(jnp.exp(draws), shape[dim] // shards_of).reshape((-1,) + (1,) * (len(shape) - dim - 1))

    loudness = one(*cuts[0])
    for cut in cuts[1:]:
        loudness = loudness * one(*cut)
    return loudness


def length_profile(amount, total, bound, skew):
    portions = [(1 << 20) // math.isqrt(rank ** skew) + 1 for rank in range(2, amount + 1)]
    rest, holding = total - bound - (amount - 1), [1] * (amount - 1)
    while rest > 0:
        free = [i for i in range(amount - 1) if holding[i] < bound]
        mass, left = sum([portions[i] for i in free]), rest
        for i in free:
            more = min(bound - holding[i], max(1, left * portions[i] // mass), rest)
            holding[i] = holding[i] + more
            rest = rest - more
    return np.array([bound] + holding)


def ragged(stream_key, number_of, total, limit, lean):
    if number_of == 2:
        one = jax.random.randint(stream_key, (), max(1, total - limit), min(limit, total - 1) + 1)
        return jnp.stack([one, total - one])
    sizes = jnp.asarray(length_profile(number_of, total, limit, lean), jnp.int32)
    couples = (number_of - 1) // 2
    giver, receiver = sizes[1:1 + 2 * couples:2], sizes[2:2 + 2 * couples:2]
    room = jnp.minimum(giver - 1, limit - receiver)
    passed = jax.random.randint(jax.random.fold_in(stream_key, 1), (couples,), 0, 1 << 20) % (room + 1)
    sizes = sizes.at[1:1 + 2 * couples:2].set(giver - passed).at[2:2 + 2 * couples:2].set(receiver + passed)
    return sizes[jax.random.permutation(jax.random.fold_in(stream_key, 2), number_of)]


def bell_draw(key, dims, deviation, limit, shards=(), held_as=jnp.bfloat16):
    values = deviation * jax.random.normal(key, dims, jnp.float32)
    if shards:
        values = values * level_of(key, dims, shards, -0.22, 0.18)
    return jnp.clip(values, -limit, limit).astype(held_as)


def setup_inputs(seed: int = 0) -> dict:
    streams_of = jax.random.split(jax.random.key(seed), 23)
    return {
        "source": bell_draw(streams_of[0], (TOKENS, D), 1.0, 6.0, ((0, 32),)),
        "first_in": bell_draw(streams_of[1], (TOKENS, D), 1.0, 6.0, ((0, 32),)),
        "second_in": bell_draw(streams_of[2], (TOKENS, D), 1.0, 6.0, ((0, 32),)),
        "cot_first": bell_draw(streams_of[3], (TOKENS, D), 1.0, 6.0, ((0, 32),)),
        "cot_second": bell_draw(streams_of[4], (TOKENS, D), 1.0, 6.0, ((0, 32),)),
        "src_lengths": jax.vmap(lambda own: ragged(own, SENTS, TOK_DEV, MOST, 2))(jax.random.split(streams_of[5], GROUPS)).reshape((GROUPS, SENTS)).astype(jnp.int32),
        "tgt_lengths": jax.vmap(lambda own: ragged(own, SENTS, TOK_DEV, MOST, 2))(jax.random.split(streams_of[6], GROUPS)).reshape((GROUPS, SENTS)).astype(jnp.int32),
        "enc_attn_in": bell_draw(streams_of[7], (D, 3 * D), D ** -0.5, 0.25, ((0, 16),)),
        "enc_attn_out": bell_draw(streams_of[8], (D, D), (D // 8) ** -0.5, 0.75, ((0, 16),)),
        "enc_ffn_in": bell_draw(streams_of[9], (D, FF), D ** -0.5, 0.25, ((0, 16),)),
        "enc_ffn_out": bell_draw(streams_of[10], (FF, D), FF ** -0.5, 0.125, ((0, 16),)),
        "enc_gain": jnp.clip(1.0 + 0.1 * jax.random.normal(streams_of[11], (2, D), jnp.float32), 0.5, 1.5).astype(jnp.bfloat16),
        "enc_bias": bell_draw(streams_of[12], (2, D), 0.5, 3.0, ((1, 16),)),
        "dec_self_in": bell_draw(streams_of[13], (D, 3 * D), D ** -0.5, 0.25, ((0, 16),)),
        "dec_self_out": bell_draw(streams_of[14], (D, D), (D // 8) ** -0.5, 0.75, ((0, 16),)),
        "dec_cross_q": bell_draw(streams_of[15], (D, D), D ** -0.5, 0.25, ((0, 16),)),
        "dec_cross_kv": bell_draw(streams_of[16], (D, 2 * D), D ** -0.5, 0.25, ((0, 16),)),
        "dec_cross_out": bell_draw(streams_of[17], (D, D), (D // 8) ** -0.5, 0.75, ((0, 16),)),
        "dec_ffn_in": bell_draw(streams_of[18], (D, FF), D ** -0.5, 0.25, ((0, 16),)),
        "dec_ffn_out": bell_draw(streams_of[19], (FF, D), FF ** -0.5, 0.125, ((0, 16),)),
        "dec_gain": jnp.clip(1.0 + 0.1 * jax.random.normal(streams_of[20], (3, D), jnp.float32), 0.5, 1.5).astype(jnp.bfloat16),
        "dec_bias": bell_draw(streams_of[21], (3, D), 0.5, 3.0, ((1, 16),)),
    }


@jax.custom_vjp
def low(v):
    return lax.optimization_barrier(v.astype(jnp.bfloat16)).astype(jnp.float32)

@jax.custom_vjp
def low_back(v):
    return v

def low_keep(v):
    return (low(v), None)

def low_pass(kept, grad):
    return (grad,)

def back_keep(v):
    return (v, None)

def back_low(kept, grad):
    return (low(grad),)
low.defvjp(low_keep, low_pass)
low_back.defvjp(back_keep, back_low)
EPSILON = 1e-05
MASKED = -1000000000.0
PRECISE = lax.Precision.HIGHEST

def matmul(left, right):
    return jnp.dot(left, right, precision=PRECISE, preferred_element_type=jnp.float32)

def layer_norm(values, norm_gain, norm_bias):
    centre = values - lax.optimization_barrier(jnp.mean(values, axis=-1, keepdims=True))
    spread = lax.optimization_barrier(jnp.mean(centre * centre, axis=-1, keepdims=True))
    return centre * lax.rsqrt(spread + EPSILON) * norm_gain + norm_bias

def attention(query_in, key_in, w_query, w_key, w_value, w_out, allowed):
    query_count = query_in.shape[0]
    key_count = key_in.shape[0]
    queries = low_back(low(matmul(query_in, w_query))).reshape(query_count, HEADS, HEAD)
    key_rows = low_back(low(matmul(key_in, w_key))).reshape(key_count, HEADS, HEAD)
    value_rows = low_back(low(matmul(key_in, w_value))).reshape(key_count, HEADS, HEAD)
    scores = jnp.einsum('qhd,khd->hqk', queries, key_rows, precision=PRECISE) * HEAD ** (-0.5)
    scores = jnp.where(allowed[None], low_back(scores), MASKED)
    attn_probs = low(jax.nn.softmax(scores, axis=-1))
    mixed_heads = jnp.einsum('hqk,khd->qhd', attn_probs, value_rows, precision=PRECISE)
    mixed_heads = low_back(low(mixed_heads.reshape(query_count, D)))
    return low_back(matmul(mixed_heads, w_out))

def feed_forward(normed, w_in, w_out):
    up_proj = low_back(matmul(normed, w_in))
    activated = low(jax.nn.gelu(up_proj, approximate=True))
    return low_back(matmul(activated, w_out))

def encoder(source, weights, allowed):
    w_joined, w_out, w_ffn_in, w_ffn_out, norm_gains, norm_biases = weights
    normed = low(layer_norm(source, norm_gains[0], norm_biases[0]))
    hidden = source + attention(normed, normed, w_joined[:, :D], w_joined[:, D:2 * D], w_joined[:, 2 * D:], w_out, allowed)
    normed = low(layer_norm(hidden, norm_gains[1], norm_biases[1]))
    return hidden + feed_forward(normed, w_ffn_in, w_ffn_out)

def decoder(inputs, memory, weights, self_allowed, cross_allowed):
    w_joined, w_self_out, w_query, w_pair, w_cross_out, w_ffn_in, w_ffn_out, norm_gains, norm_biases = weights
    normed = low(layer_norm(inputs, norm_gains[0], norm_biases[0]))
    hidden = inputs + attention(normed, normed, w_joined[:, :D], w_joined[:, D:2 * D], w_joined[:, 2 * D:], w_self_out, self_allowed)
    normed = low(layer_norm(hidden, norm_gains[1], norm_biases[1]))
    hidden = hidden + attention(normed, memory, w_query, w_pair[:, :D], w_pair[:, D:], w_cross_out, cross_allowed)
    normed = low(layer_norm(hidden, norm_gains[2], norm_biases[2]))
    return hidden + feed_forward(normed, w_ffn_in, w_ffn_out)

def segments(lengths):
    sent_ends = jnp.cumsum(lengths, dtype=jnp.int32)
    places = jnp.arange(TOK_DEV, dtype=jnp.int32)
    return lax.optimization_barrier(jnp.sum((places[:, None] >= sent_ends[None, :]).astype(jnp.int32), axis=1, dtype=jnp.int32))

def reference(source, first_in, second_in, cot_first, cot_second, src_lengths, tgt_lengths, enc_attn_in, enc_attn_out, enc_ffn_in, enc_ffn_out, enc_gain, enc_bias, dec_self_in, dec_self_out, dec_cross_q, dec_cross_kv, dec_cross_out, dec_ffn_in, dec_ffn_out, dec_gain, dec_bias):
    enc_weights = tuple((weight.astype(jnp.float32) for weight in (enc_attn_in, enc_attn_out, enc_ffn_in, enc_ffn_out, enc_gain, enc_bias)))
    dec_weights = tuple((weight.astype(jnp.float32) for weight in (dec_self_in, dec_self_out, dec_cross_q, dec_cross_kv, dec_cross_out, dec_ffn_in, dec_ffn_out, dec_gain, dec_bias)))

    def by_block(values):
        return values.astype(jnp.float32).reshape(GROUPS, TOK_DEV, D)
    blocks = (by_block(source), by_block(first_in), by_block(second_in), by_block(cot_first), by_block(cot_second), src_lengths, tgt_lengths)
    zeroes = (tuple((jnp.zeros_like(weight) for weight in enc_weights)), tuple((jnp.zeros_like(weight) for weight in dec_weights)))

    def one_block(totals, block_data):
        src_rows, first_rows, second_rows, cot_one, cot_two, src_len, tgt_len = block_data
        source_ids = segments(src_len)
        target_ids = segments(tgt_len)
        source_mask = source_ids[:, None] == source_ids[None, :]
        target_mask = target_ids[:, None] == target_ids[None, :]
        cross_mask = target_ids[:, None] == source_ids[None, :]

        def forward(enc_params, dec_params, src_values, first_values):
            encoded = encoder(src_values, enc_params, source_mask)
            memory = low(encoded)
            return (decoder(first_values, memory, dec_params, target_mask, cross_mask), decoder(second_rows, memory, dec_params, target_mask, cross_mask))
        outputs, pullback = jax.vjp(forward, enc_weights, dec_weights, src_rows, first_rows)
        enc_grads, dec_grads, src_grad, first_grad = pullback((cot_one, cot_two))
        totals = jax.tree.map(jnp.add, totals, (enc_grads, dec_grads))
        return (totals, (outputs[0].astype(jnp.bfloat16), outputs[1].astype(jnp.bfloat16), src_grad, first_grad))
    totals, results = lax.scan(one_block, zeroes, blocks)
    enc_totals, dec_totals = totals
    return (results[0].reshape(TOKENS, D), results[1].reshape(TOKENS, D), results[2].reshape(TOKENS, D), results[3].reshape(TOKENS, D), enc_totals[0], enc_totals[1], enc_totals[2], enc_totals[3], enc_totals[4], enc_totals[5], dec_totals[0], dec_totals[1], dec_totals[2], dec_totals[3], dec_totals[4], dec_totals[5], dec_totals[6], dec_totals[7], dec_totals[8])
```

```python
import functools

import jax
import jax.numpy as jnp
from jax import lax
from jax.experimental import pallas as pl
from jax.experimental.pallas import tpu as pltpu
from jax.sharding import PartitionSpec as P

D = 512
HEADS = 8
HEAD = 64
TOK = 256
FF = 2048
QUAD = 256
BLOCK = 32
EPSILON = 1e-05
MASKED = -1000000000.0
BF = jnp.bfloat16
F32 = jnp.float32
VMEM_LIMIT = 56 * 1024 * 1024


def dot(left, right):
    return lax.dot_general(left, right, (((1,), (0,)), ((), ())), preferred_element_type=F32)


def dot_nt(left, right):
    return lax.dot_general(left, right, (((1,), (1,)), ((), ())), preferred_element_type=F32)


def dot_tn(left, right):
    return lax.dot_general(left, right, (((0,), (0,)), ((), ())), preferred_element_type=F32)


def place_of(place, turn, first, second):
    which = place[3] ^ turn
    y = place[1] ^ jnp.where(which == 0, first, second)
    half = place[2] ^ jnp.where(which == 0, second, first)
    return y, half, which


def fetch(place, pieces, offset, held, sems):
    rows = held.shape[2] // 4
    copies = []
    for turn in range(2):
        for first in range(2):
            for second in range(2):
                y, half, which = place_of(place, turn, first, second)
                quarter = pl.multiple_of((2 * half + which) * rows, rows)
                for d in range(4):
                    copies.append(
                        pltpu.make_async_copy(
                            pieces[2 * turn + first].at[second, d, :, pl.ds(offset, rows)],
                            held.at[(place[0] + (4 - d)) & 3, pl.ds(2 * y, 2), pl.ds(quarter, rows)],
                            sems.at[len(copies)],
                        )
                    )
    for copy in copies:
        copy.start()
    return copies


def deliver(place, held, own, other, sems):
    rows = held.shape[2] // 4
    copies = []
    for turn in range(2):
        for first in range(2):
            for second in range(2):
                y, half, which = place_of(place, turn, first, second)
                quarter = pl.multiple_of((2 * half + which) * rows, rows)
                for d in range(4):
                    copies.append(
                        pltpu.make_async_copy(
                            held.at[(place[0] + d) & 3, pl.ds(2 * y, 2), pl.ds(quarter, rows)],
                            (own, other)[turn].at[first, second, d],
                            sems.at[len(copies)],
                        )
                    )
    for copy in copies:
        copy.start()
    return copies


def wait_all(copies):
    for copy in copies:
        copy.wait()


def column_block(held, index):
    return held[:, :, index * BLOCK : (index + 1) * BLOCK].reshape(D, D)


def row_block(held, index):
    return held[index, :, 4 * BLOCK : 8 * BLOCK].reshape(D, D)


def normed_of(values):
    centre = values - jnp.mean(values, axis=-1, keepdims=True)
    spread = jnp.mean(centre * centre, axis=-1, keepdims=True)
    inverse = lax.rsqrt(spread + EPSILON)
    return centre * inverse, inverse


def norm_back(unit, inverse, gain, grad_normed, norm_ref):
    norm_ref[0:1] = jnp.sum(grad_normed * unit, axis=0, keepdims=True)
    norm_ref[1:2] = jnp.sum(grad_normed, axis=0, keepdims=True)
    grad_unit = grad_normed * gain
    return (
        grad_unit
        - jnp.mean(grad_unit, axis=-1, keepdims=True)
        - unit * jnp.mean(grad_unit * unit, axis=-1, keepdims=True)
    ) * inverse


def mask_bias(key_lengths, query_lengths):
    key_place = lax.broadcasted_iota(jnp.int32, (TOK, 1), 0)
    query_place = lax.broadcasted_iota(jnp.int32, (1, TOK), 1)
    key_ids = jnp.zeros((TOK, 1), jnp.int32)
    query_ids = jnp.zeros((1, TOK), jnp.int32)
    key_end = jnp.int32(0)
    query_end = jnp.int32(0)
    for k in range(key_lengths.shape[1]):
        key_end = key_end + key_lengths[0, k]
        query_end = query_end + query_lengths[0, k]
        key_ids = key_ids + jnp.where(key_place >= key_end, 1, 0)
        query_ids = query_ids + jnp.where(query_place >= query_end, 1, 0)
    return jnp.where(key_ids == query_ids, 0.0, MASKED).astype(F32)


def lane_masks():
    head_of = lax.broadcasted_iota(jnp.int32, (1, QUAD), 1) // HEAD
    return [jnp.where(head_of == h, 1.0, 0.0).astype(BF) for h in range(QUAD // HEAD)]


def attend(queries, keys, values, bias, probs_ref, first):
    masks = lane_masks()
    outs = []
    for g in range(D // QUAD):
        cols = slice(g * QUAD, (g + 1) * QUAD)
        q, k, v = queries[:, cols], keys[:, cols], values[:, cols]
        total = None
        for h in range(QUAD // HEAD):
            scores = dot_nt(k * (masks[h] * (HEAD**-0.5)), q) + bias
            top = jnp.max(scores, axis=0, keepdims=True)
            grown = jnp.exp(scores - top)
            probs = (grown * (1.0 / jnp.sum(grown, axis=0, keepdims=True))).astype(BF)
            probs_ref[first + g * (QUAD // HEAD) + h] = probs
            part = dot_tn(probs, v * masks[h])
            total = part if total is None else total + part
        outs.append(total.astype(BF))
    return jnp.concatenate(outs, axis=1)


def attend_back(queries, keys, values, probs_ref, first, grad_mixed):
    masks = lane_masks()
    grads = []
    for g in range(D // QUAD):
        cols = slice(g * QUAD, (g + 1) * QUAD)
        q, k, v, go = queries[:, cols], keys[:, cols], values[:, cols], grad_mixed[:, cols]
        gq = gk = gv = None
        for h in range(QUAD // HEAD):
            probs_low = probs_ref[first + g * (QUAD // HEAD) + h]
            probs = probs_low.astype(F32)
            grad_probs = dot_nt(v * masks[h], go)
            both = probs * grad_probs
            grad_scores = (both - probs * jnp.sum(both, axis=0, keepdims=True)).astype(BF)
            part_v = dot(probs_low, go * masks[h])
            part_k = dot(grad_scores, q * masks[h])
            part_q = dot_tn(grad_scores, k * masks[h])
            gv = part_v if gv is None else gv + part_v
            gk = part_k if gk is None else gk + part_k
            gq = part_q if gq is None else gq + part_q
        grads.append((gq * (HEAD**-0.5), gk * (HEAD**-0.5), gv))
    return tuple(jnp.concatenate(parts, axis=1) for parts in zip(*grads))


def put_block(held, index, product):
    held[:, :, index * BLOCK : (index + 1) * BLOCK] = product.astype(BF).reshape(4, 4, BLOCK, D)


def self_forward_kernel(passes, row, offset, me_ref, lengths, gains, *refs):
    inputs, refs = refs[:passes], refs[passes:]
    pieces, refs = refs[:4], refs[4:]
    out_ref, normed_ref, joined_ref, probs_ref, mixed_ref, held, sems = refs
    loads = fetch(me_ref, pieces, offset, held, sems)
    for p in range(passes):
        rows = slice(p * TOK, (p + 1) * TOK)
        unit, unused = normed_of(inputs[p][...].astype(F32))
        normed_ref[rows] = (unit * gains[row : row + 1] + gains[row + 1 : row + 2]).astype(BF)
    wait_all(loads)
    for b in range(3):
        joined_ref[:, b * D : (b + 1) * D] = dot(normed_ref[...], column_block(held, b)).astype(BF)
    bias = mask_bias(lengths, lengths)
    for p in range(passes):
        rows = slice(p * TOK, (p + 1) * TOK)
        mixed = attend(
            joined_ref[rows, 0:D],
            joined_ref[rows, D : 2 * D],
            joined_ref[rows, 2 * D : 3 * D],
            bias,
            probs_ref,
            p * HEADS,
        )
        mixed_ref[rows] = mixed
        out_ref[rows] = inputs[p][...].astype(F32) + dot(mixed, column_block(held, 3))


def self_back_kernel(passes, row, offset, me_ref, gains, *refs):
    inputs, refs = refs[:passes], refs[passes:]
    grad_out, normed, joined, probs, mixed = refs[:5]
    pieces, refs = refs[5:9], refs[9:]
    grad_in, norm_ref, own, other, held, made, back, sems = refs
    loads = fetch(me_ref, pieces, offset, held, sems)
    grad_low = grad_out[...].astype(BF)
    put_block(made, 3, dot_tn(mixed[...], grad_low))
    wait_all(loads)
    grad_mixed = dot_nt(grad_low, column_block(held, 3)).astype(BF)
    for p in range(passes):
        rows = slice(p * TOK, (p + 1) * TOK)
        grads = attend_back(
            joined[rows, 0:D],
            joined[rows, D : 2 * D],
            joined[rows, 2 * D : 3 * D],
            probs,
            p * HEADS,
            grad_mixed[rows],
        )
        for b in range(3):
            back[rows, b * D : (b + 1) * D] = grads[b].astype(BF)
    grad_normed = None
    for b in range(3):
        part = back[:, b * D : (b + 1) * D]
        put_block(made, b, dot_tn(normed[...], part))
        step = dot_nt(part, column_block(held, b))
        grad_normed = step if grad_normed is None else grad_normed + step
    stores = deliver(me_ref, made, own, other, sems)
    units = [normed_of(inputs[p][...].astype(F32)) for p in range(passes)]
    unit = jnp.concatenate([u[0] for u in units], axis=0)
    inverse = jnp.concatenate([u[1] for u in units], axis=0)
    grad = norm_back(unit, inverse, gains[row : row + 1], grad_normed, norm_ref)
    grad_in[...] = grad_out[0:TOK] + grad[0:TOK]
    wait_all(stores)


def cross_forward_kernel(row, offset, me_ref, src_lengths, tgt_lengths, gains, hidden, memory, *refs):
    pieces, refs = refs[:4], refs[4:]
    out_ref, normed_ref, query_ref, pair_ref, probs_ref, mixed_ref, held, sems = refs
    loads = fetch(me_ref, pieces, offset, held, sems)
    unit, unused = normed_of(hidden[...])
    normed_ref[...] = (unit * gains[row : row + 1] + gains[row + 1 : row + 2]).astype(BF)
    wait_all(loads)
    query_ref[...] = dot(normed_ref[...], column_block(held, 0)).astype(BF)
    for b in range(2):
        pair_ref[:, b * D : (b + 1) * D] = dot(memory[...], column_block(held, 1 + b)).astype(BF)
    bias = mask_bias(src_lengths, tgt_lengths)
    for p in range(2):
        rows = slice(p * TOK, (p + 1) * TOK)
        mixed = attend(
            query_ref[rows], pair_ref[:, 0:D], pair_ref[:, D : 2 * D], bias, probs_ref, p * HEADS
        )
        mixed_ref[rows] = mixed
        out_ref[rows] = hidden[rows] + dot(mixed, column_block(held, 3))


def cross_back_kernel(row, offset, me_ref, gains, hidden, memory, grad_out, normed, query, pair, probs, mixed, *refs):
    pieces, refs = refs[:4], refs[4:]
    grad_in, grad_memory, norm_ref, own, other, held, made, back, sems = refs
    loads = fetch(me_ref, pieces, offset, held, sems)
    grad_low = grad_out[...].astype(BF)
    put_block(made, 3, dot_tn(mixed[...], grad_low))
    wait_all(loads)
    grad_mixed = dot_nt(grad_low, column_block(held, 3)).astype(BF)
    grad_key = grad_value = None
    for p in range(2):
        rows = slice(p * TOK, (p + 1) * TOK)
        grads = attend_back(
            query[rows], pair[:, 0:D], pair[:, D : 2 * D], probs, p * HEADS, grad_mixed[rows]
        )
        back[rows] = grads[0].astype(BF)
        grad_key = grads[1] if grad_key is None else grad_key + grads[1]
        grad_value = grads[2] if grad_value is None else grad_value + grads[2]
    grad_key = grad_key.astype(BF)
    grad_value = grad_value.astype(BF)
    put_block(made, 0, dot_tn(normed[...], back[...]))
    put_block(made, 1, dot_tn(memory[...], grad_key))
    put_block(made, 2, dot_tn(memory[...], grad_value))
    stores = deliver(me_ref, made, own, other, sems)
    grad_memory[...] = dot_nt(grad_key, column_block(held, 1)) + dot_nt(
        grad_value, column_block(held, 2)
    )
    grad_normed = dot_nt(back[...], column_block(held, 0))
    unit, inverse = normed_of(hidden[...])
    grad = norm_back(unit, inverse, gains[row : row + 1], grad_normed, norm_ref)
    grad_in[...] = grad_out[...] + grad
    wait_all(stores)


GELU_SCALE = 0.7978845608028654
GELU_CUBE = 0.044715


def gelu_both(up):
    square = up * up
    bent = jnp.tanh(GELU_SCALE * up * (1.0 + GELU_CUBE * square))
    half = 0.5 * (1.0 + bent)
    slope = half + 0.5 * up * (1.0 - bent * bent) * (
        GELU_SCALE * (1.0 + (3.0 * GELU_CUBE) * square)
    )
    return up * half, slope


def ffn_forward_kernel(row, offset, me_ref, gains, hidden, *refs):
    pieces, refs = refs[:4], refs[4:]
    memory, normed_ref, active_ref, slope_ref, held, sems = refs
    loads = fetch(me_ref, pieces, offset, held, sems)
    unit, unused = normed_of(hidden[...])
    normed_ref[...] = (unit * gains[row : row + 1] + gains[row + 1 : row + 2]).astype(BF)
    wait_all(loads)
    for b in range(4):
        cols = slice(b * D, (b + 1) * D)
        active, slope = gelu_both(dot(normed_ref[...], column_block(held, b)))
        active_ref[:, cols] = active.astype(BF)
        slope_ref[:, cols] = slope.astype(BF)
    total = hidden[...]
    for z in range(4):
        total = total + dot(active_ref[:, z * D : (z + 1) * D], row_block(held, z))
    memory[...] = total.astype(BF)


def ffn_back_kernel(row, offset, me_ref, gains, hidden, grad_out, normed, active, slope, *refs):
    pieces, refs = refs[:4], refs[4:]
    grad_in, norm_ref, own, other, held, made, sems = refs
    loads = fetch(me_ref, pieces, offset, held, sems)
    grad_low = grad_out[...].astype(BF)
    wait_all(loads)
    grad = ffn_back_core(gains[row : row + 1], hidden[...], grad_low, normed, active, slope, norm_ref, held, made)
    stores = deliver(me_ref, made, own, other, sems)
    grad_in[...] = grad_out[...] + grad
    wait_all(stores)


def ffn_back_core(gain, hidden, grad_low, normed, active, slope, norm_ref, held, made):
    grad_normed = None
    for b in range(4):
        cols = slice(b * D, (b + 1) * D)
        made[b, :, 4 * BLOCK : 8 * BLOCK] = dot_tn(active[:, cols], grad_low).astype(BF).reshape(4, 4 * BLOCK, D)
        grad_active = dot_nt(grad_low, row_block(held, b))
        grad_up = (slope[:, cols].astype(F32) * grad_active).astype(BF)
        put_block(made, b, dot_tn(normed[...], grad_up))
        step = dot_nt(grad_up, column_block(held, b))
        grad_normed = step if grad_normed is None else grad_normed + step
    unit, inverse = normed_of(hidden)
    return norm_back(unit, inverse, gain, grad_normed, norm_ref)


def ffn_both_kernel(row, offset, me_ref, gains, hidden, cot_first, cot_second, *refs):
    pieces, refs = refs[:4], refs[4:]
    first_out, second_out, grad_in, norm_ref, own, other, held, made, normed, active, slope, sems = refs
    loads = fetch(me_ref, pieces, offset, held, sems)
    unit, unused = normed_of(hidden[...])
    normed[...] = (unit * gains[row : row + 1] + gains[row + 1 : row + 2]).astype(BF)
    wait_all(loads)
    for b in range(4):
        cols = slice(b * D, (b + 1) * D)
        grown, bent = gelu_both(dot(normed[...], column_block(held, b)))
        active[:, cols] = grown.astype(BF)
        slope[:, cols] = bent.astype(BF)
    total = hidden[...]
    for z in range(4):
        total = total + dot(active[:, z * D : (z + 1) * D], row_block(held, z))
    first_out[...] = total[0:TOK].astype(BF)
    second_out[...] = total[TOK:].astype(BF)
    grad_low = jnp.concatenate([cot_first[...], cot_second[...]], axis=0)
    grad = ffn_back_core(gains[row : row + 1], hidden[...], grad_low, normed, active, slope, norm_ref, held, made)
    stores = deliver(me_ref, made, own, other, sems)
    grad_in[...] = grad_low.astype(F32) + grad
    wait_all(stores)


ANY = pl.BlockSpec(memory_space=pl.ANY)
VM = pl.BlockSpec(memory_space=pltpu.VMEM)
SM = pl.BlockSpec(memory_space=pltpu.SMEM)


def held_of(blocks):
    return pltpu.VMEM((4, 4, blocks * BLOCK, D), BF)


def halves(blocks):
    return [jax.ShapeDtypeStruct((2, 2, 4, 2, blocks * BLOCK // 4, D), BF)] * 2


def shape(rows, cols, dtype):
    return jax.ShapeDtypeStruct((rows, cols), dtype)


def call(body, name, in_specs, out_shape, out_specs, scratch, operands, gflop):
    return pl.pallas_call(
        body,
        name=name,
        out_shape=out_shape,
        in_specs=in_specs,
        out_specs=out_specs,
        scratch_shapes=scratch,
        compiler_params=pltpu.CompilerParams(vmem_limit_bytes=VMEM_LIMIT),
        cost_estimate=pl.CostEstimate(
            flops=int(gflop * 1e8), bytes_accessed=1 << 20, transcendentals=1 << 10
        ),
    )(*operands)


def self_forward(row, me, lengths, gains, inputs, pieces):
    count = len(inputs)
    rows = count * TOK
    return call(
        functools.partial(self_forward_kernel, count, row, pieces[0]),
        "self_forward",
        [SM, SM, VM] + [VM] * count + [ANY] * 4,
        [
            shape(rows, D, F32),
            shape(rows, D, BF),
            shape(rows, 3 * D, BF),
            jax.ShapeDtypeStruct((count * HEADS, TOK, TOK), BF),
            shape(rows, D, BF),
        ],
        [VM] * 5,
        [held_of(4), pltpu.SemaphoreType.DMA((32,))],
        (me, lengths, gains, *inputs, *pieces[1]),
        2 * count,
    )


def self_back(row, me, gains, inputs, grad_out, kept, pieces):
    count = len(inputs)
    rows = count * TOK
    return call(
        functools.partial(self_back_kernel, count, row, pieces[0]),
        "self_back",
        [SM, VM] + [VM] * count + [VM] * 5 + [ANY] * 4,
        [shape(TOK, D, F32), shape(2, D, F32)] + halves(4),
        [VM, VM, ANY, ANY],
        [held_of(4), held_of(4), pltpu.VMEM((rows, 3 * D), BF), pltpu.SemaphoreType.DMA((32,))],
        (me, gains, *inputs, grad_out, *kept, *pieces[1]),
        4 * count,
    )


def cross_forward(row, me, src_lengths, tgt_lengths, gains, hidden, memory, pieces):
    return call(
        functools.partial(cross_forward_kernel, row, pieces[0]),
        "cross_forward",
        [SM, SM, SM, VM, VM, VM] + [ANY] * 4,
        [
            shape(2 * TOK, D, F32),
            shape(2 * TOK, D, BF),
            shape(2 * TOK, D, BF),
            shape(TOK, 2 * D, BF),
            jax.ShapeDtypeStruct((2 * HEADS, TOK, TOK), BF),
            shape(2 * TOK, D, BF),
        ],
        [VM] * 6,
        [held_of(4), pltpu.SemaphoreType.DMA((32,))],
        (me, src_lengths, tgt_lengths, gains, hidden, memory, *pieces[1]),
        3,
    )


def cross_back(row, me, gains, hidden, memory, grad_out, kept, pieces):
    return call(
        functools.partial(cross_back_kernel, row, pieces[0]),
        "cross_back",
        [SM] + [VM] * 9 + [ANY] * 4,
        [shape(2 * TOK, D, F32), shape(TOK, D, F32), shape(2, D, F32)] + halves(4),
        [VM, VM, VM, ANY, ANY],
        [held_of(4), held_of(4), pltpu.VMEM((2 * TOK, D), BF), pltpu.SemaphoreType.DMA((32,))],
        (me, gains, hidden, memory, grad_out, *kept, *pieces[1]),
        6,
    )


def ffn_forward(row, me, gains, hidden, pieces):
    return call(
        functools.partial(ffn_forward_kernel, row, pieces[0]),
        "ffn_forward",
        [SM, VM, VM] + [ANY] * 4,
        [shape(TOK, D, BF), shape(TOK, D, BF), shape(TOK, FF, BF), shape(TOK, FF, BF)],
        [VM] * 4,
        [held_of(8), pltpu.SemaphoreType.DMA((32,))],
        (me, gains, hidden, *pieces[1]),
        2,
    )


def ffn_back(row, me, gains, hidden, grad_out, kept, pieces):
    return call(
        functools.partial(ffn_back_kernel, row, pieces[0]),
        "ffn_back",
        [SM, VM, VM, VM, VM, VM, VM] + [ANY] * 4,
        [shape(TOK, D, F32), shape(2, D, F32)] + halves(8),
        [VM, VM, ANY, ANY],
        [held_of(8), held_of(8), pltpu.SemaphoreType.DMA((32,))],
        (me, gains, hidden, grad_out, *kept, *pieces[1]),
        4,
    )


def ffn_both(row, me, gains, hidden, cot_first, cot_second, pieces):
    rows = 2 * TOK
    return call(
        functools.partial(ffn_both_kernel, row, pieces[0]),
        "ffn_both",
        [SM, VM, VM, VM, VM] + [ANY] * 4,
        [shape(TOK, D, BF), shape(TOK, D, BF), shape(rows, D, F32), shape(2, D, F32)] + halves(8),
        [VM, VM, VM, VM, ANY, ANY],
        [
            held_of(8),
            held_of(8),
            pltpu.VMEM((rows, D), BF),
            pltpu.VMEM((rows, FF), BF),
            pltpu.VMEM((rows, FF), BF),
            pltpu.SemaphoreType.DMA((32,)),
        ],
        (me, gains, hidden, cot_first, cot_second, *pieces[1]),
        9,
    )


AXIS = "fsdp"
BOTH = ("dp", "fsdp")
SHARDS = 16


def route(target):
    pairs = []
    for i in range(2 * SHARDS):
        dp, z, y, core = target(i // 16, (i // 4) % 4, (i // 2) % 2, i % 2)
        pairs.append((i, dp * 16 + (z % 4) * 4 + y * 2 + core))
    return pairs


def to_core(x):
    return lax.ppermute(x, BOTH, route(lambda dp, z, y, core: (dp, z, y, 1 - core)))


def to_z(x, step):
    return lax.ppermute(x, BOTH, route(lambda dp, z, y, core: (dp, z + step, y, core)))


def to_y(x):
    return lax.ppermute(x, BOTH, route(lambda dp, z, y, core: (dp, z, 1 - y, core)))


def to_dp(x):
    return lax.ppermute(x, BOTH, route(lambda dp, z, y, core: (1 - dp, z, y, core)))


def to_yx(x):
    return lax.ppermute(
        x, BOTH, route(lambda dp, z, y, core: (dp, z, y ^ 1, core) if core == 0 else (dp ^ 1, z, y, core))
    )


def to_xy(x):
    return lax.ppermute(
        x, BOTH, route(lambda dp, z, y, core: (dp ^ 1, z, y, core) if core == 0 else (dp, z, y ^ 1, core))
    )


def after(value, *earlier):
    return lax.optimization_barrier((value,) + tuple(earlier))[0]


def blocks_of(shard):
    rows, cols = shard.shape
    split = shard.reshape(rows // BLOCK, BLOCK, cols // D, D)
    return split.transpose(2, 0, 1, 3).reshape(-1, BLOCK, D)


def shard_of(blocks, cols):
    wide = blocks.reshape(cols // D, -1, D)
    return wide.transpose(1, 0, 2).reshape(-1, cols)


def quarters_of(weights):
    blocks = jnp.concatenate([blocks_of(weight) for weight in weights])
    return blocks.reshape(4, -1, D)


def as_pair(core, own, came):
    return jnp.where(core == 0, jnp.stack([own, came]), jnp.stack([came, own]))


class Gather:
    def __init__(self, place, chunk):
        core, half = place[3], place[2]
        mine = lax.dynamic_slice_in_dim(chunk, 2 * half, 2, 0)
        own = jnp.where(core == 0, mine[0], mine[1])
        other = jnp.where(core == 0, mine[1], mine[0])
        self.pair = as_pair(core, own, to_core(other))

    def along_z(self):
        self.line = jnp.stack([self.pair] + [to_z(self.pair, d) for d in (1, 2, 3)])

    def first_cross(self):
        self.both = jnp.stack([self.line, to_xy(self.line)])

    def second_cross(self):
        came = to_yx(self.both)
        self.pieces = (self.both, came, to_core(self.both), to_core(came))


def gather_norms(place, rows):
    block = jnp.pad(rows, ((0, 6), (0, D - rows.shape[1])))
    pair = as_pair(place[3], block, to_core(block))
    line = jnp.stack([pair] + [to_z(pair, d) for d in (1, 2, 3)])
    across = to_y(line)
    both = jnp.where(place[1] == 0, jnp.stack([line, across]), jnp.stack([across, line]))
    both = both[:, :, :, 0:10, 0:BLOCK]
    turned = jnp.concatenate([both, both], axis=1)
    ordered = lax.dynamic_slice_in_dim(turned[:, ::-1], 3 - place[0], 4, 1)
    return ordered[:, ::1].transpose(3, 1, 0, 2, 4).reshape(10, D)


class Reduce:
    def __init__(self):
        self.parts = []

    def add(self, own, other):
        self.parts.append((own, to_core(other)))

    def first(self):
        sums = [(own.astype(F32) + came.astype(F32)).astype(BF) for own, came in self.parts]
        self.keep = jnp.concatenate([part[0] for part in sums], axis=3)
        self.came = to_yx(jnp.concatenate([part[1] for part in sums], axis=3))

    def second(self):
        total = (self.keep.astype(F32) + self.came.astype(F32)).astype(BF)
        self.keep = total[0]
        self.came = to_xy(total[1])

    def along_z(self):
        total = (self.keep.astype(F32) + self.came.astype(F32)).astype(BF)
        self.keep = [total[0]] + [to_z(total[d], d) for d in (1, 2, 3)]

    def last(self, place):
        total = self.keep[0].astype(F32)
        for part in self.keep[1:]:
            total = total + part.astype(F32)
        total = total.astype(BF)
        core, half = place[3], place[2]
        own = jnp.where(core == 0, total[0], total[1])
        other = jnp.where(core == 0, total[1], total[0])
        pair = as_pair(core, own, to_core(other))
        self.ends = (pair, to_dp(pair))

    def shard(self, place):
        pair, came = self.ends
        whole = jnp.where(
            place[2] == 0, jnp.concatenate([pair, came]), jnp.concatenate([came, pair])
        )
        return whole.astype(F32)


def reduce_norms(place, rows):
    total = jnp.pad(rows, ((0, 6), (0, 0)))
    for move in (to_core, to_y):
        total = total + move(total)
    total = total + to_z(total, 1) + to_z(total, 2) + to_z(total, 3)
    total = total + to_dp(total)
    spot = place[0] * 4 + place[1] * 2 + place[3]
    return lax.dynamic_slice_in_dim(total, spot * BLOCK, BLOCK, 1)[0:10]


def gather_plain(weights):
    parts = []
    for weight in weights:
        whole = lax.all_gather(weight, AXIS, axis=0, tiled=True)
        shards = whole.reshape(SHARDS, -1, whole.shape[1])
        parts.append(jax.vmap(blocks_of)(shards))
    chunk = jnp.concatenate(parts, axis=1).reshape(4, 2, 2, 2, 2, -1, D)
    chunk = jnp.concatenate([chunk[0:1], chunk[:0:-1]], axis=0)
    pieces = []
    for first in range(2):
        pieces.append(chunk[:, first, :, :, 0].transpose(2, 0, 1, 3, 4))
    for first in range(2):
        pieces.append(chunk[:, :, :, first, 1].transpose(1, 0, 2, 3, 4))
    return tuple(pieces)


def reduce_plain(own, other, columns):
    sets = jnp.stack([own.transpose(2, 0, 3, 1, 4, 5), other.transpose(2, 1, 3, 0, 4, 5)], axis=4)
    shards = sets.reshape(SHARDS, -1, BLOCK, D)
    grads = []
    for first, last, cols in columns:
        whole = jax.vmap(functools.partial(shard_of, cols=cols))(shards[:, first:last])
        whole = whole.reshape(-1, cols).astype(F32)
        part = lax.psum_scatter(whole, AXIS, scatter_dimension=0, tiled=True)
        grads.append(lax.psum(part.astype(BF), "dp").astype(F32))
    return grads


def norm_rows_of(gain_enc, bias_enc, gain_dec, bias_dec):
    rows = []
    for gain, bias in ((gain_enc, bias_enc), (gain_dec, bias_dec)):
        for k in range(gain.shape[0]):
            rows += [gain[k : k + 1], bias[k : k + 1]]
    return jnp.concatenate(rows, axis=0)


ATTN_COLUMNS = ((0, 3, 3 * D), (3, 4, D))
FFN_COLUMNS = ((0, 4, FF), (4, 8, D))
CROSS_COLUMNS = ((0, 1, D), (1, 3, 2 * D), (3, 4, D))


def shards_of(group, columns):
    blocks = group.reshape(-1, BLOCK, D)
    return [shard_of(blocks[first:last], cols) for first, last, cols in columns]


def step(
    custom,
    source,
    first_in,
    second_in,
    cot_first,
    cot_second,
    src_lengths,
    tgt_lengths,
    enc_attn_in,
    enc_attn_out,
    enc_ffn_in,
    enc_ffn_out,
    enc_gain,
    enc_bias,
    dec_self_in,
    dec_self_out,
    dec_cross_q,
    dec_cross_kv,
    dec_cross_out,
    dec_ffn_in,
    dec_ffn_out,
    dec_gain,
    dec_bias,
):
    spot = lax.axis_index(AXIS)
    norm_rows = norm_rows_of(enc_gain, enc_bias, dec_gain, dec_bias)
    group_self = (dec_self_in, dec_self_out)
    group_enc = (enc_attn_in, enc_attn_out)
    group_enc_ffn = (enc_ffn_in, enc_ffn_out)
    group_cross = (dec_cross_q, dec_cross_kv, dec_cross_out)
    group_ffn = (dec_ffn_in, dec_ffn_out)
    if custom:
        place = jnp.stack([spot >> 2, (spot >> 1) & 1, lax.axis_index("dp"), spot & 1]).astype(jnp.int32)
        chunk_a = jnp.concatenate([quarters_of(group_self), quarters_of(group_enc)], axis=1)
        chunk_b = jnp.concatenate([quarters_of(group_enc_ffn), quarters_of(group_cross)], axis=1)
        chunk_c = quarters_of(group_ffn)
        one = Gather(place, chunk_a)
        one.along_z()
        norms = gather_norms(place, after(norm_rows, one.pair))
        two = Gather(place, chunk_b)
        two.pair = after(two.pair, one.line)
        one.first_cross()
        two.along_z()
        one.second_cross()
        two.line = after(two.line, one.pieces[1])
        three = Gather(place, chunk_c)
        three.pair = after(three.pair, two.line)
        three.along_z()
        two.first_cross()
        two.second_cross()
        three.line = after(three.line, two.pieces[1])
        three.first_cross()
        three.second_cross()
        w_self, w_enc = (0, one.pieces), (32, one.pieces)
        w_enc_ffn, w_cross = (0, two.pieces), (64, two.pieces)
        w_ffn = (0, three.pieces)
    else:
        place = jnp.zeros((4,), jnp.int32)
        w_self, w_enc, w_enc_ffn, w_cross, w_ffn = (
            (0, gather_plain(group))
            for group in (group_self, group_enc, group_enc_ffn, group_cross, group_ffn)
        )
        norms = lax.all_gather(norm_rows, AXIS, axis=1, tiled=True)
    gains = jnp.pad(norms.astype(F32), ((0, 6), (0, 0)))

    hidden_one, *kept_self = self_forward(4, place, tgt_lengths, gains, [first_in, second_in], w_self)
    hidden_enc, *kept_enc = self_forward(0, place, src_lengths, gains, [source], w_enc)
    memory, *kept_enc_ffn = ffn_forward(2, place, gains, hidden_enc, w_enc_ffn)
    hidden_two, *kept_cross = cross_forward(
        6, place, src_lengths, tgt_lengths, gains, hidden_one, memory, w_cross
    )
    first_out, second_out, grad_two, norm_ffn, *made_ffn = ffn_both(
        8, place, gains, hidden_two, cot_first, cot_second, w_ffn
    )
    if custom:
        red_one, red_two, red_three = Reduce(), Reduce(), Reduce()
        red_one.add(*made_ffn)
    grad_one, grad_memory, norm_cross, *made_cross = cross_back(
        6, place, gains, hidden_one, memory, grad_two, kept_cross, w_cross
    )
    if custom:
        red_two.add(*made_cross)
        red_one.first()
        grad_memory = after(grad_memory, red_one.keep)
    grad_enc, norm_enc_ffn, *made_enc_ffn = ffn_back(
        2, place, gains, hidden_enc, grad_memory, kept_enc_ffn, w_enc_ffn
    )
    if custom:
        red_two.add(*made_enc_ffn)
        grad_one = after(grad_one, grad_enc)
    grad_first, norm_self, *made_self = self_back(
        4, place, gains, [first_in, second_in], grad_one, kept_self, w_self
    )
    if custom:
        red_three.add(*made_self)
        red_one.second()
        red_two.first()
        grad_enc = after(grad_enc, grad_first, red_one.keep, red_two.keep)
    grad_source, norm_enc, *made_enc = self_back(
        0, place, gains, [source], grad_enc, kept_enc, w_enc
    )
    norm_grads = jnp.concatenate([norm_enc, norm_enc_ffn, norm_self, norm_cross, norm_ffn], axis=0)
    if custom:
        red_three.add(*made_enc)
        red_one.along_z()
        red_two.second()
        red_three.first()
        red_one.last(place)
        red_two.along_z()
        red_three.second()
        red_two.last(place)
        red_three.along_z()
        red_three.last(place)
        norm_shard = reduce_norms(place, norm_grads)
        shard_one, shard_two, shard_three = (
            red.shard(place) for red in (red_one, red_two, red_three)
        )
        grads_ffn = shards_of(shard_one, FFN_COLUMNS)
        grads_cross = shards_of(shard_two[:, 0:32], CROSS_COLUMNS)
        grads_enc_ffn = shards_of(shard_two[:, 32:96], FFN_COLUMNS)
        grads_self = shards_of(shard_three[:, 0:32], ATTN_COLUMNS)
        grads_enc = shards_of(shard_three[:, 32:64], ATTN_COLUMNS)
    else:
        grads_ffn = reduce_plain(*made_ffn, FFN_COLUMNS)
        grads_cross = reduce_plain(*made_cross, CROSS_COLUMNS)
        grads_enc_ffn = reduce_plain(*made_enc_ffn, FFN_COLUMNS)
        grads_self = reduce_plain(*made_self, ATTN_COLUMNS)
        grads_enc = reduce_plain(*made_enc, ATTN_COLUMNS)
        norm_shard = lax.psum_scatter(norm_grads, AXIS, scatter_dimension=1, tiled=True)
        norm_shard = lax.psum(norm_shard.astype(BF), "dp").astype(F32)
    return (
        first_out,
        second_out,
        grad_source,
        grad_first,
        *grads_enc,
        *grads_enc_ffn,
        norm_shard[0:4:2],
        norm_shard[1:4:2],
        *grads_self,
        *grads_cross,
        *grads_ffn,
        norm_shard[4:10:2],
        norm_shard[5:10:2],
    )


def solution(mesh):
    blocked = P(("dp", "fsdp"), None)
    rows = P("fsdp", None)
    columns = P(None, "fsdp")
    custom = mesh.shape["fsdp"] == SHARDS and mesh.shape["dp"] == 2
    return jax.shard_map(
        functools.partial(step, custom),
        mesh=mesh,
        in_specs=(blocked,) * 7 + (rows,) * 4 + (columns,) * 2 + (rows,) * 7 + (columns,) * 2,
        out_specs=(blocked,) * 4 + (rows,) * 4 + (columns,) * 2 + (rows,) * 7 + (columns,) * 2,
        check_vma=False,
    )
```

```python
import functools
import typing

import jax
import jax.numpy as jnp
from jax import lax
from jax.experimental import pallas as pl
from jax.experimental.pallas import tpu as pltpu
from jax.sharding import PartitionSpec as P

D = 512
HEADS = 8
HEAD = 64
TOK = 256
FF = 2048
QUAD = 256
BLOCK = 32
EPSILON = 1e-05
MASKED = -1000000000.0
BF = jnp.bfloat16
F32 = jnp.float32
VMEM_LIMIT = 64 * 1024 * 1024
COST = 1.1e9


class Layout(typing.NamedTuple):
    offset: int
    pieces: int
    made: int = 2
    made_offset: int = 0
    made_rows: int = 0


def dot(left, right):
    return lax.dot_general(left, right, (((1,), (0,)), ((), ())), preferred_element_type=F32)


def dot_nt(left, right):
    return lax.dot_general(left, right, (((1,), (1,)), ((), ())), preferred_element_type=F32)


def dot_tn(left, right):
    return lax.dot_general(left, right, (((0,), (0,)), ((), ())), preferred_element_type=F32)


def place_of(place, turn, first, second):
    which = place[3] ^ turn
    y = place[1] ^ jnp.where(which == 0, first, second)
    half = place[2] ^ jnp.where(which == 0, second, first)
    return y, half, which


def fetch(place, pieces, layout, held, sems):
    copies = []
    if layout.pieces == 1:
        part = pieces[0].at[:, :, pl.ds(layout.offset, held.shape[2])]
        copies.append(pltpu.make_async_copy(part, held, sems.at[0]))
    else:
        rows = held.shape[2] // 4
        for turn in range(2):
            for first in range(2):
                for second in range(2):
                    y, half, which = place_of(place, turn, first, second)
                    quarter = pl.multiple_of((2 * half + which) * rows, rows)
                    piece = pieces[4 * turn + 2 * first + second]
                    for d in range(4):
                        z = (place[0] + (4 - d)) & 3
                        copies.append(
                            pltpu.make_async_copy(
                                piece.at[d, :, pl.ds(layout.offset, rows)],
                                held.at[z, pl.ds(2 * y, 2), pl.ds(quarter, rows)],
                                sems.at[len(copies)],
                            )
                        )
    for copy in copies:
        copy.start()
    return copies


def deliver(place, held, layout, outs, sems):
    copies = []
    if layout.made == 1:
        part = outs[0].at[:, :, pl.ds(layout.made_offset, held.shape[2])]
        copies.append(pltpu.make_async_copy(held, part, sems.at[0]))
    else:
        rows = held.shape[2] // 4
        for turn in range(2):
            for first in range(2):
                for second in range(2):
                    y, half, which = place_of(place, turn, first, second)
                    quarter = pl.multiple_of((2 * half + which) * rows, rows)
                    for d in range(4):
                        z = (place[0] + d) & 3
                        copies.append(
                            pltpu.make_async_copy(
                                held.at[z, pl.ds(2 * y, 2), pl.ds(quarter, rows)],
                                outs[turn].at[first, second, d],
                                sems.at[len(copies)],
                            )
                        )
    for copy in copies:
        copy.start()
    return copies


def wait_all(copies):
    for copy in copies:
        copy.wait()


def column_block(held, index):
    return held[:, :, index * BLOCK : (index + 1) * BLOCK].reshape(D, D)


def row_block(held, index):
    return held[index, :, 4 * BLOCK : 8 * BLOCK].reshape(D, D)


def normed_of(values):
    centre = values - jnp.mean(values, axis=-1, keepdims=True)
    spread = jnp.mean(centre * centre, axis=-1, keepdims=True)
    inverse = lax.rsqrt(spread + EPSILON)
    return centre * inverse, inverse


def norm_back(unit, inverse, gain, grad_normed, norm_ref):
    norm_ref[0:1] = jnp.sum(grad_normed * unit, axis=0, keepdims=True)
    norm_ref[1:2] = jnp.sum(grad_normed, axis=0, keepdims=True)
    grad_unit = grad_normed * gain
    return (
        grad_unit
        - jnp.mean(grad_unit, axis=-1, keepdims=True)
        - unit * jnp.mean(grad_unit * unit, axis=-1, keepdims=True)
    ) * inverse


def mask_bias(key_lengths, query_lengths):
    key_place = lax.broadcasted_iota(jnp.int32, (TOK, 1), 0)
    query_place = lax.broadcasted_iota(jnp.int32, (1, TOK), 1)
    key_ids = jnp.zeros((TOK, 1), jnp.int32)
    query_ids = jnp.zeros((1, TOK), jnp.int32)
    key_end = jnp.int32(0)
    query_end = jnp.int32(0)
    for k in range(key_lengths.shape[1]):
        key_end = key_end + key_lengths[0, k]
        query_end = query_end + query_lengths[0, k]
        key_ids = key_ids + jnp.where(key_place >= key_end, 1, 0)
        query_ids = query_ids + jnp.where(query_place >= query_end, 1, 0)
    return jnp.where(key_ids == query_ids, 0.0, MASKED).astype(F32)


def lane_masks():
    head_of = lax.broadcasted_iota(jnp.int32, (1, QUAD), 1) // HEAD
    return [jnp.where(head_of == h, 1.0, 0.0).astype(BF) for h in range(QUAD // HEAD)]


def attend(queries, keys, values, bias, probs_ref, first):
    masks = lane_masks()
    outs = []
    for g in range(D // QUAD):
        cols = slice(g * QUAD, (g + 1) * QUAD)
        q, k, v = queries[:, cols], keys[:, cols], values[:, cols]
        total = None
        for h in range(QUAD // HEAD):
            scores = dot_nt(k * (masks[h] * (HEAD**-0.5)), q) + bias
            top = jnp.max(scores, axis=0, keepdims=True)
            grown = jnp.exp(scores - top)
            probs = (grown * (1.0 / jnp.sum(grown, axis=0, keepdims=True))).astype(BF)
            probs_ref[first + g * (QUAD // HEAD) + h] = probs
            part = dot_tn(probs, v * masks[h])
            total = part if total is None else total + part
        outs.append(total.astype(BF))
    return jnp.concatenate(outs, axis=1)


def attend_back(queries, keys, values, probs_ref, first, grad_mixed):
    masks = lane_masks()
    grads = []
    for g in range(D // QUAD):
        cols = slice(g * QUAD, (g + 1) * QUAD)
        q, k, v, go = queries[:, cols], keys[:, cols], values[:, cols], grad_mixed[:, cols]
        gq = gk = gv = None
        for h in range(QUAD // HEAD):
            probs_low = probs_ref[first + g * (QUAD // HEAD) + h]
            probs = probs_low.astype(F32)
            grad_probs = dot_nt(v * masks[h], go)
            both = probs * grad_probs
            grad_scores = (both - probs * jnp.sum(both, axis=0, keepdims=True)).astype(BF)
            part_v = dot(probs_low, go * masks[h])
            part_k = dot(grad_scores, q * masks[h])
            part_q = dot_tn(grad_scores, k * masks[h])
            gv = part_v if gv is None else gv + part_v
            gk = part_k if gk is None else gk + part_k
            gq = part_q if gq is None else gq + part_q
        grads.append((gq * (HEAD**-0.5), gk * (HEAD**-0.5), gv))
    return tuple(jnp.concatenate(parts, axis=1) for parts in zip(*grads))


def put_block(held, index, product):
    held[:, :, index * BLOCK : (index + 1) * BLOCK] = product.astype(BF).reshape(4, 4, BLOCK, D)


def self_forward_kernel(passes, row, layout, me_ref, lengths, gains, *refs):
    inputs, refs = refs[:passes], refs[passes:]
    pieces, refs = refs[: layout.pieces], refs[layout.pieces :]
    out_ref, normed_ref, joined_ref, probs_ref, mixed_ref, held, sems = refs
    loads = fetch(me_ref, pieces, layout, held, sems)
    for p in range(passes):
        rows = slice(p * TOK, (p + 1) * TOK)
        unit, unused = normed_of(inputs[p][...].astype(F32))
        normed_ref[rows] = (unit * gains[row : row + 1] + gains[row + 1 : row + 2]).astype(BF)
    wait_all(loads)
    for b in range(3):
        joined_ref[:, b * D : (b + 1) * D] = dot(normed_ref[...], column_block(held, b)).astype(BF)
    bias = mask_bias(lengths, lengths)
    for p in range(passes):
        rows = slice(p * TOK, (p + 1) * TOK)
        mixed = attend(
            joined_ref[rows, 0:D],
            joined_ref[rows, D : 2 * D],
            joined_ref[rows, 2 * D : 3 * D],
            bias,
            probs_ref,
            p * HEADS,
        )
        mixed_ref[rows] = mixed
        out_ref[rows] = inputs[p][...].astype(F32) + dot(mixed, column_block(held, 3))


def self_back_kernel(passes, row, layout, me_ref, gains, *refs):
    inputs, refs = refs[:passes], refs[passes:]
    grad_out, normed, joined, probs, mixed = refs[:5]
    pieces, refs = refs[5 : 5 + layout.pieces], refs[5 + layout.pieces :]
    grad_in, norm_ref, *refs = refs
    outs, (held, made, back, sems) = refs[: layout.made], refs[layout.made :]
    loads = fetch(me_ref, pieces, layout, held, sems)
    grad_low = grad_out[...].astype(BF)
    put_block(made, 3, dot_tn(mixed[...], grad_low))
    wait_all(loads)
    grad_mixed = dot_nt(grad_low, column_block(held, 3)).astype(BF)
    for p in range(passes):
        rows = slice(p * TOK, (p + 1) * TOK)
        grads = attend_back(
            joined[rows, 0:D],
            joined[rows, D : 2 * D],
            joined[rows, 2 * D : 3 * D],
            probs,
            p * HEADS,
            grad_mixed[rows],
        )
        for b in range(3):
            back[rows, b * D : (b + 1) * D] = grads[b].astype(BF)
    grad_normed = None
    for b in range(3):
        part = back[:, b * D : (b + 1) * D]
        put_block(made, b, dot_tn(normed[...], part))
        step = dot_nt(part, column_block(held, b))
        grad_normed = step if grad_normed is None else grad_normed + step
    stores = deliver(me_ref, made, layout, outs, sems)
    units = [normed_of(inputs[p][...].astype(F32)) for p in range(passes)]
    unit = jnp.concatenate([u[0] for u in units], axis=0)
    inverse = jnp.concatenate([u[1] for u in units], axis=0)
    grad = norm_back(unit, inverse, gains[row : row + 1], grad_normed, norm_ref)
    grad_in[...] = grad_out[0:TOK] + grad[0:TOK]
    wait_all(stores)


def cross_forward_kernel(row, layout, me_ref, src_lengths, tgt_lengths, gains, hidden, memory, *refs):
    pieces, refs = refs[: layout.pieces], refs[layout.pieces :]
    out_ref, normed_ref, query_ref, pair_ref, probs_ref, mixed_ref, held, sems = refs
    loads = fetch(me_ref, pieces, layout, held, sems)
    unit, unused = normed_of(hidden[...])
    normed_ref[...] = (unit * gains[row : row + 1] + gains[row + 1 : row + 2]).astype(BF)
    wait_all(loads)
    query_ref[...] = dot(normed_ref[...], column_block(held, 0)).astype(BF)
    for b in range(2):
        pair_ref[:, b * D : (b + 1) * D] = dot(memory[...], column_block(held, 1 + b)).astype(BF)
    bias = mask_bias(src_lengths, tgt_lengths)
    for p in range(2):
        rows = slice(p * TOK, (p + 1) * TOK)
        mixed = attend(
            query_ref[rows], pair_ref[:, 0:D], pair_ref[:, D : 2 * D], bias, probs_ref, p * HEADS
        )
        mixed_ref[rows] = mixed
        out_ref[rows] = hidden[rows] + dot(mixed, column_block(held, 3))


def cross_back_kernel(row, layout, me_ref, gains, hidden, memory, grad_out, normed, query, pair, probs, mixed, *refs):
    pieces, refs = refs[: layout.pieces], refs[layout.pieces :]
    grad_in, grad_memory, norm_ref, *refs = refs
    outs, (held, made, back, sems) = refs[: layout.made], refs[layout.made :]
    loads = fetch(me_ref, pieces, layout, held, sems)
    grad_low = grad_out[...].astype(BF)
    put_block(made, 3, dot_tn(mixed[...], grad_low))
    wait_all(loads)
    grad_mixed = dot_nt(grad_low, column_block(held, 3)).astype(BF)
    grad_key = grad_value = None
    for p in range(2):
        rows = slice(p * TOK, (p + 1) * TOK)
        grads = attend_back(
            query[rows], pair[:, 0:D], pair[:, D : 2 * D], probs, p * HEADS, grad_mixed[rows]
        )
        back[rows] = grads[0].astype(BF)
        grad_key = grads[1] if grad_key is None else grad_key + grads[1]
        grad_value = grads[2] if grad_value is None else grad_value + grads[2]
    grad_key = grad_key.astype(BF)
    grad_value = grad_value.astype(BF)
    put_block(made, 0, dot_tn(normed[...], back[...]))
    put_block(made, 1, dot_tn(memory[...], grad_key))
    put_block(made, 2, dot_tn(memory[...], grad_value))
    stores = deliver(me_ref, made, layout, outs, sems)
    grad_memory[...] = dot_nt(grad_key, column_block(held, 1)) + dot_nt(
        grad_value, column_block(held, 2)
    )
    grad_normed = dot_nt(back[...], column_block(held, 0))
    unit, inverse = normed_of(hidden[...])
    grad = norm_back(unit, inverse, gains[row : row + 1], grad_normed, norm_ref)
    grad_in[...] = grad_out[...] + grad
    wait_all(stores)


GELU_SCALE = 0.7978845608028654
GELU_CUBE = 0.044715


def gelu_both(up):
    square = up * up
    bent = jnp.tanh(GELU_SCALE * up * (1.0 + GELU_CUBE * square))
    half = 0.5 * (1.0 + bent)
    slope = half + 0.5 * up * (1.0 - bent * bent) * (
        GELU_SCALE * (1.0 + (3.0 * GELU_CUBE) * square)
    )
    return up * half, slope


def ffn_forward_kernel(row, layout, me_ref, gains, hidden, *refs):
    pieces, refs = refs[: layout.pieces], refs[layout.pieces :]
    memory, normed_ref, active_ref, slope_ref, held, sems = refs
    loads = fetch(me_ref, pieces, layout, held, sems)
    unit, unused = normed_of(hidden[...])
    normed_ref[...] = (unit * gains[row : row + 1] + gains[row + 1 : row + 2]).astype(BF)
    wait_all(loads)
    for b in range(4):
        cols = slice(b * D, (b + 1) * D)
        active, slope = gelu_both(dot(normed_ref[...], column_block(held, b)))
        active_ref[:, cols] = active.astype(BF)
        slope_ref[:, cols] = slope.astype(BF)
    total = hidden[...]
    for z in range(4):
        total = total + dot(active_ref[:, z * D : (z + 1) * D], row_block(held, z))
    memory[...] = total.astype(BF)


def ffn_back_kernel(row, layout, me_ref, gains, hidden, grad_out, normed, active, slope, *refs):
    pieces, refs = refs[: layout.pieces], refs[layout.pieces :]
    grad_in, norm_ref, *refs = refs
    outs, (held, made, sems) = refs[: layout.made], refs[layout.made :]
    loads = fetch(me_ref, pieces, layout, held, sems)
    grad_low = grad_out[...].astype(BF)
    wait_all(loads)
    grad = ffn_back_core(gains[row : row + 1], hidden[...], grad_low, normed, active, slope, norm_ref, held, made)
    stores = deliver(me_ref, made, layout, outs, sems)
    grad_in[...] = grad_out[...] + grad
    wait_all(stores)


def ffn_back_core(gain, hidden, grad_low, normed, active, slope, norm_ref, held, made):
    grad_normed = None
    for b in range(4):
        cols = slice(b * D, (b + 1) * D)
        made[b, :, 4 * BLOCK : 8 * BLOCK] = dot_tn(active[:, cols], grad_low).astype(BF).reshape(4, 4 * BLOCK, D)
        grad_active = dot_nt(grad_low, row_block(held, b))
        grad_up = (slope[:, cols].astype(F32) * grad_active).astype(BF)
        put_block(made, b, dot_tn(normed[...], grad_up))
        step = dot_nt(grad_up, column_block(held, b))
        grad_normed = step if grad_normed is None else grad_normed + step
    unit, inverse = normed_of(hidden)
    return norm_back(unit, inverse, gain, grad_normed, norm_ref)


def ffn_both_kernel(row, layout, me_ref, gains, hidden, cot_first, cot_second, *refs):
    pieces, refs = refs[: layout.pieces], refs[layout.pieces :]
    first_out, second_out, grad_in, norm_ref, *refs = refs
    outs, refs = refs[: layout.made], refs[layout.made :]
    held, made, normed, active, slope, sems = refs
    loads = fetch(me_ref, pieces, layout, held, sems)
    unit, unused = normed_of(hidden[...])
    normed[...] = (unit * gains[row : row + 1] + gains[row + 1 : row + 2]).astype(BF)
    wait_all(loads)
    for b in range(4):
        cols = slice(b * D, (b + 1) * D)
        grown, bent = gelu_both(dot(normed[...], column_block(held, b)))
        active[:, cols] = grown.astype(BF)
        slope[:, cols] = bent.astype(BF)
    total = hidden[...]
    for z in range(4):
        total = total + dot(active[:, z * D : (z + 1) * D], row_block(held, z))
    first_out[...] = total[0:TOK].astype(BF)
    second_out[...] = total[TOK:].astype(BF)
    grad_low = jnp.concatenate([cot_first[...], cot_second[...]], axis=0)
    grad = ffn_back_core(gains[row : row + 1], hidden[...], grad_low, normed, active, slope, norm_ref, held, made)
    stores = deliver(me_ref, made, layout, outs, sems)
    grad_in[...] = grad_low.astype(F32) + grad
    wait_all(stores)


ANY = pl.BlockSpec(memory_space=pl.ANY)
HB = pl.BlockSpec(memory_space=pltpu.HBM)
VM = pl.BlockSpec(memory_space=pltpu.VMEM)
SM = pl.BlockSpec(memory_space=pltpu.SMEM)


def held_of(blocks):
    return pltpu.VMEM((4, 4, blocks * BLOCK, D), BF)


def made_of(layout, blocks):
    if layout.made == 1:
        return [jax.ShapeDtypeStruct((4, 4, layout.made_rows, D), BF)]
    return [jax.ShapeDtypeStruct((2, 2, 4, 2, blocks * BLOCK // 4, D), BF)] * 2


def shape(rows, cols, dtype):
    return jax.ShapeDtypeStruct((rows, cols), dtype)


class Order:
    def __init__(self):
        self.token = jnp.zeros((8, 128), F32)

    def tie(self, value):
        return self.tie_all([value])[0]

    def tie_all(self, values):
        arrays = list(values) + [self.token]
        *values, self.token = pl.pallas_call(
            nothing_kernel,
            name="tie",
            out_shape=[jax.ShapeDtypeStruct(x.shape, x.dtype) for x in arrays],
            in_specs=[HB] * len(arrays),
            out_specs=[HB] * len(arrays),
            input_output_aliases={k: k for k in range(len(arrays))},
            compiler_params=pltpu.CompilerParams(vmem_limit_bytes=VMEM_LIMIT),
        )(*arrays)
        return values


def nothing_kernel(*refs):
    pass


def call(order, body, name, in_specs, out_shape, out_specs, scratch, operands, micros, grid=None, inplace=()):
    count, more, outs = len(operands), len(inplace) + 1, len(out_shape)

    def ordered(*refs):
        body(*refs[:count], *refs[count + more : count + more + outs], *refs[count + more + outs + 1 :])

    aliases = {count + k: out for k, (unused, out) in enumerate(inplace)}
    aliases[count + len(inplace)] = outs
    *results, order.token = pl.pallas_call(
        ordered,
        name=name,
        out_shape=out_shape + [jax.ShapeDtypeStruct(order.token.shape, order.token.dtype)],
        in_specs=in_specs + [HB] * more,
        out_specs=out_specs + [HB],
        input_output_aliases=aliases,
        scratch_shapes=scratch,
        compiler_params=pltpu.CompilerParams(vmem_limit_bytes=VMEM_LIMIT),
        cost_estimate=pl.CostEstimate(
            flops=int((micros + 0.01) * COST), bytes_accessed=0, transcendentals=0
        ),
        **({} if grid is None else {"grid": grid}),
    )(*operands, *(array for array, unused in inplace), order.token)
    return results


def self_forward(order, row, me, lengths, gains, inputs, pieces):
    count = len(inputs)
    rows = count * TOK
    return call(
        order,
        functools.partial(self_forward_kernel, count, row, pieces[0]),
        "self_forward",
        [SM, SM, VM] + [VM] * count + [ANY] * pieces[0].pieces,
        [
            shape(rows, D, F32),
            shape(rows, D, BF),
            shape(rows, 3 * D, BF),
            jax.ShapeDtypeStruct((count * HEADS, TOK, TOK), BF),
            shape(rows, D, BF),
        ],
        [VM] * 5,
        [held_of(4), pltpu.SemaphoreType.DMA((32,))],
        (me, lengths, gains, *inputs, *pieces[1]),
        3.2 + 2.5 * count,
    )


def self_back(order, row, me, gains, inputs, grad_out, kept, pieces):
    count = len(inputs)
    rows = count * TOK
    return call(
        order,
        functools.partial(self_back_kernel, count, row, pieces[0]),
        "self_back",
        [SM, VM] + [VM] * count + [VM] * 5 + [ANY] * pieces[0].pieces,
        [shape(TOK, D, F32), shape(2, D, F32)] + made_of(pieces[0], 4),
        [VM, VM] + [HB] * pieces[0].made,
        [held_of(4), held_of(4), pltpu.VMEM((rows, 3 * D), BF), pltpu.SemaphoreType.DMA((32,))],
        (me, gains, *inputs, grad_out, *kept, *pieces[1]),
        5.8 + 3.4 * count,
    )


def cross_forward(order, row, me, src_lengths, tgt_lengths, gains, hidden, memory, pieces):
    return call(
        order,
        functools.partial(cross_forward_kernel, row, pieces[0]),
        "cross_forward",
        [SM, SM, SM, VM, VM, VM] + [ANY] * pieces[0].pieces,
        [
            shape(2 * TOK, D, F32),
            shape(2 * TOK, D, BF),
            shape(2 * TOK, D, BF),
            shape(TOK, 2 * D, BF),
            jax.ShapeDtypeStruct((2 * HEADS, TOK, TOK), BF),
            shape(2 * TOK, D, BF),
        ],
        [VM] * 6,
        [held_of(4), pltpu.SemaphoreType.DMA((32,))],
        (me, src_lengths, tgt_lengths, gains, hidden, memory, *pieces[1]),
        8,
    )


def cross_back(order, row, me, gains, hidden, memory, grad_out, kept, pieces, whole):
    return call(
        order,
        functools.partial(cross_back_kernel, row, pieces[0]),
        "cross_back",
        [SM, VM] + [VM] * 8 + [ANY] * pieces[0].pieces,
        [shape(2 * TOK, D, F32), shape(TOK, D, F32), shape(2, D, F32)] + made_of(pieces[0], 4),
        [VM, VM, VM] + [HB] * pieces[0].made,
        [held_of(4), held_of(4), pltpu.VMEM((2 * TOK, D), BF), pltpu.SemaphoreType.DMA((32,))],
        (me, gains, hidden, memory, grad_out, *kept, *pieces[1]),
        12.3,
        inplace=[(whole, 3)],
    )


def ffn_forward(order, row, me, gains, hidden, pieces):
    return call(
        order,
        functools.partial(ffn_forward_kernel, row, pieces[0]),
        "ffn_forward",
        [SM, VM, VM] + [ANY] * pieces[0].pieces,
        [shape(TOK, D, BF), shape(TOK, D, BF), shape(TOK, FF, BF), shape(TOK, FF, BF)],
        [VM] * 4,
        [held_of(8), pltpu.SemaphoreType.DMA((32,))],
        (me, gains, hidden, *pieces[1]),
        6.6,
    )


def ffn_back(order, row, me, gains, hidden, grad_out, kept, pieces):
    return call(
        order,
        functools.partial(ffn_back_kernel, row, pieces[0]),
        "ffn_back",
        [SM, VM, VM, VM, VM, VM, VM] + [ANY] * pieces[0].pieces,
        [shape(TOK, D, F32), shape(2, D, F32)] + made_of(pieces[0], 8),
        [VM, VM] + [HB] * pieces[0].made,
        [held_of(8), held_of(8), pltpu.SemaphoreType.DMA((32,))],
        (me, gains, hidden, grad_out, *kept, *pieces[1]),
        10.2,
    )


def ffn_both(order, row, me, gains, hidden, cot_first, cot_second, pieces):
    rows = 2 * TOK
    return call(
        order,
        functools.partial(ffn_both_kernel, row, pieces[0]),
        "ffn_both",
        [SM, VM, VM, VM, VM] + [ANY] * pieces[0].pieces,
        [shape(TOK, D, BF), shape(TOK, D, BF), shape(rows, D, F32), shape(2, D, F32)] + made_of(pieces[0], 8),
        [VM, VM, VM, VM] + [HB] * pieces[0].made,
        [
            held_of(8),
            held_of(8),
            pltpu.VMEM((rows, D), BF),
            pltpu.VMEM((rows, FF), BF),
            pltpu.VMEM((rows, FF), BF),
            pltpu.SemaphoreType.DMA((32,)),
        ],
        (me, gains, hidden, cot_first, cot_second, *pieces[1]),
        15.5,
    )


AXIS = "fsdp"
BOTH = ("dp", "fsdp")
SHARDS = 16


def route(target):
    pairs = []
    for i in range(2 * SHARDS):
        dp, z, y, core = target(i // 16, (i // 4) % 4, (i // 2) % 2, i % 2)
        pairs.append((i, dp * 16 + (z % 4) * 4 + y * 2 + core))
    return pairs


def to_core(x):
    return lax.ppermute(x, BOTH, route(lambda dp, z, y, core: (dp, z, y, 1 - core)))


def to_z(x, step):
    return lax.ppermute(x, BOTH, route(lambda dp, z, y, core: (dp, z + step, y, core)))


def to_z_pair(x, step):
    return lax.ppermute(x, BOTH, route(lambda dp, z, y, core: (dp, z ^ step, y, core)))


def to_y(x):
    return lax.ppermute(x, BOTH, route(lambda dp, z, y, core: (dp, z, 1 - y, core)))


def to_dp(x):
    return lax.ppermute(x, BOTH, route(lambda dp, z, y, core: (1 - dp, z, y, core)))


def to_yx(x):
    return lax.ppermute(
        x, BOTH, route(lambda dp, z, y, core: (dp, z, y ^ 1, core) if core == 0 else (dp ^ 1, z, y, core))
    )


def to_xy(x):
    return lax.ppermute(
        x, BOTH, route(lambda dp, z, y, core: (dp ^ 1, z, y, core) if core == 0 else (dp, z, y ^ 1, core))
    )


def blocks_of(shard):
    rows, cols = shard.shape
    split = shard.reshape(rows // BLOCK, BLOCK, cols // D, D)
    return split.transpose(2, 0, 1, 3).reshape(-1, BLOCK, D)


def shard_of(blocks, cols):
    wide = blocks.reshape(cols // D, -1, D)
    return wide.transpose(1, 0, 2).reshape(-1, cols)


def small(order, body, name, out, operands, scratch=(), in_specs=None, out_specs=None, micros=0, grid=None):
    return call(
        order,
        body,
        name,
        in_specs if in_specs is not None else [VM] * len(operands),
        [jax.ShapeDtypeStruct(dims, dtype) for dims, dtype in out],
        out_specs if out_specs is not None else [VM] * len(out),
        list(scratch),
        operands,
        micros,
        grid,
    )


def pack_kernel(place, *refs):
    weights, (one, two, three, norms) = refs[:15], refs[15:]
    self_in, self_out, enc_in, enc_out, enc_ffn_in, enc_ffn_out = weights[:6]
    cross_q, cross_kv, cross_out, ffn_in, ffn_out = weights[6:11]
    for half in range(2):

        @pl.when(place[2] == half)
        def _():
            for k in range(2):
                quarter = 2 * half + k
                cols = slice(quarter * D, (quarter + 1) * D)
                one[k, 0:32] = self_out[...] if quarter == 3 else self_in[:, cols]
                one[k, 32:64] = enc_out[...] if quarter == 3 else enc_in[:, cols]
                for j in range(2):
                    block = 2 * quarter + j
                    rows = slice(j * BLOCK, (j + 1) * BLOCK)
                    cols = slice(block * D, (block + 1) * D)
                    part = slice((block - 4) * BLOCK, (block - 3) * BLOCK)
                    three[k, rows] = ffn_in[:, cols] if block < 4 else ffn_out[part]

    for block in range(4):
        rows = slice(block * BLOCK, (block + 1) * BLOCK)
        two[rows] = enc_ffn_in[:, block * D : (block + 1) * D]
    two[128:256] = enc_ffn_out[...]
    two[256:288] = cross_q[...]
    two[288:320] = cross_kv[:, 0:D]
    two[320:352] = cross_kv[:, D : 2 * D]
    two[352:384] = cross_out[...]
    norms[...] = jnp.zeros(norms.shape, F32)
    row = 0
    for gain, bias in (weights[11:13], weights[13:15]):
        for k in range(gain.shape[0]):
            norms[row : row + 1, 0:BLOCK] = gain[k : k + 1].astype(F32)
            norms[row + 1 : row + 2, 0:BLOCK] = bias[k : k + 1].astype(F32)
            row += 2
    for k in range(2):
        one[k, 64:80] = norms[...].astype(BF)


def pack(order, place, weights, norms):
    return small(
        order,
        pack_kernel,
        "pack",
        [((2, 80, D), BF), ((384, D), BF), ((2, 64, D), BF)],
        (place, *weights, *norms),
        [pltpu.VMEM((16, D), F32)],
        in_specs=[SM] + [VM] * 15,
    )


def pair_kernel(place, *refs):
    core = place[3]
    for k in range(2):
        mine, near, pair = refs[2 * k], refs[2 * k + 1], refs[4 + k]
        pair[core] = mine[core]
        pair[1 - core] = near[core]


def pair_up(order, place, mine, near):
    operands = [x for both in zip(mine, near) for x in both]
    return small(
        order,
        pair_kernel,
        "pair_up",
        [(x.shape, x.dtype) for x in mine],
        (place, *operands),
        in_specs=[SM] + [VM] * 4,
    )


def stack_kernel(*refs):
    parts, (out, held, sems) = refs[:-3], refs[-3:]
    count = len(parts)
    loads = [pltpu.make_async_copy(parts[d], held.at[d], sems.at[d]) for d in range(count)]
    stores = [pltpu.make_async_copy(held.at[d], out.at[d], sems.at[count + d]) for d in range(count)]
    for copy in loads:
        copy.start()
    for d in range(count):
        loads[d].wait()
        stores[d].start()
    wait_all(stores)


def stack(order, parts):
    dims = (len(parts),) + parts[0].shape
    dtype = parts[0].dtype
    return small(
        order,
        stack_kernel,
        "stack",
        [(dims, dtype)],
        tuple(parts),
        [pltpu.VMEM(dims, dtype), pltpu.SemaphoreType.DMA((2 * len(parts),))],
        [ANY] * len(parts),
        [ANY],
    )[0]


def table_kernel(place, own, across, down, gains, held, sems):
    copies = []
    for k, piece in enumerate((own, across, down)):
        copies.append(pltpu.make_async_copy(piece.at[:, :, pl.ds(64, 16)], held.at[k], sems.at[k]))
    for copy in copies:
        copy.start()
    wait_all(copies)
    far = jnp.where(place[3] == 0, 2, 1)
    for y in range(2):
        where = jnp.where(place[1] == y, 0, far)
        for z in range(4):
            turn = (place[0] + (4 - z)) & 3
            for core in range(2):
                spot = 4 * z + 2 * y + core
                row = held[where, turn, core]
                gains[:, spot * BLOCK : (spot + 1) * BLOCK] = row[:, 0:BLOCK].astype(F32)


def norm_table(order, place, pieces):
    return small(
        order,
        table_kernel,
        "norm_table",
        [((16, D), F32)],
        (place, pieces[0], pieces[1], pieces[2]),
        [pltpu.VMEM((3, 4, 2, 16, D), BF), pltpu.SemaphoreType.DMA((3,))],
        [SM, ANY, ANY, ANY],
    )[0]


class Gather:
    def __init__(self, order, pair):
        self.order, self.pair = order, pair

    def along_z(self):
        pair = self.order.tie(self.pair)
        self.parts = [pair] + [to_z(pair, d) for d in (1, 2, 3)]

    def lined(self):
        self.line = stack(self.order, self.parts)

    def first_cross(self):
        line = self.order.tie(self.line)
        self.own = [line, to_xy(line), to_yx(line)]
        self.near = []

    def crossed(self, others=()):
        arrived = self.order.tie_all(self.own[1:3] + list(others[1:]))
        self.own[1:3] = arrived[:2]
        if others:
            others[1:] = arrived[2:]

    def second_cross(self):
        self.own.append(to_yx(self.own[1]))

    def share(self, k):
        self.near.append(self.order.tie(to_core(self.own[k])))

    def done(self):
        last = self.order.tie(self.own[3])
        self.own = self.own[:3] + [last]
        self.near.append(self.order.tie(to_core(last)))
        self.pieces = tuple(self.own + self.near)


def low_sum(*parts):
    total = parts[0].astype(F32)
    for part in parts[1:]:
        total = total + part.astype(F32)
    return total.astype(BF)


def rows_of(parts):
    row = 0
    for k, part in enumerate(parts[::2]):
        yield slice(row, row + part.shape[4]), part, parts[2 * k + 1]
        row += part.shape[4]


def reduce_first_kernel(norm_own, norm_came, *refs):
    sent, norm = refs[-2:]
    norm[...] = norm_own[...] + norm_came[...]
    for rows, own, came in rows_of(refs[:-2]):
        sent[:, :, :, rows] = own[0] + came[0]


def reduce_second_kernel(norm_own, norm_came, came_first, *refs):
    sent, norm = refs[-2:]
    norm[...] = norm_own[...] + norm_came[...]
    for rows, own, came in rows_of(refs[:-2]):
        sent[:, :, rows] = low_sum(own[0, 0], came[0, 0], came_first[0, :, :, rows])


def reduce_third_kernel(norm_own, norm_came, came_first, came_second, *refs):
    outs, norm = refs[-5:-1], refs[-1]
    norm[...] = norm_own[...] + norm_came[...]
    for rows, own, came in rows_of(refs[:-5]):
        for d in range(4):
            outs[d][:, rows] = low_sum(
                own[0, 0, d], came[0, 0, d], came_first[0, d, :, rows], came_second[d, :, rows]
            )


def reduce_fourth_kernel(norm_own, norm_came, a, b, c, d, out, norm):
    norm[...] = norm_own[...] + norm_came[...]
    out[...] = low_sum(a[...], b[...], c[...], d[...])


NORM_SPEC = pl.BlockSpec((16, D), lambda i: (0, 0))


class Reduce:
    def __init__(self, order):
        self.order, self.own, self.came = order, [], []

    def add(self, own, other):
        self.own.append(own)
        self.came.append(to_core(self.order.tie(other)))

    def arrive(self):
        self.came[-1] = self.order.tie(self.came[-1])

    def start_norm(self, norm):
        self.norm = self.order.tie(norm)
        self.norm_came = to_core(self.norm)

    def run(self, body, name, out, extra, in_specs, out_specs, grid):
        parts = [x for both in zip(self.own, self.came) for x in both]
        specs = [
            pl.BlockSpec(in_specs[-1][0] + (part.shape[4], D), in_specs[-1][1]) for part in parts
        ]
        *sent, norm = small(
            self.order,
            body,
            name,
            out + [((16, D), F32)],
            [self.norm, self.norm_came] + extra + parts,
            in_specs=[NORM_SPEC] * 2 + in_specs[:-1] + specs,
            out_specs=out_specs + [NORM_SPEC],
            grid=grid,
        )
        return [self.order.tie(x) for x in sent], self.order.tie(norm)

    def first(self):
        rows = self.rows = sum(own.shape[4] for own in self.own)
        (sent,), self.norm = self.run(
            reduce_first_kernel,
            "reduce_first",
            [((2, 4, 2, rows, D), BF)],
            [],
            [((1, 2, 1, 2), lambda i: (1, 0, i, 0, 0, 0))],
            [pl.BlockSpec((2, 1, 2, rows, D), lambda i: (0, i, 0, 0, 0))],
            (4,),
        )
        self.first_came = to_yx(sent)
        self.norm_came = to_y(self.norm)

    def second(self):
        rows = self.rows
        (sent,), self.norm = self.run(
            reduce_second_kernel,
            "reduce_second",
            [((4, 2, rows, D), BF)],
            [self.first_came],
            [
                pl.BlockSpec((1, 1, 2, rows, D), lambda i: (1, i, 0, 0, 0)),
                ((1, 1, 1, 2), lambda i: (0, 1, i, 0, 0, 0)),
            ],
            [pl.BlockSpec((1, 2, rows, D), lambda i: (i, 0, 0, 0))],
            (4,),
        )
        self.second_came = to_xy(sent)
        self.norm_came = to_z_pair(self.norm, 1)

    def third(self):
        rows = self.rows
        parts, self.norm = self.run(
            reduce_third_kernel,
            "reduce_third",
            [((2, rows, D), BF)] * 4,
            [self.first_came, self.second_came],
            [
                pl.BlockSpec((1, 4, 2, rows, D), lambda i: (0, 0, 0, 0, 0)),
                pl.BlockSpec((4, 2, rows, D), lambda i: (0, 0, 0, 0)),
                ((1, 1, 4, 2), lambda i: (0, 0, 0, 0, 0, 0)),
            ],
            [pl.BlockSpec((2, rows, D), lambda i: (0, 0, 0))] * 4,
            (1,),
        )
        self.lines = [parts[0]] + [to_z(parts[d], d) for d in (1, 2, 3)]
        self.norm_came = to_z_pair(self.norm, 2)

    def fourth(self):
        total, norm = small(
            self.order,
            reduce_fourth_kernel,
            "reduce_fourth",
            [(self.lines[0].shape, BF), ((16, D), F32)],
            [self.norm, self.norm_came] + self.lines,
        )
        total, self.norm = self.order.tie(total), self.order.tie(norm)
        self.ends = [total, to_dp(total), to_core(total)]
        self.norm_came = to_dp(self.norm)

    def last(self):
        near = self.order.tie(self.ends[2])
        came = self.order.tie(self.ends[1])
        self.ends = [self.ends[0], came, near, to_core(came)]


def quarter_of(place, ends, quarter, rows):
    core = place[3]
    half, which = quarter >> 1, quarter & 1
    first = jnp.where(place[3] == which, ends[0][core, rows], ends[2][core, rows].astype(BF))
    second = jnp.where(place[3] == which, ends[1][core, rows], ends[3][core, rows])
    return jnp.where(place[2] == half, first, second).astype(F32)


def unpack_kernel(layout, place, *refs):
    ends, outs = refs[:4], refs[4:]
    first = 0
    for kind, row in layout:
        for quarter in range(4):
            if kind == "ffn":
                for j in range(2):
                    block = 2 * quarter + j
                    rows = slice(row + j * BLOCK, row + (j + 1) * BLOCK)
                    value = quarter_of(place, ends, quarter, rows)
                    if block < 4:
                        outs[first][:, block * D : (block + 1) * D] = value
                    else:
                        outs[first + 1][(block - 4) * BLOCK : (block - 3) * BLOCK] = value
            else:
                value = quarter_of(place, ends, quarter, slice(row, row + BLOCK))
                if kind == "attn":
                    if quarter < 3:
                        outs[first][:, quarter * D : (quarter + 1) * D] = value
                    else:
                        outs[first + 1][...] = value
                elif quarter in (1, 2):
                    outs[first + 1][:, (quarter - 1) * D : quarter * D] = value
                else:
                    outs[first + (quarter + 1) // 2][...] = value
        first += 3 if kind == "cross" else 2


SHARD_SHAPES = {
    "ffn": [((BLOCK, FF), F32), ((4 * BLOCK, D), F32)],
    "attn": [((BLOCK, 3 * D), F32), ((BLOCK, D), F32)],
    "cross": [((BLOCK, D), F32), ((BLOCK, 2 * D), F32), ((BLOCK, D), F32)],
}


def unpack(order, place, ends, layout):
    return small(
        order,
        functools.partial(unpack_kernel, layout),
        "unpack",
        [item for kind, unused in layout for item in SHARD_SHAPES[kind]],
        (place, *ends),
        in_specs=[SM] + [VM] * 4,
    )


def norm_join_kernel(*refs):
    parts, out = refs[:5], refs[5]
    out[...] = jnp.zeros(out.shape, F32)
    for k in range(5):
        out[2 * k : 2 * k + 2] = parts[k][...]


def norm_last_kernel(place, own, came, *outs):
    total = own[...] + came[...]
    spot = place[0] * 4 + place[1] * 2 + place[3]
    turned = jnp.zeros((16, BLOCK), F32)
    for k in range(SHARDS):
        turned = jnp.where(spot == k, total[:, k * BLOCK : (k + 1) * BLOCK], turned)
    for first, gain, bias in ((0, outs[0], outs[1]), (4, outs[2], outs[3])):
        for k in range(gain.shape[0]):
            gain[k : k + 1] = turned[first + 2 * k : first + 2 * k + 1]
            bias[k : k + 1] = turned[first + 2 * k + 1 : first + 2 * k + 2]


def norm_last(order, place, own, came):
    return small(
        order,
        norm_last_kernel,
        "norm_last",
        [((2, BLOCK), F32), ((2, BLOCK), F32), ((3, BLOCK), F32), ((3, BLOCK), F32)],
        (place, own, came),
        in_specs=[SM, VM, VM],
    )


def spread_kernel(own, came, ffn_in, ffn_out, cross_q, cross_kv, cross_out):
    total = own[...].astype(F32) + came[...].astype(F32)
    for block in range(4):
        ffn_in[:, block * D : (block + 1) * D] = total[block * BLOCK : (block + 1) * BLOCK]
    ffn_out[...] = total[128:256]
    cross_q[...] = total[256:288]
    cross_kv[:, 0:D] = total[288:320]
    cross_kv[:, D : 2 * D] = total[320:352]
    cross_out[...] = total[352:384]


def spread(order, own, came):
    return small(
        order,
        spread_kernel,
        "spread",
        SHARD_SHAPES["ffn"] + SHARD_SHAPES["cross"],
        (own, came),
    )


def gather_plain(weights):
    parts = []
    for weight in weights:
        whole = lax.all_gather(weight, AXIS, axis=0, tiled=True)
        parts.append(jax.vmap(blocks_of)(whole.reshape(SHARDS, -1, whole.shape[1])))
    return jnp.concatenate(parts, axis=1).reshape(4, 4, -1, D)


def reduce_plain(made, columns):
    shards = made.reshape(SHARDS, -1, BLOCK, D)
    grads = []
    for first, last, cols in columns:
        whole = jax.vmap(functools.partial(shard_of, cols=cols))(shards[:, first:last])
        whole = whole.reshape(-1, cols).astype(F32)
        part = lax.psum_scatter(whole, AXIS, scatter_dimension=0, tiled=True)
        grads.append(lax.psum(part.astype(BF), "dp").astype(F32))
    return grads


def norm_rows_of(gain_enc, bias_enc, gain_dec, bias_dec):
    rows = []
    for gain, bias in ((gain_enc, bias_enc), (gain_dec, bias_dec)):
        for k in range(gain.shape[0]):
            rows += [gain[k : k + 1], bias[k : k + 1]]
    return jnp.concatenate(rows, axis=0)


ATTN_COLUMNS = ((0, 3, 3 * D), (3, 4, D))
FFN_COLUMNS = ((0, 4, FF), (4, 8, D))
CROSS_COLUMNS = ((0, 1, D), (1, 3, 2 * D), (3, 4, D))


def step(
    custom,
    source,
    first_in,
    second_in,
    cot_first,
    cot_second,
    src_lengths,
    tgt_lengths,
    enc_attn_in,
    enc_attn_out,
    enc_ffn_in,
    enc_ffn_out,
    enc_gain,
    enc_bias,
    dec_self_in,
    dec_self_out,
    dec_cross_q,
    dec_cross_kv,
    dec_cross_out,
    dec_ffn_in,
    dec_ffn_out,
    dec_gain,
    dec_bias,
):
    spot = lax.axis_index(AXIS)
    order = Order()
    group_self = (dec_self_in, dec_self_out)
    group_enc = (enc_attn_in, enc_attn_out)
    group_enc_ffn = (enc_ffn_in, enc_ffn_out)
    group_cross = (dec_cross_q, dec_cross_kv, dec_cross_out)
    group_ffn = (dec_ffn_in, dec_ffn_out)
    if custom:
        place = jnp.stack([spot >> 2, (spot >> 1) & 1, lax.axis_index("dp"), spot & 1]).astype(jnp.int32)
        weights = group_self + group_enc + group_enc_ffn + group_cross + group_ffn
        mine_one, mine_two, mine_three = pack(
            order, place, weights, (enc_gain, enc_bias, dec_gain, dec_bias)
        )
        whole = lax.all_gather(mine_two, AXIS, axis=0, tiled=True).reshape(4, 4, -1, D)
        mine = (mine_one, mine_three)
        pairs = pair_up(order, place, mine, [to_core(x) for x in mine])
        one, three = (Gather(order, pair) for pair in pairs)
        one.along_z()
        one.lined()
        one.first_cross()
        three.along_z()
        one.crossed(three.parts)
        one.second_cross()
        for k in range(3):
            one.share(k)
        one.done()
        gains = norm_table(order, place, one.pieces)
        three.lined()
        three.first_cross()
        w_self, w_enc = (Layout(0, 8), one.pieces), (Layout(32, 8), one.pieces)
        w_enc_ffn = (Layout(0, 1), (whole,))
        w_cross = (Layout(256, 1, 1, 256, 384), (whole,))
    else:
        place = jnp.zeros((4,), jnp.int32)
        w_self, w_enc, w_enc_ffn = (
            (Layout(0, 1, 1, 0, rows), (gather_plain(group),))
            for group, rows in ((group_self, 128), (group_enc, 128), (group_enc_ffn, 256))
        )
        w_cross = (Layout(0, 1, 1, 256, 384), (gather_plain(group_cross),))
        w_ffn = (Layout(0, 1, 1, 0, 384), (gather_plain(group_ffn),))
        norm_rows = norm_rows_of(enc_gain, enc_bias, dec_gain, dec_bias)
        gains = lax.all_gather(norm_rows, AXIS, axis=1, tiled=True)
        gains = jnp.pad(gains.astype(F32), ((0, 6), (0, 0)))

    hidden_one, *kept_self = self_forward(
        order, 4, place, tgt_lengths, gains, [first_in, second_in], w_self
    )
    if custom:
        three.crossed()
        three.second_cross()
        for k in range(3):
            three.share(k)
    hidden_enc, *kept_enc = self_forward(order, 0, place, src_lengths, gains, [source], w_enc)
    if custom:
        three.done()
        w_ffn = (Layout(0, 8, 1, 0, 384), three.pieces)
    memory, *kept_enc_ffn = ffn_forward(order, 2, place, gains, hidden_enc, w_enc_ffn)
    hidden_two, *kept_cross = cross_forward(
        order, 6, place, src_lengths, tgt_lengths, gains, hidden_one, memory, w_cross
    )
    first_out, second_out, grad_two, norm_ffn, made = ffn_both(
        order, 8, place, gains, hidden_two, cot_first, cot_second, w_ffn
    )
    grad_one, grad_memory, norm_cross, made = cross_back(
        order, 6, place, gains, hidden_one, memory, grad_two, kept_cross, w_cross, made
    )
    if custom:
        scattered = lax.psum_scatter(
            made.reshape(-1, D), AXIS, scatter_dimension=0, tiled=True
        )
    grad_enc, norm_enc_ffn, *made_enc_ffn = ffn_back(
        order, 2, place, gains, hidden_enc, grad_memory, kept_enc_ffn, w_enc_ffn
    )
    if custom:
        red = Reduce(order)
        red.add(*made_enc_ffn)
    grad_first, norm_self, *made_self = self_back(
        order, 4, place, gains, [first_in, second_in], grad_one, kept_self, w_self
    )
    if custom:
        red.arrive()
        red.add(*made_self)
    grad_source, norm_enc, *made_enc = self_back(
        order, 0, place, gains, [source], grad_enc, kept_enc, w_enc
    )
    if custom:
        red.arrive()
        red.add(*made_enc)
        (norm_total,) = small(
            order,
            norm_join_kernel,
            "norm_join",
            [((16, D), F32)],
            (norm_enc, norm_enc_ffn, norm_self, norm_cross, norm_ffn),
        )
        red.start_norm(norm_total)
        red.first()
        red.second()
        red.third()
        scattered = order.tie(scattered)
        scattered_came = to_dp(scattered)
        red.fourth()
        red.last()
        grads_ffn_cross = spread(order, scattered, scattered_came)
        norm_grads = norm_last(order, place, red.norm, red.norm_came)
        grads_ffn, grads_cross = grads_ffn_cross[:2], grads_ffn_cross[2:]
        g = unpack(order, place, red.ends, (("ffn", 0), ("attn", 64), ("attn", 96)))
        grads_enc_ffn, grads_self, grads_enc = g[:2], g[2:4], g[4:6]
    else:
        norm_grads = jnp.concatenate(
            [norm_enc, norm_enc_ffn, norm_self, norm_cross, norm_ffn], axis=0
        )
        grads_ffn = reduce_plain(made[:, :, 0:256], FFN_COLUMNS)
        grads_cross = reduce_plain(made[:, :, 256:384], CROSS_COLUMNS)
        grads_enc_ffn = reduce_plain(*made_enc_ffn, FFN_COLUMNS)
        grads_self = reduce_plain(*made_self, ATTN_COLUMNS)
        grads_enc = reduce_plain(*made_enc, ATTN_COLUMNS)
        norm_shard = lax.psum_scatter(norm_grads, AXIS, scatter_dimension=1, tiled=True)
        norm_shard = lax.psum(norm_shard.astype(BF), "dp").astype(F32)
        norm_grads = (norm_shard[0:4:2], norm_shard[1:4:2], norm_shard[4:10:2], norm_shard[5:10:2])
    return (
        first_out,
        second_out,
        grad_source,
        grad_first,
        *grads_enc,
        *grads_enc_ffn,
        *norm_grads[:2],
        *grads_self,
        *grads_cross,
        *grads_ffn,
        *norm_grads[2:],
    )


def solution(mesh):
    blocked = P(("dp", "fsdp"), None)
    rows = P("fsdp", None)
    columns = P(None, "fsdp")
    custom = mesh.shape["fsdp"] == SHARDS and mesh.shape["dp"] == 2
    return jax.shard_map(
        functools.partial(step, custom),
        mesh=mesh,
        in_specs=(blocked,) * 7 + (rows,) * 4 + (columns,) * 2 + (rows,) * 7 + (columns,) * 2,
        out_specs=(blocked,) * 4 + (rows,) * 4 + (columns,) * 2 + (rows,) * 7 + (columns,) * 2,
        check_vma=False,
    )
```

```python
import functools
import typing

import jax
import jax.numpy as jnp
from jax import lax
from jax.experimental import pallas as pl
from jax.experimental.pallas import tpu as pltpu
from jax.sharding import PartitionSpec as P

D = 512
HEADS = 8
HEAD = 64
TOK = 256
FF = 2048
QUAD = 256
BLOCK = 32
EPSILON = 1e-05
MASKED = -1000000000.0
BF = jnp.bfloat16
F32 = jnp.float32
VMEM_LIMIT = 64 * 1024 * 1024
COST = 1.1e9


class Layout(typing.NamedTuple):
    offset: int
    pieces: int
    made: int = 2
    made_offset: int = 0
    made_rows: int = 0


def dot(left, right):
    return lax.dot_general(left, right, (((1,), (0,)), ((), ())), preferred_element_type=F32)


def dot_nt(left, right):
    return lax.dot_general(left, right, (((1,), (1,)), ((), ())), preferred_element_type=F32)


def dot_tn(left, right):
    return lax.dot_general(left, right, (((0,), (0,)), ((), ())), preferred_element_type=F32)


def wait_all(copies):
    for copy in copies:
        copy.wait()


def column_block(held, index):
    return held[:, :, index * BLOCK : (index + 1) * BLOCK].reshape(D, D)


def row_block(held, index):
    return held[index, :, 4 * BLOCK : 8 * BLOCK].reshape(D, D)


def normed_of(values):
    centre = values - jnp.mean(values, axis=-1, keepdims=True)
    spread = jnp.mean(centre * centre, axis=-1, keepdims=True)
    inverse = lax.rsqrt(spread + EPSILON)
    return centre * inverse, inverse


def norm_back(unit, inverse, gain, grad_normed, norm_ref):
    norm_ref[0:1] = jnp.sum(grad_normed * unit, axis=0, keepdims=True)
    norm_ref[1:2] = jnp.sum(grad_normed, axis=0, keepdims=True)
    grad_unit = grad_normed * gain
    return (
        grad_unit
        - jnp.mean(grad_unit, axis=-1, keepdims=True)
        - unit * jnp.mean(grad_unit * unit, axis=-1, keepdims=True)
    ) * inverse


def mask_bias(key_lengths, query_lengths):
    key_place = lax.broadcasted_iota(jnp.int32, (TOK, 1), 0)
    query_place = lax.broadcasted_iota(jnp.int32, (1, TOK), 1)
    key_ids = jnp.zeros((TOK, 1), jnp.int32)
    query_ids = jnp.zeros((1, TOK), jnp.int32)
    key_end = jnp.int32(0)
    query_end = jnp.int32(0)
    for k in range(key_lengths.shape[1]):
        key_end = key_end + key_lengths[0, k]
        query_end = query_end + query_lengths[0, k]
        key_ids = key_ids + jnp.where(key_place >= key_end, 1, 0)
        query_ids = query_ids + jnp.where(query_place >= query_end, 1, 0)
    return jnp.where(key_ids == query_ids, 0.0, MASKED).astype(F32)


def lane_masks():
    head_of = lax.broadcasted_iota(jnp.int32, (1, QUAD), 1) // HEAD
    return [jnp.where(head_of == h, 1.0, 0.0).astype(BF) for h in range(QUAD // HEAD)]


def attend(queries, keys, values, bias, probs_ref, first):
    masks = lane_masks()
    outs = []
    for g in range(D // QUAD):
        cols = slice(g * QUAD, (g + 1) * QUAD)
        q, k, v = queries[:, cols], keys[:, cols], values[:, cols]
        total = None
        for h in range(QUAD // HEAD):
            scores = dot_nt(k * (masks[h] * (HEAD**-0.5)), q) + bias
            top = jnp.max(scores, axis=0, keepdims=True)
            grown = jnp.exp(scores - top)
            probs = (grown * (1.0 / jnp.sum(grown, axis=0, keepdims=True))).astype(BF)
            probs_ref[first + g * (QUAD // HEAD) + h] = probs
            part = dot_tn(probs, v * masks[h])
            total = part if total is None else total + part
        outs.append(total.astype(BF))
    return jnp.concatenate(outs, axis=1)


def attend_back(queries, keys, values, probs_ref, first, grad_mixed):
    masks = lane_masks()
    grads = []
    for g in range(D // QUAD):
        cols = slice(g * QUAD, (g + 1) * QUAD)
        q, k, v, go = queries[:, cols], keys[:, cols], values[:, cols], grad_mixed[:, cols]
        gq = gk = gv = None
        for h in range(QUAD // HEAD):
            probs_low = probs_ref[first + g * (QUAD // HEAD) + h]
            probs = probs_low.astype(F32)
            grad_probs = dot_nt(v * masks[h], go)
            both = probs * grad_probs
            grad_scores = (both - probs * jnp.sum(both, axis=0, keepdims=True)).astype(BF)
            part_v = dot(probs_low, go * masks[h])
            part_k = dot(grad_scores, q * masks[h])
            part_q = dot_tn(grad_scores, k * masks[h])
            gv = part_v if gv is None else gv + part_v
            gk = part_k if gk is None else gk + part_k
            gq = part_q if gq is None else gq + part_q
        grads.append((gq * (HEAD**-0.5), gk * (HEAD**-0.5), gv))
    return tuple(jnp.concatenate(parts, axis=1) for parts in zip(*grads))


def put_block(held, index, product):
    held[:, :, index * BLOCK : (index + 1) * BLOCK] = product.astype(BF).reshape(4, 4, BLOCK, D)


class Copies:
    def __init__(self, sems):
        self.sems, self.count, self.out = sems, 0, []

    def start(self, source, target):
        copy = pltpu.make_async_copy(source, target, self.sems.at[self.count])
        self.count += 1
        copy.start()
        return copy

    def load(self, source, target):
        return Loaded(target, [self.start(source, target)])

    def store(self, source, target):
        self.out.append(self.start(source, target))

    def finish(self):
        wait_all(self.out)

    def fetch(self, place, pieces, layout, held):
        rows = held.shape[2] // 4
        if layout.pieces == 1:
            loads = []
            for half in range(2):
                part = pieces[0].at[:, :, pl.ds(layout.offset + 2 * half * rows, 2 * rows)]
                loads.append(self.load(part, held.at[:, :, pl.ds(2 * half * rows, 2 * rows)]))
            return loads
        copies = []
        for turn in range(2):
            for first in range(2):
                for second in range(2):
                    y, half, which = place_of(place, turn, first, second)
                    quarter = pl.multiple_of((2 * half + which) * rows, rows)
                    piece = pieces[4 * turn + 2 * first + second]
                    copies.append(
                        self.start(
                            piece.at[:, :, pl.ds(layout.offset, rows)],
                            held.at[:, pl.ds(2 * y, 2), pl.ds(quarter, rows)],
                        )
                    )
        return [Loaded(held, copies)] * 2

    def deliver(self, place, held, layout, outs, *quarters):
        rows = held.shape[2] // 4
        if layout.made == 1:
            for quarter in (q for q in quarters if q < 4):
                part = pl.ds(layout.made_offset + quarter * rows, rows)
                self.store(held.at[:, :, pl.ds(quarter * rows, rows)], outs[0].at[:, :, part])
        elif 4 in quarters:
            for turn in range(2):
                for first in range(2):
                    for second in range(2):
                        y, half, which = place_of(place, turn, first, second)
                        quarter = pl.multiple_of((2 * half + which) * rows, rows)
                        self.store(
                            held.at[:, pl.ds(2 * y, 2), pl.ds(quarter, rows)],
                            outs[turn].at[first, second],
                        )


def place_of(place, turn, first, second):
    which = place[3] ^ turn
    y = place[1] ^ jnp.where(which == 0, first, second)
    half = place[2] ^ jnp.where(which == 0, second, first)
    return y, half, which


class Loaded:
    def __init__(self, target, copies):
        self.target, self.copies = target, copies

    def arrive(self):
        wait_all(self.copies)
        self.copies.clear()
        return self.target

    def __getitem__(self, index):
        return self.arrive()[index]


def self_forward_part(copies, row, gains, bias, inputs, loads, held, scratch, outs):
    out, normed, joined, probs, mixed = scratch
    out_ref, normed_ref, joined_ref, probs_ref, mixed_ref = outs
    passes = len(inputs)
    for p in range(passes):
        rows = slice(p * TOK, (p + 1) * TOK)
        unit, unused = normed_of(inputs[p][...].astype(F32))
        normed[rows] = (unit * gains[row : row + 1] + gains[row + 1 : row + 2]).astype(BF)
    copies.store(normed, normed_ref)
    for b in range(3):
        loads[b // 2].arrive()
        joined[:, b * D : (b + 1) * D] = dot(normed[...], column_block(held, b)).astype(BF)
    copies.store(joined, joined_ref)
    for p in range(passes):
        rows = slice(p * TOK, (p + 1) * TOK)
        mixed_part = attend(
            joined[rows, 0:D], joined[rows, D : 2 * D], joined[rows, 2 * D : 3 * D], bias, probs, p * HEADS
        )
        heads = pl.ds(p * HEADS, HEADS)
        copies.store(probs.at[heads], probs_ref.at[heads])
        mixed[rows] = mixed_part
        out[rows] = inputs[p][...].astype(F32) + dot(mixed_part, column_block(held, 3))
    copies.store(out, out_ref)
    copies.store(mixed, mixed_ref)


def self_forward_kernel(decoder, encoder, me_ref, src_lengths, tgt_lengths, gains, *refs):
    taken, refs = refs[:3], refs[3:]
    pieces, refs = refs[: decoder.pieces], refs[decoder.pieces :]
    more, refs = refs[: encoder.pieces], refs[encoder.pieces :]
    outs, scratch, (held, held_enc, *come, sems) = refs[:10], refs[10:20], refs[20:]
    copies = Copies(sems)
    inputs = [copies.load(taken[p], come[p]) for p in range(3)]
    loads = copies.fetch(me_ref, pieces, decoder, held)
    loads_enc = copies.fetch(me_ref, more, encoder, held_enc)
    bias = mask_bias(tgt_lengths, tgt_lengths)
    self_forward_part(copies, 4, gains, bias, inputs[:2], loads, held, scratch[:5], outs[:5])
    bias = mask_bias(src_lengths, src_lengths)
    self_forward_part(copies, 0, gains, bias, inputs[2:], loads_enc, held_enc, scratch[5:], outs[5:])
    copies.finish()


def self_back_kernel(passes, row, layout, me_ref, gains, *refs):
    inputs, refs = refs[:passes], refs[passes:]
    taken, refs = refs[:5], refs[5:]
    pieces, refs = refs[: layout.pieces], refs[layout.pieces :]
    grad_in_ref, norm_ref, *refs = refs
    outs, refs = refs[: layout.made], refs[layout.made :]
    grad_in, held, made, back, grad_out, normed, joined, probs, mixed, *come, sems = refs
    copies = Copies(sems)
    grad_out = copies.load(taken[0], grad_out)
    mixed = copies.load(taken[4], mixed)
    loads = copies.fetch(me_ref, pieces, layout, held)
    probs = [
        copies.load(taken[3].at[pl.ds(p * HEADS, HEADS)], probs.at[pl.ds(p * HEADS, HEADS)])
        for p in range(passes)
    ]
    joined = copies.load(taken[2], joined)
    normed = copies.load(taken[1], normed)
    inputs = [copies.load(inputs[p], come[p]) for p in range(passes)]
    grad_low = grad_out[...].astype(BF)
    put_block(made, 3, dot_tn(mixed[...], grad_low))
    copies.deliver(me_ref, made, layout, outs, 3)
    loads[1].arrive()
    grad_mixed = dot_nt(grad_low, column_block(held, 3)).astype(BF)
    for p in range(passes):
        rows = slice(p * TOK, (p + 1) * TOK)
        grads = attend_back(
            joined[rows, 0:D],
            joined[rows, D : 2 * D],
            joined[rows, 2 * D : 3 * D],
            probs[p].arrive(),
            0,
            grad_mixed[rows],
        )
        for b in range(3):
            back[rows, b * D : (b + 1) * D] = grads[b].astype(BF)
    loads[0].arrive()
    for b in range(3):
        part = back[:, b * D : (b + 1) * D]
        put_block(made, b, dot_tn(normed[...], part))
        copies.deliver(me_ref, made, layout, outs, b)
    copies.deliver(me_ref, made, layout, outs, 4)
    grad_normed = None
    for b in range(3):
        step = dot_nt(back[:, b * D : (b + 1) * D], column_block(held, b))
        grad_normed = step if grad_normed is None else grad_normed + step
    units = [normed_of(inputs[p][...].astype(F32)) for p in range(passes)]
    unit = jnp.concatenate([u[0] for u in units], axis=0)
    inverse = jnp.concatenate([u[1] for u in units], axis=0)
    grad = norm_back(unit, inverse, gains[row : row + 1], grad_normed, norm_ref)
    grad_in[...] = grad_out[0:TOK] + grad[0:TOK]
    copies.store(grad_in, grad_in_ref)
    copies.finish()


GELU_SCALE = 0.7978845608028654
GELU_CUBE = 0.044715


def gelu_both(up):
    square = up * up
    bent = jnp.tanh(GELU_SCALE * up * (1.0 + GELU_CUBE * square))
    half = 0.5 * (1.0 + bent)
    slope = half + 0.5 * up * (1.0 - bent * bent) * (
        GELU_SCALE * (1.0 + (3.0 * GELU_CUBE) * square)
    )
    return up * half, slope


def ffn_grads(copies, place, layout, outs, gain, hidden, grad_low, normed, active, slope, norm_ref, held, made):
    for z in range(4):
        product = dot_tn(active[:, z * D : (z + 1) * D], grad_low)
        made[z, :, 4 * BLOCK : 8 * BLOCK] = product.astype(BF).reshape(4, 4 * BLOCK, D)
    copies.deliver(place, made, layout, outs, 2)
    copies.deliver(place, made, layout, outs, 3)
    grad_normed = None
    for b in range(4):
        cols = slice(b * D, (b + 1) * D)
        grad_active = dot_nt(grad_low, row_block(held, b))
        grad_up = (slope[:, cols].astype(F32) * grad_active).astype(BF)
        put_block(made, b, dot_tn(normed[...], grad_up))
        if b % 2 == 1:
            copies.deliver(place, made, layout, outs, b // 2)
        step = dot_nt(grad_up, column_block(held, b))
        grad_normed = step if grad_normed is None else grad_normed + step
    copies.deliver(place, made, layout, outs, 4)
    unit, inverse = normed_of(hidden)
    return norm_back(unit, inverse, gain, grad_normed, norm_ref)


def ffn_back_kernel(row, layout, me_ref, gains, *refs):
    taken, refs = refs[:5], refs[5:]
    pieces, refs = refs[: layout.pieces], refs[layout.pieces :]
    grad_in_ref, norm_ref, *refs = refs
    outs, refs = refs[: layout.made], refs[layout.made :]
    grad_in, held, made, hidden, grad_out, normed, active, slope, sems = refs
    copies = Copies(sems)
    grad_out = copies.load(taken[1], grad_out)
    active = copies.load(taken[3], active)
    loads = copies.fetch(me_ref, pieces, layout, held)
    slope = copies.load(taken[4], slope)
    normed = copies.load(taken[2], normed)
    hidden = copies.load(taken[0], hidden)
    grad_low = grad_out[...].astype(BF)
    active = active.arrive()
    for load in loads:
        load.arrive()
    hidden.arrive()
    grad = ffn_grads(
        copies, me_ref, layout, outs, gains[row : row + 1], hidden[...], grad_low, normed, active, slope, norm_ref, held, made
    )
    grad_in[...] = grad_out[...] + grad
    copies.store(grad_in, grad_in_ref)
    copies.finish()


def second_kernel(encoder, cross, me_ref, src_lengths, tgt_lengths, gains, *refs):
    taken, whole, refs = refs[:2], refs[2:4], refs[4:]
    sent, made, (held_enc, held_cross, hidden_enc, hidden_one, sems) = refs[:10], refs[10:20], refs[20:]
    normed_enc, active_enc, slope_enc, memory, normed, query, pair, probs, mixed, hidden = made
    copies = Copies(sems)
    hidden_enc = copies.load(taken[0], hidden_enc)
    loads_enc = copies.fetch(me_ref, whole[:1], encoder, held_enc)
    hidden_one = copies.load(taken[1], hidden_one)
    loads_cross = copies.fetch(me_ref, whole[1:], cross, held_cross)

    unit, unused = normed_of(hidden_enc[...])
    normed_enc[...] = (unit * gains[2:3] + gains[3:4]).astype(BF)
    copies.store(normed_enc, sent[0])
    unit, unused = normed_of(hidden_one[...])
    normed[...] = (unit * gains[6:7] + gains[7:8]).astype(BF)
    copies.store(normed, sent[4])
    loads_enc[0].arrive()
    for b in range(4):
        cols = slice(b * D, (b + 1) * D)
        grown, bent = gelu_both(dot(normed_enc[...], column_block(held_enc, b)))
        active_enc[:, cols] = grown.astype(BF)
        slope_enc[:, cols] = bent.astype(BF)
    copies.store(active_enc, sent[1])
    copies.store(slope_enc, sent[2])
    loads_enc[1].arrive()
    total = hidden_enc[...]
    for z in range(4):
        total = total + dot(active_enc[:, z * D : (z + 1) * D], row_block(held_enc, z))
    memory[...] = total.astype(BF)
    copies.store(memory, sent[3])

    loads_cross[0].arrive()
    query[...] = dot(normed[...], column_block(held_cross, 0)).astype(BF)
    copies.store(query, sent[5])
    pair[:, 0:D] = dot(memory[...], column_block(held_cross, 1)).astype(BF)
    loads_cross[1].arrive()
    pair[:, D : 2 * D] = dot(memory[...], column_block(held_cross, 2)).astype(BF)
    copies.store(pair, sent[6])
    bias = mask_bias(src_lengths, tgt_lengths)
    for p in range(2):
        rows = slice(p * TOK, (p + 1) * TOK)
        part = attend(query[rows], pair[:, 0:D], pair[:, D : 2 * D], bias, probs, p * HEADS)
        heads = pl.ds(p * HEADS, HEADS)
        copies.store(probs.at[heads], sent[7].at[heads])
        mixed[rows] = part
        hidden[rows] = hidden_one[rows] + dot(part, column_block(held_cross, 3))
    copies.store(mixed, sent[8])
    copies.store(hidden, sent[9])
    copies.finish()


def middle_kernel(cross, decoder, me_ref, gains, *refs):
    taken, whole, refs = refs[:10], refs[10:11], refs[11:]
    pieces, refs = refs[: decoder.pieces], refs[decoder.pieces :]
    norm_ffn, norm_cross, *refs = refs
    sent, refs = refs[:5], refs[5:]
    come, refs = refs[:10], refs[10:]
    held_cross, held, made_cross, made, first_out, second_out, grad_memory, grad_one, *refs = refs
    normed_two, active, slope, grad_two, back, sems = refs
    copies = Copies(sems)
    hidden = copies.load(taken[0], come[0])
    loads = copies.fetch(me_ref, pieces, decoder, held)
    cots = [copies.load(taken[k], come[k]) for k in (1, 2)]
    loads_cross = copies.fetch(me_ref, whole, cross, held_cross)
    mixed, probs, query, pair, normed, memory, hidden_one = (
        copies.load(taken[k], come[k]) for k in range(3, 10)
    )

    unit, unused = normed_of(hidden[...])
    normed_two[...] = (unit * gains[8:9] + gains[9:10]).astype(BF)
    loads[0].arrive()
    for b in range(4):
        cols = slice(b * D, (b + 1) * D)
        grown, bent = gelu_both(dot(normed_two[...], column_block(held, b)))
        active[:, cols] = grown.astype(BF)
        slope[:, cols] = bent.astype(BF)
    loads[1].arrive()
    total = hidden[...]
    for z in range(4):
        total = total + dot(active[:, z * D : (z + 1) * D], row_block(held, z))
    first_out[...] = total[0:TOK].astype(BF)
    second_out[...] = total[TOK:].astype(BF)
    copies.store(first_out, sent[0])
    copies.store(second_out, sent[1])
    grad_low = jnp.concatenate([cots[0][...], cots[1][...]], axis=0)
    grad = ffn_grads(
        copies, me_ref, decoder, sent[4:], gains[8:9], hidden[...], grad_low, normed_two, active, slope, norm_ffn, held, made
    )
    grad_two[...] = grad_low.astype(F32) + grad

    grad_low = grad_two[...].astype(BF)
    put_block(made_cross, 3, dot_tn(mixed[...], grad_low))
    copies.deliver(me_ref, made_cross, cross, sent[4:], 3)
    loads_cross[1].arrive()
    grad_mixed = dot_nt(grad_low, column_block(held_cross, 3)).astype(BF)
    grad_key = grad_value = None
    probs = probs.arrive()
    for p in range(2):
        rows = slice(p * TOK, (p + 1) * TOK)
        grads = attend_back(
            query[rows], pair[:, 0:D], pair[:, D : 2 * D], probs, p * HEADS, grad_mixed[rows]
        )
        back[rows] = grads[0].astype(BF)
        grad_key = grads[1] if grad_key is None else grad_key + grads[1]
        grad_value = grads[2] if grad_value is None else grad_value + grads[2]
    grad_key = grad_key.astype(BF)
    grad_value = grad_value.astype(BF)
    for b, (left, right) in enumerate(
        ((normed[...], back[...]), (memory[...], grad_key), (memory[...], grad_value))
    ):
        put_block(made_cross, b, dot_tn(left, right))
        copies.deliver(me_ref, made_cross, cross, sent[4:], b)
    loads_cross[0].arrive()
    grad_memory[...] = dot_nt(grad_key, column_block(held_cross, 1)) + dot_nt(
        grad_value, column_block(held_cross, 2)
    )
    copies.store(grad_memory, sent[2])
    grad_normed = dot_nt(back[...], column_block(held_cross, 0))
    unit, inverse = normed_of(hidden_one[...])
    grad = norm_back(unit, inverse, gains[6:7], grad_normed, norm_cross)
    grad_one[...] = grad_two[...] + grad
    copies.store(grad_one, sent[3])
    copies.finish()


ANY = pl.BlockSpec(memory_space=pl.ANY)
HB = pl.BlockSpec(memory_space=pltpu.HBM)
VM = pl.BlockSpec(memory_space=pltpu.VMEM)
SM = pl.BlockSpec(memory_space=pltpu.SMEM)


def held_of(blocks):
    return pltpu.VMEM((4, 4, blocks * BLOCK, D), BF)


def made_of(layout, blocks):
    if layout.made == 1:
        return [jax.ShapeDtypeStruct((4, 4, layout.made_rows, D), BF)]
    return [jax.ShapeDtypeStruct((2, 2, 4, 2, blocks * BLOCK // 4, D), BF)] * 2


def shape(rows, cols, dtype):
    return jax.ShapeDtypeStruct((rows, cols), dtype)


class Order:
    def __init__(self):
        self.token = jnp.zeros((8, 128), F32)

    def tie(self, value):
        return self.tie_all([value])[0]

    def tie_all(self, values):
        arrays = list(values) + [self.token]
        *values, self.token = pl.pallas_call(
            nothing_kernel,
            name="tie",
            out_shape=[jax.ShapeDtypeStruct(x.shape, x.dtype) for x in arrays],
            in_specs=[HB] * len(arrays),
            out_specs=[HB] * len(arrays),
            input_output_aliases={k: k for k in range(len(arrays))},
            compiler_params=pltpu.CompilerParams(vmem_limit_bytes=VMEM_LIMIT),
        )(*arrays)
        return values


def nothing_kernel(*refs):
    pass


def call(order, body, name, in_specs, out_shape, out_specs, scratch, operands, micros, grid=None, inplace=()):
    count, more, outs = len(operands), len(inplace) + 1, len(out_shape)

    def ordered(*refs):
        body(*refs[:count], *refs[count + more : count + more + outs], *refs[count + more + outs + 1 :])

    aliases = {count + k: out for k, (unused, out) in enumerate(inplace)}
    aliases[count + len(inplace)] = outs
    *results, order.token = pl.pallas_call(
        ordered,
        name=name,
        out_shape=out_shape + [jax.ShapeDtypeStruct(order.token.shape, order.token.dtype)],
        in_specs=in_specs + [HB] * more,
        out_specs=out_specs + [HB],
        input_output_aliases=aliases,
        scratch_shapes=scratch,
        compiler_params=pltpu.CompilerParams(vmem_limit_bytes=VMEM_LIMIT),
        cost_estimate=pl.CostEstimate(
            flops=int((micros + 0.01) * COST), bytes_accessed=0, transcendentals=0
        ),
        **({} if grid is None else {"grid": grid}),
    )(*operands, *(array for array, unused in inplace), order.token)
    return results


def vmem(rows, cols, dtype):
    return pltpu.VMEM((rows, cols), dtype)


def probs_of(count, scratch=False):
    dims = (count * HEADS, TOK, TOK)
    return pltpu.VMEM(dims, BF) if scratch else jax.ShapeDtypeStruct(dims, BF)


SEMS = pltpu.SemaphoreType.DMA((64,))


def arrays(items):
    return [jax.ShapeDtypeStruct(dims, dtype) for dims, dtype in items]


def buffers(items):
    return [pltpu.VMEM(dims, dtype) for dims, dtype in items]


def self_kept(count):
    rows = count * TOK
    return [
        ((rows, D), F32),
        ((rows, D), BF),
        ((rows, 3 * D), BF),
        ((count * HEADS, TOK, TOK), BF),
        ((rows, D), BF),
    ]


def self_forward(order, me, src_lengths, tgt_lengths, gains, inputs, decoder, encoder):
    kept = self_kept(2) + self_kept(1)
    results = call(
        order,
        functools.partial(self_forward_kernel, decoder[0], encoder[0]),
        "self_forward",
        [SM, SM, SM, VM] + [HB] * 3 + [ANY] * (decoder[0].pieces + encoder[0].pieces),
        arrays(kept),
        [HB] * 10,
        buffers(kept) + [held_of(4), held_of(4)] + [vmem(TOK, D, BF)] * 3 + [SEMS],
        (me, src_lengths, tgt_lengths, gains, *inputs, *decoder[1], *encoder[1]),
        12,
    )
    return results[:5], results[5:]


def second(order, me, src_lengths, tgt_lengths, gains, hidden_enc, hidden_one, encoder, cross):
    rows = 2 * TOK
    kept = [
        ((TOK, D), BF),
        ((TOK, FF), BF),
        ((TOK, FF), BF),
        ((TOK, D), BF),
        ((rows, D), BF),
        ((rows, D), BF),
        ((TOK, 2 * D), BF),
        ((2 * HEADS, TOK, TOK), BF),
        ((rows, D), BF),
        ((rows, D), F32),
    ]
    results = call(
        order,
        functools.partial(second_kernel, encoder[0], cross[0]),
        "second",
        [SM, SM, SM, VM] + [HB] * 2 + [ANY] * 2,
        arrays(kept),
        [HB] * 10,
        buffers(kept) + [held_of(8), held_of(4), vmem(TOK, D, F32), vmem(rows, D, F32), SEMS],
        (me, src_lengths, tgt_lengths, gains, hidden_enc, hidden_one, encoder[1][0], cross[1][0]),
        13,
    )
    return results[:3], results[3:]


def self_back(order, row, me, gains, inputs, grad_out, kept, pieces):
    count = len(inputs)
    rows = count * TOK
    return call(
        order,
        functools.partial(self_back_kernel, count, row, pieces[0]),
        "self_back",
        [SM, VM] + [HB] * count + [HB] * 5 + [ANY] * pieces[0].pieces,
        [shape(TOK, D, F32), shape(2, D, F32)] + made_of(pieces[0], 4),
        [HB, VM] + [HB] * pieces[0].made,
        [
            vmem(TOK, D, F32),
            held_of(4),
            held_of(4),
            vmem(rows, 3 * D, BF),
            vmem(rows, D, F32),
            vmem(rows, D, BF),
            vmem(rows, 3 * D, BF),
            probs_of(count, True),
            vmem(rows, D, BF),
        ]
        + [vmem(TOK, D, BF)] * count
        + [SEMS],
        (me, gains, *inputs, grad_out, *kept, *pieces[1]),
        5.8 + 3.4 * count,
    )


def ffn_back(order, row, me, gains, hidden, grad_out, kept, pieces):
    return call(
        order,
        functools.partial(ffn_back_kernel, row, pieces[0]),
        "ffn_back",
        [SM, VM] + [HB] * 5 + [ANY] * pieces[0].pieces,
        [shape(TOK, D, F32), shape(2, D, F32)] + made_of(pieces[0], 8),
        [HB, VM] + [HB] * pieces[0].made,
        [
            vmem(TOK, D, F32),
            held_of(8),
            held_of(8),
            vmem(TOK, D, F32),
            vmem(TOK, D, F32),
            vmem(TOK, D, BF),
            vmem(TOK, FF, BF),
            vmem(TOK, FF, BF),
            SEMS,
        ],
        (me, gains, hidden, grad_out, *kept, *pieces[1]),
        10.2,
    )


def middle(order, me, gains, hidden_one, kept, cots, cross, decoder):
    rows = 2 * TOK
    memory, normed, query, pair, probs, mixed, hidden = kept
    taken = [hidden, *cots, mixed, probs, query, pair, normed, memory, hidden_one]
    sent = [((TOK, D), BF), ((TOK, D), BF), ((TOK, D), F32), ((rows, D), F32)]
    return call(
        order,
        functools.partial(middle_kernel, cross[0], decoder[0]),
        "middle",
        [SM, VM] + [HB] * 10 + [ANY] * (1 + decoder[0].pieces),
        [shape(2, D, F32)] * 2 + arrays(sent + [((4, 4, 384, D), BF)]),
        [VM] * 2 + [HB] * 5,
        buffers([(x.shape, x.dtype) for x in taken])
        + [held_of(4), held_of(8), held_of(4), held_of(8)]
        + buffers(sent)
        + [
            vmem(rows, D, BF),
            vmem(rows, FF, BF),
            vmem(rows, FF, BF),
            vmem(rows, D, F32),
            vmem(rows, D, BF),
            SEMS,
        ],
        (me, gains, *taken, cross[1][0], *decoder[1]),
        25,
    )


AXIS = "fsdp"
BOTH = ("dp", "fsdp")
SHARDS = 16


def route(target):
    pairs = []
    for i in range(2 * SHARDS):
        dp, z, y, core = target(i // 16, (i // 4) % 4, (i // 2) % 2, i % 2)
        pairs.append((i, dp * 16 + (z % 4) * 4 + y * 2 + core))
    return pairs


def to_core(x):
    return lax.ppermute(x, BOTH, route(lambda dp, z, y, core: (dp, z, y, 1 - core)))


def to_z(x, step):
    return lax.ppermute(x, BOTH, route(lambda dp, z, y, core: (dp, z + step, y, core)))


def to_z_pair(x, step):
    return lax.ppermute(x, BOTH, route(lambda dp, z, y, core: (dp, z ^ step, y, core)))


def to_y(x):
    return lax.ppermute(x, BOTH, route(lambda dp, z, y, core: (dp, z, 1 - y, core)))


def to_dp(x):
    return lax.ppermute(x, BOTH, route(lambda dp, z, y, core: (1 - dp, z, y, core)))


def to_yx(x):
    return lax.ppermute(
        x, BOTH, route(lambda dp, z, y, core: (dp, z, y ^ 1, core) if core == 0 else (dp ^ 1, z, y, core))
    )


def to_xy(x):
    return lax.ppermute(
        x, BOTH, route(lambda dp, z, y, core: (dp ^ 1, z, y, core) if core == 0 else (dp, z, y ^ 1, core))
    )


def blocks_of(shard):
    rows, cols = shard.shape
    split = shard.reshape(rows // BLOCK, BLOCK, cols // D, D)
    return split.transpose(2, 0, 1, 3).reshape(-1, BLOCK, D)


def shard_of(blocks, cols):
    wide = blocks.reshape(cols // D, -1, D)
    return wide.transpose(1, 0, 2).reshape(-1, cols)


def small(order, body, name, out, operands, scratch=(), in_specs=None, out_specs=None, micros=0, grid=None):
    return call(
        order,
        body,
        name,
        in_specs if in_specs is not None else [VM] * len(operands),
        [jax.ShapeDtypeStruct(dims, dtype) for dims, dtype in out],
        out_specs if out_specs is not None else [VM] * len(out),
        list(scratch),
        operands,
        micros,
        grid,
    )


def pack_kernel(place, *refs):
    weights, (one, two, three, norms) = refs[:15], refs[15:]
    self_in, self_out, enc_in, enc_out, enc_ffn_in, enc_ffn_out = weights[:6]
    cross_q, cross_kv, cross_out, ffn_in, ffn_out = weights[6:11]
    for half in range(2):

        @pl.when(place[2] == half)
        def _():
            for k in range(2):
                quarter = 2 * half + k
                cols = slice(quarter * D, (quarter + 1) * D)
                one[k, 0:32] = self_out[...] if quarter == 3 else self_in[:, cols]
                one[k, 32:64] = enc_out[...] if quarter == 3 else enc_in[:, cols]
                for j in range(2):
                    block = 2 * quarter + j
                    rows = slice(j * BLOCK, (j + 1) * BLOCK)
                    cols = slice(block * D, (block + 1) * D)
                    part = slice((block - 4) * BLOCK, (block - 3) * BLOCK)
                    three[k, rows] = ffn_in[:, cols] if block < 4 else ffn_out[part]

    for block in range(4):
        rows = slice(block * BLOCK, (block + 1) * BLOCK)
        two[rows] = enc_ffn_in[:, block * D : (block + 1) * D]
    two[128:256] = enc_ffn_out[...]
    two[256:288] = cross_q[...]
    two[288:320] = cross_kv[:, 0:D]
    two[320:352] = cross_kv[:, D : 2 * D]
    two[352:384] = cross_out[...]
    norms[...] = jnp.zeros(norms.shape, F32)
    row = 0
    for gain, bias in (weights[11:13], weights[13:15]):
        for k in range(gain.shape[0]):
            norms[row : row + 1, 0:BLOCK] = gain[k : k + 1].astype(F32)
            norms[row + 1 : row + 2, 0:BLOCK] = bias[k : k + 1].astype(F32)
            row += 2
    for k in range(2):
        one[k, 64:80] = norms[...].astype(BF)


def pack(order, place, weights, norms):
    return small(
        order,
        pack_kernel,
        "pack",
        [((2, 80, D), BF), ((384, D), BF), ((2, 64, D), BF)],
        (place, *weights, *norms),
        [pltpu.VMEM((16, D), F32)],
        in_specs=[SM] + [VM] * 15,
    )


def pair_kernel(place, *refs):
    core = place[3]
    for k in range(2):
        mine, near, pair = refs[2 * k], refs[2 * k + 1], refs[4 + k]
        pair[core] = mine[core]
        pair[1 - core] = near[core]


def pair_up(order, place, mine, near):
    operands = [x for both in zip(mine, near) for x in both]
    return small(
        order,
        pair_kernel,
        "pair_up",
        [(x.shape, x.dtype) for x in mine],
        (place, *operands),
        in_specs=[SM] + [VM] * 4,
    )


def stack_kernel(place, *refs):
    parts, (out, held, sems) = refs[:-3], refs[-3:]
    count = len(parts)
    loads = [pltpu.make_async_copy(parts[d], held.at[d], sems.at[d]) for d in range(count)]
    stores = [
        pltpu.make_async_copy(held.at[d], out.at[(place[0] + (4 - d)) & 3], sems.at[count + d])
        for d in range(count)
    ]
    for copy in loads:
        copy.start()
    for d in range(count):
        loads[d].wait()
        stores[d].start()
    wait_all(stores)


def stack(order, place, parts):
    dims = (len(parts),) + parts[0].shape
    dtype = parts[0].dtype
    return small(
        order,
        stack_kernel,
        "stack",
        [(dims, dtype)],
        (place, *parts),
        [pltpu.VMEM(dims, dtype), pltpu.SemaphoreType.DMA((2 * len(parts),))],
        [SM] + [ANY] * len(parts),
        [ANY],
    )[0]


def table_kernel(place, own, across, down, gains, held, sems):
    copies = []
    for k, piece in enumerate((own, across, down)):
        copies.append(pltpu.make_async_copy(piece.at[:, :, pl.ds(64, 16)], held.at[k], sems.at[k]))
    for copy in copies:
        copy.start()
    wait_all(copies)
    far = jnp.where(place[3] == 0, 2, 1)
    for y in range(2):
        where = jnp.where(place[1] == y, 0, far)
        for z in range(4):
            for core in range(2):
                spot = 4 * z + 2 * y + core
                row = held[where, z, core]
                gains[:, spot * BLOCK : (spot + 1) * BLOCK] = row[:, 0:BLOCK].astype(F32)


def norm_table(order, place, pieces):
    return small(
        order,
        table_kernel,
        "norm_table",
        [((16, D), F32)],
        (place, pieces[0], pieces[1], pieces[2]),
        [pltpu.VMEM((3, 4, 2, 16, D), BF), pltpu.SemaphoreType.DMA((3,))],
        [SM, ANY, ANY, ANY],
    )[0]


class Gather:
    def __init__(self, order, pair):
        self.order, self.pair = order, pair

    def along_z(self):
        pair = self.order.tie(self.pair)
        self.parts = [pair] + [to_z(pair, d) for d in (1, 2, 3)]

    def lined(self, place):
        self.line = stack(self.order, place, self.parts)

    def first_cross(self):
        line = self.order.tie(self.line)
        self.own = [line, to_xy(line), to_yx(line)]
        self.near = []

    def crossed(self, others=()):
        arrived = self.order.tie_all(self.own[1:3] + list(others[1:]))
        self.own[1:3] = arrived[:2]
        if others:
            others[1:] = arrived[2:]

    def second_cross(self):
        self.own.append(to_yx(self.own[1]))

    def share(self, k):
        self.near.append(self.order.tie(to_core(self.own[k])))

    def done(self):
        last = self.order.tie(self.own[3])
        self.own = self.own[:3] + [last]
        self.near.append(self.order.tie(to_core(last)))
        self.pieces = tuple(self.own + self.near)


def low_sum(*parts):
    total = parts[0].astype(F32)
    for part in parts[1:]:
        total = total + part.astype(F32)
    return total.astype(BF)


def rows_of(parts):
    row = 0
    for k, part in enumerate(parts[::2]):
        yield slice(row, row + part.shape[4]), part, parts[2 * k + 1]
        row += part.shape[4]


def reduce_first_kernel(norm_own, norm_came, *refs):
    sent, norm = refs[-2:]
    norm[...] = norm_own[...] + norm_came[...]
    for rows, own, came in rows_of(refs[:-2]):
        sent[:, :, :, rows] = own[0] + came[0]


def reduce_second_kernel(norm_own, norm_came, came_first, *refs):
    sent, norm = refs[-2:]
    norm[...] = norm_own[...] + norm_came[...]
    for rows, own, came in rows_of(refs[:-2]):
        sent[:, :, rows] = low_sum(own[0, 0], came[0, 0], came_first[0, :, :, rows])


def reduce_third_kernel(norm_own, norm_came, place, came_first, came_second, *refs):
    outs, norm = refs[-5:-1], refs[-1]
    norm[...] = norm_own[...] + norm_came[...]
    for rows, own, came in rows_of(refs[:-5]):
        for d in range(4):
            z = (place[0] + d) & 3
            outs[d][:, rows] = low_sum(
                own[0, 0, z], came[0, 0, z], came_first[0, z, :, rows], came_second[z, :, rows]
            )


def reduce_fourth_kernel(norm_own, norm_came, a, b, c, d, out, norm):
    norm[...] = norm_own[...] + norm_came[...]
    out[...] = low_sum(a[...], b[...], c[...], d[...])


NORM_SPEC = pl.BlockSpec((16, D), lambda i: (0, 0))


class Reduce:
    def __init__(self, order):
        self.order, self.own, self.came = order, [], []

    def add(self, own, other):
        self.own.append(own)
        self.came.append(to_core(self.order.tie(other)))

    def arrive(self):
        self.came[-1] = self.order.tie(self.came[-1])

    def start_norm(self, norm):
        self.norm = self.order.tie(norm)
        self.norm_came = to_core(self.norm)

    def run(self, body, name, out, extra, in_specs, out_specs, grid):
        parts = [x for both in zip(self.own, self.came) for x in both]
        specs = [
            pl.BlockSpec(in_specs[-1][0] + (part.shape[4], D), in_specs[-1][1]) for part in parts
        ]
        *sent, norm = small(
            self.order,
            body,
            name,
            out + [((16, D), F32)],
            [self.norm, self.norm_came] + extra + parts,
            in_specs=[NORM_SPEC] * 2 + in_specs[:-1] + specs,
            out_specs=out_specs + [NORM_SPEC],
            grid=grid,
        )
        return [self.order.tie(x) for x in sent], self.order.tie(norm)

    def first(self):
        rows = self.rows = sum(own.shape[4] for own in self.own)
        (sent,), self.norm = self.run(
            reduce_first_kernel,
            "reduce_first",
            [((2, 4, 2, rows, D), BF)],
            [],
            [((1, 2, 1, 2), lambda i: (1, 0, i, 0, 0, 0))],
            [pl.BlockSpec((2, 1, 2, rows, D), lambda i: (0, i, 0, 0, 0))],
            (4,),
        )
        self.first_came = to_yx(sent)
        self.norm_came = to_y(self.norm)

    def second(self):
        rows = self.rows
        (sent,), self.norm = self.run(
            reduce_second_kernel,
            "reduce_second",
            [((4, 2, rows, D), BF)],
            [self.first_came],
            [
                pl.BlockSpec((1, 1, 2, rows, D), lambda i: (1, i, 0, 0, 0)),
                ((1, 1, 1, 2), lambda i: (0, 1, i, 0, 0, 0)),
            ],
            [pl.BlockSpec((1, 2, rows, D), lambda i: (i, 0, 0, 0))],
            (4,),
        )
        self.second_came = to_xy(sent)
        self.norm_came = to_z_pair(self.norm, 1)

    def third(self, place):
        rows = self.rows
        parts, self.norm = self.run(
            reduce_third_kernel,
            "reduce_third",
            [((2, rows, D), BF)] * 4,
            [place, self.first_came, self.second_came],
            [
                SM,
                pl.BlockSpec((1, 4, 2, rows, D), lambda i: (0, 0, 0, 0, 0)),
                pl.BlockSpec((4, 2, rows, D), lambda i: (0, 0, 0, 0)),
                ((1, 1, 4, 2), lambda i: (0, 0, 0, 0, 0, 0)),
            ],
            [pl.BlockSpec((2, rows, D), lambda i: (0, 0, 0))] * 4,
            (1,),
        )
        self.lines = [parts[0]] + [to_z(parts[d], d) for d in (1, 2, 3)]
        self.norm_came = to_z_pair(self.norm, 2)

    def fourth(self):
        total, norm = small(
            self.order,
            reduce_fourth_kernel,
            "reduce_fourth",
            [(self.lines[0].shape, BF), ((16, D), F32)],
            [self.norm, self.norm_came] + self.lines,
        )
        total, self.norm = self.order.tie(total), self.order.tie(norm)
        self.ends = [total, to_dp(total), to_core(total)]
        self.norm_came = to_dp(self.norm)

    def last(self):
        near = self.order.tie(self.ends[2])
        came = self.order.tie(self.ends[1])
        self.ends = [self.ends[0], came, near, to_core(came)]


def quarter_of(place, ends, quarter, rows):
    core = place[3]
    half, which = quarter >> 1, quarter & 1
    first = jnp.where(place[3] == which, ends[0][core, rows], ends[2][core, rows].astype(BF))
    second = jnp.where(place[3] == which, ends[1][core, rows], ends[3][core, rows])
    return jnp.where(place[2] == half, first, second).astype(F32)


def unpack_kernel(layout, place, *refs):
    ends, outs = refs[:4], refs[4:]
    first = 0
    for kind, row in layout:
        for quarter in range(4):
            if kind == "ffn":
                for j in range(2):
                    block = 2 * quarter + j
                    rows = slice(row + j * BLOCK, row + (j + 1) * BLOCK)
                    value = quarter_of(place, ends, quarter, rows)
                    if block < 4:
                        outs[first][:, block * D : (block + 1) * D] = value
                    else:
                        outs[first + 1][(block - 4) * BLOCK : (block - 3) * BLOCK] = value
            else:
                value = quarter_of(place, ends, quarter, slice(row, row + BLOCK))
                if kind == "attn":
                    if quarter < 3:
                        outs[first][:, quarter * D : (quarter + 1) * D] = value
                    else:
                        outs[first + 1][...] = value
                elif quarter in (1, 2):
                    outs[first + 1][:, (quarter - 1) * D : quarter * D] = value
                else:
                    outs[first + (quarter + 1) // 2][...] = value
        first += 3 if kind == "cross" else 2


SHARD_SHAPES = {
    "ffn": [((BLOCK, FF), F32), ((4 * BLOCK, D), F32)],
    "attn": [((BLOCK, 3 * D), F32), ((BLOCK, D), F32)],
    "cross": [((BLOCK, D), F32), ((BLOCK, 2 * D), F32), ((BLOCK, D), F32)],
}


def unpack(order, place, ends, layout):
    return small(
        order,
        functools.partial(unpack_kernel, layout),
        "unpack",
        [item for kind, unused in layout for item in SHARD_SHAPES[kind]],
        (place, *ends),
        in_specs=[SM] + [VM] * 4,
    )


def norm_join_kernel(*refs):
    parts, out = refs[:5], refs[5]
    out[...] = jnp.zeros(out.shape, F32)
    for k in range(5):
        out[2 * k : 2 * k + 2] = parts[k][...]


def norm_last_kernel(place, own, came, *outs):
    total = own[...] + came[...]
    spot = place[0] * 4 + place[1] * 2 + place[3]
    turned = jnp.zeros((16, BLOCK), F32)
    for k in range(SHARDS):
        turned = jnp.where(spot == k, total[:, k * BLOCK : (k + 1) * BLOCK], turned)
    for first, gain, bias in ((0, outs[0], outs[1]), (4, outs[2], outs[3])):
        for k in range(gain.shape[0]):
            gain[k : k + 1] = turned[first + 2 * k : first + 2 * k + 1]
            bias[k : k + 1] = turned[first + 2 * k + 1 : first + 2 * k + 2]


def norm_last(order, place, own, came):
    return small(
        order,
        norm_last_kernel,
        "norm_last",
        [((2, BLOCK), F32), ((2, BLOCK), F32), ((3, BLOCK), F32), ((3, BLOCK), F32)],
        (place, own, came),
        in_specs=[SM, VM, VM],
    )


def spread_kernel(own, came, ffn_in, ffn_out, cross_q, cross_kv, cross_out):
    total = own[...].astype(F32) + came[...].astype(F32)
    for block in range(4):
        ffn_in[:, block * D : (block + 1) * D] = total[block * BLOCK : (block + 1) * BLOCK]
    ffn_out[...] = total[128:256]
    cross_q[...] = total[256:288]
    cross_kv[:, 0:D] = total[288:320]
    cross_kv[:, D : 2 * D] = total[320:352]
    cross_out[...] = total[352:384]


def spread(order, own, came):
    return small(
        order,
        spread_kernel,
        "spread",
        SHARD_SHAPES["ffn"] + SHARD_SHAPES["cross"],
        (own, came),
    )


def gather_plain(weights):
    parts = []
    for weight in weights:
        whole = lax.all_gather(weight, AXIS, axis=0, tiled=True)
        parts.append(jax.vmap(blocks_of)(whole.reshape(SHARDS, -1, whole.shape[1])))
    return jnp.concatenate(parts, axis=1).reshape(4, 4, -1, D)


def reduce_plain(made, columns):
    shards = made.reshape(SHARDS, -1, BLOCK, D)
    grads = []
    for first, last, cols in columns:
        whole = jax.vmap(functools.partial(shard_of, cols=cols))(shards[:, first:last])
        whole = whole.reshape(-1, cols).astype(F32)
        part = lax.psum_scatter(whole, AXIS, scatter_dimension=0, tiled=True)
        grads.append(lax.psum(part.astype(BF), "dp").astype(F32))
    return grads


def norm_rows_of(gain_enc, bias_enc, gain_dec, bias_dec):
    rows = []
    for gain, bias in ((gain_enc, bias_enc), (gain_dec, bias_dec)):
        for k in range(gain.shape[0]):
            rows += [gain[k : k + 1], bias[k : k + 1]]
    return jnp.concatenate(rows, axis=0)


ATTN_COLUMNS = ((0, 3, 3 * D), (3, 4, D))
FFN_COLUMNS = ((0, 4, FF), (4, 8, D))
CROSS_COLUMNS = ((0, 1, D), (1, 3, 2 * D), (3, 4, D))


def step(
    custom,
    source,
    first_in,
    second_in,
    cot_first,
    cot_second,
    src_lengths,
    tgt_lengths,
    enc_attn_in,
    enc_attn_out,
    enc_ffn_in,
    enc_ffn_out,
    enc_gain,
    enc_bias,
    dec_self_in,
    dec_self_out,
    dec_cross_q,
    dec_cross_kv,
    dec_cross_out,
    dec_ffn_in,
    dec_ffn_out,
    dec_gain,
    dec_bias,
):
    spot = lax.axis_index(AXIS)
    order = Order()
    group_self = (dec_self_in, dec_self_out)
    group_enc = (enc_attn_in, enc_attn_out)
    group_enc_ffn = (enc_ffn_in, enc_ffn_out)
    group_cross = (dec_cross_q, dec_cross_kv, dec_cross_out)
    group_ffn = (dec_ffn_in, dec_ffn_out)
    if custom:
        place = jnp.stack([spot >> 2, (spot >> 1) & 1, lax.axis_index("dp"), spot & 1]).astype(jnp.int32)
        weights = group_self + group_enc + group_enc_ffn + group_cross + group_ffn
        mine_one, mine_two, mine_three = pack(
            order, place, weights, (enc_gain, enc_bias, dec_gain, dec_bias)
        )
        mine = (mine_one, mine_three)
        pairs = pair_up(order, place, mine, [to_core(x) for x in mine])
        one, three = (Gather(order, pair) for pair in pairs)
        one.along_z()
        one.lined(place)
        mine_two = order.tie(mine_two)
        whole = lax.all_gather(mine_two, AXIS, axis=0, tiled=True).reshape(4, 4, -1, D)
        one.first_cross()
        three.along_z()
        one.crossed(three.parts)
        one.second_cross()
        for k in range(3):
            one.share(k)
        one.done()
        gains = norm_table(order, place, one.pieces)
        three.lined(place)
        three.first_cross()
        w_self, w_enc = (Layout(0, 8), one.pieces), (Layout(32, 8), one.pieces)
        w_enc_ffn = (Layout(0, 1), (whole,))
        w_cross = (Layout(256, 1, 1, 256, 384), (whole,))
    else:
        place = jnp.zeros((4,), jnp.int32)
        w_self, w_enc, w_enc_ffn = (
            (Layout(0, 1, 1, 0, rows), (gather_plain(group),))
            for group, rows in ((group_self, 128), (group_enc, 128), (group_enc_ffn, 256))
        )
        w_cross = (Layout(0, 1, 1, 256, 384), (gather_plain(group_cross),))
        w_ffn = (Layout(0, 1, 1, 0, 384), (gather_plain(group_ffn),))
        norm_rows = norm_rows_of(enc_gain, enc_bias, dec_gain, dec_bias)
        gains = lax.all_gather(norm_rows, AXIS, axis=1, tiled=True)
        gains = jnp.pad(gains.astype(F32), ((0, 6), (0, 0)))

    (hidden_one, *kept_self), (hidden_enc, *kept_enc) = self_forward(
        order, place, src_lengths, tgt_lengths, gains, [first_in, second_in, source], w_self, w_enc
    )
    if custom:
        three.crossed()
        three.second_cross()
        for k in range(3):
            three.share(k)
    kept_enc_ffn, kept_cross = second(
        order, place, src_lengths, tgt_lengths, gains, hidden_enc, hidden_one, w_enc_ffn, w_cross
    )
    if custom:
        three.done()
        w_ffn = (Layout(0, 8, 1, 0, 384), three.pieces)
    norm_ffn, norm_cross, first_out, second_out, grad_memory, grad_one, made = middle(
        order, place, gains, hidden_one, kept_cross, (cot_first, cot_second), w_cross, w_ffn
    )
    if custom:
        scattered = lax.psum_scatter(
            made.reshape(-1, D), AXIS, scatter_dimension=0, tiled=True
        )
    grad_enc, norm_enc_ffn, *made_enc_ffn = ffn_back(
        order, 2, place, gains, hidden_enc, grad_memory, kept_enc_ffn, w_enc_ffn
    )
    if custom:
        red = Reduce(order)
        red.add(*made_enc_ffn)
    grad_first, norm_self, *made_self = self_back(
        order, 4, place, gains, [first_in, second_in], grad_one, kept_self, w_self
    )
    if custom:
        red.arrive()
        red.add(*made_self)
    grad_source, norm_enc, *made_enc = self_back(
        order, 0, place, gains, [source], grad_enc, kept_enc, w_enc
    )
    if custom:
        red.arrive()
        red.add(*made_enc)
        (norm_total,) = small(
            order,
            norm_join_kernel,
            "norm_join",
            [((16, D), F32)],
            (norm_enc, norm_enc_ffn, norm_self, norm_cross, norm_ffn),
        )
        red.start_norm(norm_total)
        red.first()
        red.second()
        red.third(place)
        scattered = order.tie(scattered)
        scattered_came = order.tie(to_dp(scattered))
        red.fourth()
        grads_ffn_cross = spread(order, scattered, scattered_came)
        red.last()
        norm_grads = norm_last(order, place, red.norm, red.norm_came)
        grads_ffn, grads_cross = grads_ffn_cross[:2], grads_ffn_cross[2:]
        g = unpack(order, place, red.ends, (("ffn", 0), ("attn", 64), ("attn", 96)))
        grads_enc_ffn, grads_self, grads_enc = g[:2], g[2:4], g[4:6]
    else:
        norm_grads = jnp.concatenate(
            [norm_enc, norm_enc_ffn, norm_self, norm_cross, norm_ffn], axis=0
        )
        grads_ffn = reduce_plain(made[:, :, 0:256], FFN_COLUMNS)
        grads_cross = reduce_plain(made[:, :, 256:384], CROSS_COLUMNS)
        grads_enc_ffn = reduce_plain(*made_enc_ffn, FFN_COLUMNS)
        grads_self = reduce_plain(*made_self, ATTN_COLUMNS)
        grads_enc = reduce_plain(*made_enc, ATTN_COLUMNS)
        norm_shard = lax.psum_scatter(norm_grads, AXIS, scatter_dimension=1, tiled=True)
        norm_shard = lax.psum(norm_shard.astype(BF), "dp").astype(F32)
        norm_grads = (norm_shard[0:4:2], norm_shard[1:4:2], norm_shard[4:10:2], norm_shard[5:10:2])
    return (
        first_out,
        second_out,
        grad_source,
        grad_first,
        *grads_enc,
        *grads_enc_ffn,
        *norm_grads[:2],
        *grads_self,
        *grads_cross,
        *grads_ffn,
        *norm_grads[2:],
    )


def solution(mesh):
    blocked = P(("dp", "fsdp"), None)
    rows = P("fsdp", None)
    columns = P(None, "fsdp")
    custom = mesh.shape["fsdp"] == SHARDS and mesh.shape["dp"] == 2
    return jax.shard_map(
        functools.partial(step, custom),
        mesh=mesh,
        in_specs=(blocked,) * 7 + (rows,) * 4 + (columns,) * 2 + (rows,) * 7 + (columns,) * 2,
        out_specs=(blocked,) * 4 + (rows,) * 4 + (columns,) * 2 + (rows,) * 7 + (columns,) * 2,
        check_vma=False,
    )
```

```python
import functools
import typing

import jax
import jax.numpy as jnp
from jax import lax
from jax.experimental import pallas as pl
from jax.experimental.pallas import tpu as pltpu
from jax.sharding import PartitionSpec as P

D = 512
HEADS = 8
HEAD = 64
TOK = 256
FF = 2048
QUAD = 256
BLOCK = 32
EPSILON = 1e-05
MASKED = -1000000000.0
BF = jnp.bfloat16
F32 = jnp.float32
VMEM_LIMIT = 64 * 1024 * 1024
COST = 1.1e9


class Layout(typing.NamedTuple):
    offset: int
    pieces: int
    made: int = 2
    made_offset: int = 0
    made_rows: int = 0


def dot(left, right):
    return lax.dot_general(left, right, (((1,), (0,)), ((), ())), preferred_element_type=F32)


def dot_nt(left, right):
    return lax.dot_general(left, right, (((1,), (1,)), ((), ())), preferred_element_type=F32)


def dot_tn(left, right):
    return lax.dot_general(left, right, (((0,), (0,)), ((), ())), preferred_element_type=F32)


def wait_all(copies):
    for copy in copies:
        copy.wait()


def column_block(held, index):
    return held[:, :, index * BLOCK : (index + 1) * BLOCK].reshape(D, D)


def row_block(held, index):
    return held[index, :, 4 * BLOCK : 8 * BLOCK].reshape(D, D)


def normed_of(values):
    centre = values - jnp.mean(values, axis=-1, keepdims=True)
    spread = jnp.mean(centre * centre, axis=-1, keepdims=True)
    inverse = lax.rsqrt(spread + EPSILON)
    return centre * inverse, inverse


def norm_back(unit, inverse, gain, grad_normed, norm_ref):
    norm_ref[0:1] = jnp.sum(grad_normed * unit, axis=0, keepdims=True)
    norm_ref[1:2] = jnp.sum(grad_normed, axis=0, keepdims=True)
    grad_unit = grad_normed * gain
    return (
        grad_unit
        - jnp.mean(grad_unit, axis=-1, keepdims=True)
        - unit * jnp.mean(grad_unit * unit, axis=-1, keepdims=True)
    ) * inverse


def mask_bias(key_lengths, query_lengths):
    key_place = lax.broadcasted_iota(jnp.int32, (TOK, 1), 0)
    query_place = lax.broadcasted_iota(jnp.int32, (1, TOK), 1)
    key_ids = jnp.zeros((TOK, 1), jnp.int32)
    query_ids = jnp.zeros((1, TOK), jnp.int32)
    key_end = jnp.int32(0)
    query_end = jnp.int32(0)
    for k in range(key_lengths.shape[1]):
        key_end = key_end + key_lengths[0, k]
        query_end = query_end + query_lengths[0, k]
        key_ids = key_ids + jnp.where(key_place >= key_end, 1, 0)
        query_ids = query_ids + jnp.where(query_place >= query_end, 1, 0)
    return jnp.where(key_ids == query_ids, 0.0, MASKED).astype(F32)


def lane_masks():
    head_of = lax.broadcasted_iota(jnp.int32, (1, QUAD), 1) // HEAD
    return [jnp.where(head_of == h, 1.0, 0.0).astype(BF) for h in range(QUAD // HEAD)]


def attend(queries, keys, values, bias, probs_ref, first):
    masks = lane_masks()
    outs = []
    for g in range(D // QUAD):
        cols = slice(g * QUAD, (g + 1) * QUAD)
        q, k, v = queries[:, cols], keys[:, cols], values[:, cols]
        total = None
        for h in range(QUAD // HEAD):
            scores = dot_nt(k * (masks[h] * (HEAD**-0.5)), q) + bias
            top = jnp.max(scores, axis=0, keepdims=True)
            grown = jnp.exp(scores - top)
            probs = (grown * (1.0 / jnp.sum(grown, axis=0, keepdims=True))).astype(BF)
            probs_ref[first + g * (QUAD // HEAD) + h] = probs
            part = dot_tn(probs, v * masks[h])
            total = part if total is None else total + part
        outs.append(total.astype(BF))
    return jnp.concatenate(outs, axis=1)


def attend_back(queries, keys, values, probs_ref, first, grad_mixed):
    masks = lane_masks()
    grads = []
    for g in range(D // QUAD):
        cols = slice(g * QUAD, (g + 1) * QUAD)
        q, k, v, go = queries[:, cols], keys[:, cols], values[:, cols], grad_mixed[:, cols]
        gq = gk = gv = None
        for h in range(QUAD // HEAD):
            probs_low = probs_ref[first + g * (QUAD // HEAD) + h]
            probs = probs_low.astype(F32)
            grad_probs = dot_nt(v * masks[h], go)
            both = probs * grad_probs
            grad_scores = (both - probs * jnp.sum(both, axis=0, keepdims=True)).astype(BF)
            part_v = dot(probs_low, go * masks[h])
            part_k = dot(grad_scores, q * masks[h])
            part_q = dot_tn(grad_scores, k * masks[h])
            gv = part_v if gv is None else gv + part_v
            gk = part_k if gk is None else gk + part_k
            gq = part_q if gq is None else gq + part_q
        grads.append((gq * (HEAD**-0.5), gk * (HEAD**-0.5), gv))
    return tuple(jnp.concatenate(parts, axis=1) for parts in zip(*grads))


def put_block(held, index, product):
    held[:, :, index * BLOCK : (index + 1) * BLOCK] = product.astype(BF).reshape(4, 4, BLOCK, D)


class Copies:
    def __init__(self, sems):
        self.sems, self.count, self.out = sems, 0, []

    def start(self, source, target):
        copy = pltpu.make_async_copy(source, target, self.sems.at[self.count])
        self.count += 1
        copy.start()
        return copy

    def load(self, source, target):
        return Loaded(target, [self.start(source, target)])

    def store(self, source, target):
        self.out.append(self.start(source, target))

    def finish(self):
        wait_all(self.out)

    def fetch(self, place, pieces, layout, held):
        rows = held.shape[2] // 4
        if layout.pieces == 1:
            loads = []
            for half in range(2):
                part = pieces[0].at[:, :, pl.ds(layout.offset + 2 * half * rows, 2 * rows)]
                loads.append(self.load(part, held.at[:, :, pl.ds(2 * half * rows, 2 * rows)]))
            return loads
        copies = []
        for turn in range(2):
            for first in range(2):
                for second in range(2):
                    y, half, which = place_of(place, turn, first, second)
                    quarter = pl.multiple_of((2 * half + which) * rows, rows)
                    piece = pieces[4 * turn + 2 * first + second]
                    copies.append(
                        self.start(
                            piece.at[:, :, pl.ds(layout.offset, rows)],
                            held.at[:, pl.ds(2 * y, 2), pl.ds(quarter, rows)],
                        )
                    )
        return [Loaded(held, copies)] * 2

    def deliver(self, place, held, layout, outs, *quarters):
        rows = held.shape[2] // 4
        if layout.made == 1:
            for quarter in (q for q in quarters if q < 4):
                part = pl.ds(layout.made_offset + quarter * rows, rows)
                self.store(held.at[:, :, pl.ds(quarter * rows, rows)], outs[0].at[:, :, part])
        elif 4 in quarters:
            for turn in range(2):
                for first in range(2):
                    for second in range(2):
                        y, half, which = place_of(place, turn, first, second)
                        quarter = pl.multiple_of((2 * half + which) * rows, rows)
                        self.store(
                            held.at[:, pl.ds(2 * y, 2), pl.ds(quarter, rows)],
                            outs[turn].at[first, second],
                        )


def place_of(place, turn, first, second):
    which = place[3] ^ turn
    y = place[1] ^ jnp.where(which == 0, first, second)
    half = place[2] ^ jnp.where(which == 0, second, first)
    return y, half, which


class Loaded:
    def __init__(self, target, copies):
        self.target, self.copies = target, copies

    def arrive(self):
        wait_all(self.copies)
        self.copies.clear()
        return self.target

    def __getitem__(self, index):
        return self.arrive()[index]


def self_forward_part(copies, row, gains, bias, inputs, loads, held, scratch, outs):
    out, normed, joined, probs, mixed = scratch
    out_ref, normed_ref, joined_ref, probs_ref, mixed_ref = outs
    passes = len(inputs)
    for p in range(passes):
        rows = slice(p * TOK, (p + 1) * TOK)
        unit, unused = normed_of(inputs[p][...].astype(F32))
        normed[rows] = (unit * gains[row : row + 1] + gains[row + 1 : row + 2]).astype(BF)
    copies.store(normed, normed_ref)
    for b in range(3):
        loads[b // 2].arrive()
        joined[:, b * D : (b + 1) * D] = dot(normed[...], column_block(held, b)).astype(BF)
    copies.store(joined, joined_ref)
    for p in range(passes):
        rows = slice(p * TOK, (p + 1) * TOK)
        mixed_part = attend(
            joined[rows, 0:D], joined[rows, D : 2 * D], joined[rows, 2 * D : 3 * D], bias, probs, p * HEADS
        )
        heads = pl.ds(p * HEADS, HEADS)
        copies.store(probs.at[heads], probs_ref.at[heads])
        mixed[rows] = mixed_part
        out[rows] = inputs[p][...].astype(F32) + dot(mixed_part, column_block(held, 3))
    copies.store(out, out_ref)
    copies.store(mixed, mixed_ref)


def self_forward_kernel(decoder, encoder, me_ref, src_lengths, tgt_lengths, gains, *refs):
    taken, refs = refs[:3], refs[3:]
    pieces, refs = refs[: decoder.pieces], refs[decoder.pieces :]
    more, refs = refs[: encoder.pieces], refs[encoder.pieces :]
    outs, scratch, (held, held_enc, *come, sems) = refs[:10], refs[10:20], refs[20:]
    copies = Copies(sems)
    inputs = [copies.load(taken[p], come[p]) for p in range(3)]
    loads = copies.fetch(me_ref, pieces, decoder, held)
    loads_enc = copies.fetch(me_ref, more, encoder, held_enc)
    bias = mask_bias(tgt_lengths, tgt_lengths)
    self_forward_part(copies, 4, gains, bias, inputs[:2], loads, held, scratch[:5], outs[:5])
    bias = mask_bias(src_lengths, src_lengths)
    self_forward_part(copies, 0, gains, bias, inputs[2:], loads_enc, held_enc, scratch[5:], outs[5:])
    copies.finish()


def self_back_kernel(passes, row, more, layout, me_ref, gains, *refs):
    others, refs = refs[:more], refs[more:]
    inputs, refs = refs[:passes], refs[passes:]
    taken, refs = refs[:5], refs[5:]
    pieces, refs = refs[: layout.pieces], refs[layout.pieces :]
    grad_in_ref, norm_ref, *refs = refs
    outs, refs = refs[: layout.made], refs[layout.made :]
    grad_in, held, made, back, grad_out, normed, joined, probs, mixed, *come, sems = refs
    copies = Copies(sems)
    grad_out = copies.load(taken[0], grad_out)
    mixed = copies.load(taken[4], mixed)
    loads = copies.fetch(me_ref, pieces, layout, held)
    probs = [
        copies.load(taken[3].at[pl.ds(p * HEADS, HEADS)], probs.at[pl.ds(p * HEADS, HEADS)])
        for p in range(passes)
    ]
    joined = copies.load(taken[2], joined)
    normed = copies.load(taken[1], normed)
    inputs = [copies.load(inputs[p], come[p]) for p in range(passes)]
    grad_low = grad_out[...].astype(BF)
    put_block(made, 3, dot_tn(mixed[...], grad_low))
    copies.deliver(me_ref, made, layout, outs, 3)
    loads[1].arrive()
    grad_mixed = dot_nt(grad_low, column_block(held, 3)).astype(BF)
    for p in range(passes):
        rows = slice(p * TOK, (p + 1) * TOK)
        grads = attend_back(
            joined[rows, 0:D],
            joined[rows, D : 2 * D],
            joined[rows, 2 * D : 3 * D],
            probs[p].arrive(),
            0,
            grad_mixed[rows],
        )
        for b in range(3):
            back[rows, b * D : (b + 1) * D] = grads[b].astype(BF)
    loads[0].arrive()
    for b in range(3):
        part = back[:, b * D : (b + 1) * D]
        put_block(made, b, dot_tn(normed[...], part))
        copies.deliver(me_ref, made, layout, outs, b)
    copies.deliver(me_ref, made, layout, outs, 4)
    grad_normed = None
    for b in range(3):
        step = dot_nt(back[:, b * D : (b + 1) * D], column_block(held, b))
        grad_normed = step if grad_normed is None else grad_normed + step
    units = [normed_of(inputs[p][...].astype(F32)) for p in range(passes)]
    unit = jnp.concatenate([u[0] for u in units], axis=0)
    inverse = jnp.concatenate([u[1] for u in units], axis=0)
    if more:
        norm_ref[...] = jnp.zeros(norm_ref.shape, F32)
        for k, other in enumerate(others):
            norm_ref[2 * k + 2 : 2 * k + 4] = other[...]
    grad = norm_back(unit, inverse, gains[row : row + 1], grad_normed, norm_ref)
    grad_in[...] = grad_out[0:TOK] + grad[0:TOK]
    copies.store(grad_in, grad_in_ref)
    copies.finish()


GELU_SCALE = 0.7978845608028654
GELU_CUBE = 0.044715


def gelu_both(up):
    square = up * up
    bent = jnp.tanh(GELU_SCALE * up * (1.0 + GELU_CUBE * square))
    half = 0.5 * (1.0 + bent)
    slope = half + 0.5 * up * (1.0 - bent * bent) * (
        GELU_SCALE * (1.0 + (3.0 * GELU_CUBE) * square)
    )
    return up * half, slope


def ffn_grads(copies, place, layout, outs, gain, hidden, grad_low, normed, active, slope, norm_ref, held, made):
    for z in range(4):
        product = dot_tn(active[:, z * D : (z + 1) * D], grad_low)
        made[z, :, 4 * BLOCK : 8 * BLOCK] = product.astype(BF).reshape(4, 4 * BLOCK, D)
    copies.deliver(place, made, layout, outs, 2)
    copies.deliver(place, made, layout, outs, 3)
    grad_normed = None
    for b in range(4):
        cols = slice(b * D, (b + 1) * D)
        grad_active = dot_nt(grad_low, row_block(held, b))
        grad_up = (slope[:, cols].astype(F32) * grad_active).astype(BF)
        put_block(made, b, dot_tn(normed[...], grad_up))
        if b % 2 == 1:
            copies.deliver(place, made, layout, outs, b // 2)
        step = dot_nt(grad_up, column_block(held, b))
        grad_normed = step if grad_normed is None else grad_normed + step
    copies.deliver(place, made, layout, outs, 4)
    unit, inverse = normed_of(hidden)
    return norm_back(unit, inverse, gain, grad_normed, norm_ref)


def ffn_back_kernel(row, layout, me_ref, gains, *refs):
    taken, refs = refs[:5], refs[5:]
    pieces, refs = refs[: layout.pieces], refs[layout.pieces :]
    grad_in_ref, norm_ref, *refs = refs
    outs, refs = refs[: layout.made], refs[layout.made :]
    grad_in, held, made, hidden, grad_out, normed, active, slope, sems = refs
    copies = Copies(sems)
    grad_out = copies.load(taken[1], grad_out)
    active = copies.load(taken[3], active)
    loads = copies.fetch(me_ref, pieces, layout, held)
    slope = copies.load(taken[4], slope)
    normed = copies.load(taken[2], normed)
    hidden = copies.load(taken[0], hidden)
    grad_low = grad_out[...].astype(BF)
    active = active.arrive()
    for load in loads:
        load.arrive()
    hidden.arrive()
    grad = ffn_grads(
        copies, me_ref, layout, outs, gains[row : row + 1], hidden[...], grad_low, normed, active, slope, norm_ref, held, made
    )
    grad_in[...] = grad_out[...] + grad
    copies.store(grad_in, grad_in_ref)
    copies.finish()


def second_kernel(encoder, cross, me_ref, src_lengths, tgt_lengths, gains, *refs):
    taken, whole, refs = refs[:2], refs[2:4], refs[4:]
    sent, made, (held_enc, held_cross, hidden_enc, hidden_one, sems) = refs[:10], refs[10:20], refs[20:]
    normed_enc, active_enc, slope_enc, memory, normed, query, pair, probs, mixed, hidden = made
    copies = Copies(sems)
    hidden_enc = copies.load(taken[0], hidden_enc)
    loads_enc = copies.fetch(me_ref, whole[:1], encoder, held_enc)
    hidden_one = copies.load(taken[1], hidden_one)
    loads_cross = copies.fetch(me_ref, whole[1:], cross, held_cross)

    unit, unused = normed_of(hidden_enc[...])
    normed_enc[...] = (unit * gains[2:3] + gains[3:4]).astype(BF)
    copies.store(normed_enc, sent[0])
    unit, unused = normed_of(hidden_one[...])
    normed[...] = (unit * gains[6:7] + gains[7:8]).astype(BF)
    copies.store(normed, sent[4])
    loads_enc[0].arrive()
    for b in range(4):
        cols = slice(b * D, (b + 1) * D)
        grown, bent = gelu_both(dot(normed_enc[...], column_block(held_enc, b)))
        active_enc[:, cols] = grown.astype(BF)
        slope_enc[:, cols] = bent.astype(BF)
    copies.store(active_enc, sent[1])
    copies.store(slope_enc, sent[2])
    loads_enc[1].arrive()
    total = hidden_enc[...]
    for z in range(4):
        total = total + dot(active_enc[:, z * D : (z + 1) * D], row_block(held_enc, z))
    memory[...] = total.astype(BF)
    copies.store(memory, sent[3])

    loads_cross[0].arrive()
    query[...] = dot(normed[...], column_block(held_cross, 0)).astype(BF)
    copies.store(query, sent[5])
    pair[:, 0:D] = dot(memory[...], column_block(held_cross, 1)).astype(BF)
    loads_cross[1].arrive()
    pair[:, D : 2 * D] = dot(memory[...], column_block(held_cross, 2)).astype(BF)
    copies.store(pair, sent[6])
    bias = mask_bias(src_lengths, tgt_lengths)
    for p in range(2):
        rows = slice(p * TOK, (p + 1) * TOK)
        part = attend(query[rows], pair[:, 0:D], pair[:, D : 2 * D], bias, probs, p * HEADS)
        heads = pl.ds(p * HEADS, HEADS)
        copies.store(probs.at[heads], sent[7].at[heads])
        mixed[rows] = part
        hidden[rows] = hidden_one[rows] + dot(part, column_block(held_cross, 3))
    copies.store(mixed, sent[8])
    copies.store(hidden, sent[9])
    copies.finish()


def middle_kernel(cross, decoder, me_ref, gains, *refs):
    taken, whole, refs = refs[:10], refs[10:11], refs[11:]
    pieces, refs = refs[: decoder.pieces], refs[decoder.pieces :]
    norm_ffn, norm_cross, *refs = refs
    sent, refs = refs[:5], refs[5:]
    come, refs = refs[:10], refs[10:]
    held_cross, held, made_cross, made, first_out, second_out, grad_memory, grad_one, *refs = refs
    normed_two, active, slope, grad_two, back, sems = refs
    copies = Copies(sems)
    hidden = copies.load(taken[0], come[0])
    loads = copies.fetch(me_ref, pieces, decoder, held)
    cots = [copies.load(taken[k], come[k]) for k in (1, 2)]
    loads_cross = copies.fetch(me_ref, whole, cross, held_cross)
    mixed, probs, query, pair, normed, memory, hidden_one = (
        copies.load(taken[k], come[k]) for k in range(3, 10)
    )

    unit, unused = normed_of(hidden[...])
    normed_two[...] = (unit * gains[8:9] + gains[9:10]).astype(BF)
    loads[0].arrive()
    for b in range(4):
        cols = slice(b * D, (b + 1) * D)
        grown, bent = gelu_both(dot(normed_two[...], column_block(held, b)))
        active[:, cols] = grown.astype(BF)
        slope[:, cols] = bent.astype(BF)
    loads[1].arrive()
    total = hidden[...]
    for z in range(4):
        total = total + dot(active[:, z * D : (z + 1) * D], row_block(held, z))
    first_out[...] = total[0:TOK].astype(BF)
    second_out[...] = total[TOK:].astype(BF)
    copies.store(first_out, sent[0])
    copies.store(second_out, sent[1])
    grad_low = jnp.concatenate([cots[0][...], cots[1][...]], axis=0)
    grad = ffn_grads(
        copies, me_ref, decoder, sent[4:], gains[8:9], hidden[...], grad_low, normed_two, active, slope, norm_ffn, held, made
    )
    grad_two[...] = grad_low.astype(F32) + grad

    grad_low = grad_two[...].astype(BF)
    put_block(made_cross, 3, dot_tn(mixed[...], grad_low))
    copies.deliver(me_ref, made_cross, cross, sent[4:], 3)
    loads_cross[1].arrive()
    grad_mixed = dot_nt(grad_low, column_block(held_cross, 3)).astype(BF)
    grad_key = grad_value = None
    probs = probs.arrive()
    for p in range(2):
        rows = slice(p * TOK, (p + 1) * TOK)
        grads = attend_back(
            query[rows], pair[:, 0:D], pair[:, D : 2 * D], probs, p * HEADS, grad_mixed[rows]
        )
        back[rows] = grads[0].astype(BF)
        grad_key = grads[1] if grad_key is None else grad_key + grads[1]
        grad_value = grads[2] if grad_value is None else grad_value + grads[2]
    grad_key = grad_key.astype(BF)
    grad_value = grad_value.astype(BF)
    for b, (left, right) in enumerate(
        ((normed[...], back[...]), (memory[...], grad_key), (memory[...], grad_value))
    ):
        put_block(made_cross, b, dot_tn(left, right))
        copies.deliver(me_ref, made_cross, cross, sent[4:], b)
    loads_cross[0].arrive()
    grad_memory[...] = dot_nt(grad_key, column_block(held_cross, 1)) + dot_nt(
        grad_value, column_block(held_cross, 2)
    )
    copies.store(grad_memory, sent[2])
    grad_normed = dot_nt(back[...], column_block(held_cross, 0))
    unit, inverse = normed_of(hidden_one[...])
    grad = norm_back(unit, inverse, gains[6:7], grad_normed, norm_cross)
    grad_one[...] = grad_two[...] + grad
    copies.store(grad_one, sent[3])
    copies.finish()


ANY = pl.BlockSpec(memory_space=pl.ANY)
HB = pl.BlockSpec(memory_space=pltpu.HBM)
VM = pl.BlockSpec(memory_space=pltpu.VMEM)
SM = pl.BlockSpec(memory_space=pltpu.SMEM)


def held_of(blocks):
    return pltpu.VMEM((4, 4, blocks * BLOCK, D), BF)


def made_of(layout, blocks):
    if layout.made == 1:
        return [jax.ShapeDtypeStruct((4, 4, layout.made_rows, D), BF)]
    return [jax.ShapeDtypeStruct((2, 2, 4, 2, blocks * BLOCK // 4, D), BF)] * 2


def shape(rows, cols, dtype):
    return jax.ShapeDtypeStruct((rows, cols), dtype)


class Order:
    def __init__(self):
        self.token = jnp.zeros((8, 128), F32)

    def tie(self, value):
        return self.tie_all([value])[0]

    def tie_all(self, values):
        arrays = list(values) + [self.token]
        *values, self.token = pl.pallas_call(
            nothing_kernel,
            name="tie",
            out_shape=[jax.ShapeDtypeStruct(x.shape, x.dtype) for x in arrays],
            in_specs=[HB] * len(arrays),
            out_specs=[HB] * len(arrays),
            input_output_aliases={k: k for k in range(len(arrays))},
            compiler_params=pltpu.CompilerParams(vmem_limit_bytes=VMEM_LIMIT),
        )(*arrays)
        return values


def nothing_kernel(*refs):
    pass


def call(order, body, name, in_specs, out_shape, out_specs, scratch, operands, micros, grid=None, inplace=()):
    count, more, outs = len(operands), len(inplace) + 1, len(out_shape)

    def ordered(*refs):
        body(*refs[:count], *refs[count + more : count + more + outs], *refs[count + more + outs + 1 :])

    aliases = {count + k: out for k, (unused, out) in enumerate(inplace)}
    aliases[count + len(inplace)] = outs
    *results, order.token = pl.pallas_call(
        ordered,
        name=name,
        out_shape=out_shape + [jax.ShapeDtypeStruct(order.token.shape, order.token.dtype)],
        in_specs=in_specs + [HB] * more,
        out_specs=out_specs + [HB],
        input_output_aliases=aliases,
        scratch_shapes=scratch,
        compiler_params=pltpu.CompilerParams(vmem_limit_bytes=VMEM_LIMIT),
        cost_estimate=pl.CostEstimate(
            flops=int((micros + 0.01) * COST), bytes_accessed=0, transcendentals=0
        ),
        **({} if grid is None else {"grid": grid}),
    )(*operands, *(array for array, unused in inplace), order.token)
    return results


def vmem(rows, cols, dtype):
    return pltpu.VMEM((rows, cols), dtype)


def probs_of(count, scratch=False):
    dims = (count * HEADS, TOK, TOK)
    return pltpu.VMEM(dims, BF) if scratch else jax.ShapeDtypeStruct(dims, BF)


SEMS = pltpu.SemaphoreType.DMA((64,))


def arrays(items):
    return [jax.ShapeDtypeStruct(dims, dtype) for dims, dtype in items]


def buffers(items):
    return [pltpu.VMEM(dims, dtype) for dims, dtype in items]


def self_kept(count):
    rows = count * TOK
    return [
        ((rows, D), F32),
        ((rows, D), BF),
        ((rows, 3 * D), BF),
        ((count * HEADS, TOK, TOK), BF),
        ((rows, D), BF),
    ]


def self_forward(order, me, src_lengths, tgt_lengths, gains, inputs, decoder, encoder):
    kept = self_kept(2) + self_kept(1)
    results = call(
        order,
        functools.partial(self_forward_kernel, decoder[0], encoder[0]),
        "self_forward",
        [SM, SM, SM, VM] + [HB] * 3 + [ANY] * (decoder[0].pieces + encoder[0].pieces),
        arrays(kept),
        [HB] * 10,
        buffers(kept) + [held_of(4), held_of(4)] + [vmem(TOK, D, BF)] * 3 + [SEMS],
        (me, src_lengths, tgt_lengths, gains, *inputs, *decoder[1], *encoder[1]),
        12,
    )
    return results[:5], results[5:]


def second(order, me, src_lengths, tgt_lengths, gains, hidden_enc, hidden_one, encoder, cross):
    rows = 2 * TOK
    kept = [
        ((TOK, D), BF),
        ((TOK, FF), BF),
        ((TOK, FF), BF),
        ((TOK, D), BF),
        ((rows, D), BF),
        ((rows, D), BF),
        ((TOK, 2 * D), BF),
        ((2 * HEADS, TOK, TOK), BF),
        ((rows, D), BF),
        ((rows, D), F32),
    ]
    results = call(
        order,
        functools.partial(second_kernel, encoder[0], cross[0]),
        "second",
        [SM, SM, SM, VM] + [HB] * 2 + [ANY] * 2,
        arrays(kept),
        [HB] * 10,
        buffers(kept) + [held_of(8), held_of(4), vmem(TOK, D, F32), vmem(rows, D, F32), SEMS],
        (me, src_lengths, tgt_lengths, gains, hidden_enc, hidden_one, encoder[1][0], cross[1][0]),
        13,
    )
    return results[:3], results[3:]


def self_back(order, row, me, gains, inputs, grad_out, kept, pieces, others=()):
    count = len(inputs)
    rows = count * TOK
    return call(
        order,
        functools.partial(self_back_kernel, count, row, len(others), pieces[0]),
        "self_back",
        [SM, VM] + [VM] * len(others) + [HB] * count + [HB] * 5 + [ANY] * pieces[0].pieces,
        [shape(TOK, D, F32), shape(16 if others else 2, D, F32)] + made_of(pieces[0], 4),
        [HB, VM] + [HB] * pieces[0].made,
        [
            vmem(TOK, D, F32),
            held_of(4),
            held_of(4),
            vmem(rows, 3 * D, BF),
            vmem(rows, D, F32),
            vmem(rows, D, BF),
            vmem(rows, 3 * D, BF),
            probs_of(count, True),
            vmem(rows, D, BF),
        ]
        + [vmem(TOK, D, BF)] * count
        + [SEMS],
        (me, gains, *others, *inputs, grad_out, *kept, *pieces[1]),
        5.8 + 3.4 * count,
    )


def ffn_back(order, row, me, gains, hidden, grad_out, kept, pieces):
    return call(
        order,
        functools.partial(ffn_back_kernel, row, pieces[0]),
        "ffn_back",
        [SM, VM] + [HB] * 5 + [ANY] * pieces[0].pieces,
        [shape(TOK, D, F32), shape(2, D, F32)] + made_of(pieces[0], 8),
        [HB, VM] + [HB] * pieces[0].made,
        [
            vmem(TOK, D, F32),
            held_of(8),
            held_of(8),
            vmem(TOK, D, F32),
            vmem(TOK, D, F32),
            vmem(TOK, D, BF),
            vmem(TOK, FF, BF),
            vmem(TOK, FF, BF),
            SEMS,
        ],
        (me, gains, hidden, grad_out, *kept, *pieces[1]),
        10.2,
    )


def middle(order, me, gains, hidden_one, kept, cots, cross, decoder):
    rows = 2 * TOK
    memory, normed, query, pair, probs, mixed, hidden = kept
    taken = [hidden, *cots, mixed, probs, query, pair, normed, memory, hidden_one]
    sent = [((TOK, D), BF), ((TOK, D), BF), ((TOK, D), F32), ((rows, D), F32)]
    return call(
        order,
        functools.partial(middle_kernel, cross[0], decoder[0]),
        "middle",
        [SM, VM] + [HB] * 10 + [ANY] * (1 + decoder[0].pieces),
        [shape(2, D, F32)] * 2 + arrays(sent + [((4, 4, 384, D), BF)]),
        [VM] * 2 + [HB] * 5,
        buffers([(x.shape, x.dtype) for x in taken])
        + [held_of(4), held_of(8), held_of(4), held_of(8)]
        + buffers(sent)
        + [
            vmem(rows, D, BF),
            vmem(rows, FF, BF),
            vmem(rows, FF, BF),
            vmem(rows, D, F32),
            vmem(rows, D, BF),
            SEMS,
        ],
        (me, gains, *taken, cross[1][0], *decoder[1]),
        25,
    )


AXIS = "fsdp"
BOTH = ("dp", "fsdp")
SHARDS = 16


def route(target):
    pairs = []
    for i in range(2 * SHARDS):
        dp, z, y, core = target(i // 16, (i // 4) % 4, (i // 2) % 2, i % 2)
        pairs.append((i, dp * 16 + (z % 4) * 4 + y * 2 + core))
    return pairs


def to_core(x):
    return lax.ppermute(x, BOTH, route(lambda dp, z, y, core: (dp, z, y, 1 - core)))


def to_z(x, step):
    return lax.ppermute(x, BOTH, route(lambda dp, z, y, core: (dp, z + step, y, core)))


def to_z_pair(x, step):
    return lax.ppermute(x, BOTH, route(lambda dp, z, y, core: (dp, z ^ step, y, core)))


def to_y(x):
    return lax.ppermute(x, BOTH, route(lambda dp, z, y, core: (dp, z, 1 - y, core)))


def to_dp(x):
    return lax.ppermute(x, BOTH, route(lambda dp, z, y, core: (1 - dp, z, y, core)))


def to_yx(x):
    return lax.ppermute(
        x, BOTH, route(lambda dp, z, y, core: (dp, z, y ^ 1, core) if core == 0 else (dp ^ 1, z, y, core))
    )


def to_xy(x):
    return lax.ppermute(
        x, BOTH, route(lambda dp, z, y, core: (dp ^ 1, z, y, core) if core == 0 else (dp, z, y ^ 1, core))
    )


def blocks_of(shard):
    rows, cols = shard.shape
    split = shard.reshape(rows // BLOCK, BLOCK, cols // D, D)
    return split.transpose(2, 0, 1, 3).reshape(-1, BLOCK, D)


def shard_of(blocks, cols):
    wide = blocks.reshape(cols // D, -1, D)
    return wide.transpose(1, 0, 2).reshape(-1, cols)


def small(order, body, name, out, operands, scratch=(), in_specs=None, out_specs=None, micros=0, grid=None):
    return call(
        order,
        body,
        name,
        in_specs if in_specs is not None else [VM] * len(operands),
        [jax.ShapeDtypeStruct(dims, dtype) for dims, dtype in out],
        out_specs if out_specs is not None else [VM] * len(out),
        list(scratch),
        operands,
        micros,
        grid,
    )


def pack_kernel(place, *refs):
    weights, (one, two, three, norms) = refs[:15], refs[15:]
    self_in, self_out, enc_in, enc_out, enc_ffn_in, enc_ffn_out = weights[:6]
    cross_q, cross_kv, cross_out, ffn_in, ffn_out = weights[6:11]
    for half in range(2):

        @pl.when(place[2] == half)
        def _():
            for k in range(2):
                quarter = 2 * half + k
                cols = slice(quarter * D, (quarter + 1) * D)
                one[k, 0:32] = self_out[...] if quarter == 3 else self_in[:, cols]
                one[k, 32:64] = enc_out[...] if quarter == 3 else enc_in[:, cols]
                for j in range(2):
                    block = 2 * quarter + j
                    rows = slice(j * BLOCK, (j + 1) * BLOCK)
                    cols = slice(block * D, (block + 1) * D)
                    part = slice((block - 4) * BLOCK, (block - 3) * BLOCK)
                    three[k, rows] = ffn_in[:, cols] if block < 4 else ffn_out[part]

    for block in range(4):
        rows = slice(block * BLOCK, (block + 1) * BLOCK)
        two[rows] = enc_ffn_in[:, block * D : (block + 1) * D]
    two[128:256] = enc_ffn_out[...]
    two[256:288] = cross_q[...]
    two[288:320] = cross_kv[:, 0:D]
    two[320:352] = cross_kv[:, D : 2 * D]
    two[352:384] = cross_out[...]
    norms[...] = jnp.zeros(norms.shape, F32)
    row = 0
    for gain, bias in (weights[11:13], weights[13:15]):
        for k in range(gain.shape[0]):
            norms[row : row + 1, 0:BLOCK] = gain[k : k + 1].astype(F32)
            norms[row + 1 : row + 2, 0:BLOCK] = bias[k : k + 1].astype(F32)
            row += 2
    for k in range(2):
        one[k, 64:80] = norms[...].astype(BF)


def pack(order, place, weights, norms):
    return small(
        order,
        pack_kernel,
        "pack",
        [((2, 80, D), BF), ((384, D), BF), ((2, 64, D), BF)],
        (place, *weights, *norms),
        [pltpu.VMEM((16, D), F32)],
        in_specs=[SM] + [VM] * 15,
    )


def pair_kernel(place, *refs):
    core = place[3]
    for k in range(2):
        mine, near, pair = refs[2 * k], refs[2 * k + 1], refs[4 + k]
        pair[core] = mine[core]
        pair[1 - core] = near[core]


def pair_up(order, place, mine, near):
    operands = [x for both in zip(mine, near) for x in both]
    return small(
        order,
        pair_kernel,
        "pair_up",
        [(x.shape, x.dtype) for x in mine],
        (place, *operands),
        in_specs=[SM] + [VM] * 4,
    )


def stack_kernel(place, *refs):
    parts, (out, held, sems) = refs[:-3], refs[-3:]
    count = len(parts)
    loads = [pltpu.make_async_copy(parts[d], held.at[d], sems.at[d]) for d in range(count)]
    stores = [
        pltpu.make_async_copy(held.at[d], out.at[(place[0] + (4 - d)) & 3], sems.at[count + d])
        for d in range(count)
    ]
    for copy in loads:
        copy.start()
    for d in range(count):
        loads[d].wait()
        stores[d].start()
    wait_all(stores)


def stack(order, place, parts):
    dims = (len(parts),) + parts[0].shape
    dtype = parts[0].dtype
    return small(
        order,
        stack_kernel,
        "stack",
        [(dims, dtype)],
        (place, *parts),
        [pltpu.VMEM(dims, dtype), pltpu.SemaphoreType.DMA((2 * len(parts),))],
        [SM] + [ANY] * len(parts),
        [ANY],
    )[0]


def table_kernel(place, own, across, down, gains, held, sems):
    copies = []
    for k, piece in enumerate((own, across, down)):
        copies.append(pltpu.make_async_copy(piece.at[:, :, pl.ds(64, 16)], held.at[k], sems.at[k]))
    for copy in copies:
        copy.start()
    wait_all(copies)
    far = jnp.where(place[3] == 0, 2, 1)
    for y in range(2):
        where = jnp.where(place[1] == y, 0, far)
        for z in range(4):
            for core in range(2):
                spot = 4 * z + 2 * y + core
                row = held[where, z, core]
                gains[:, spot * BLOCK : (spot + 1) * BLOCK] = row[:, 0:BLOCK].astype(F32)


def norm_table(order, place, pieces):
    return small(
        order,
        table_kernel,
        "norm_table",
        [((16, D), F32)],
        (place, pieces[0], pieces[1], pieces[2]),
        [pltpu.VMEM((3, 4, 2, 16, D), BF), pltpu.SemaphoreType.DMA((3,))],
        [SM, ANY, ANY, ANY],
    )[0]


class Gather:
    def __init__(self, order, pair):
        self.order, self.pair = order, pair

    def along_z(self):
        pair = self.order.tie(self.pair)
        self.parts = [pair] + [to_z(pair, d) for d in (1, 2, 3)]

    def lined(self, place):
        self.line = stack(self.order, place, self.parts)

    def first_cross(self):
        line = self.order.tie(self.line)
        self.own = [line, to_xy(line), to_yx(line)]
        self.near = []

    def crossed(self, others=()):
        arrived = self.order.tie_all(self.own[1:3] + list(others[1:]))
        self.own[1:3] = arrived[:2]
        if others:
            others[1:] = arrived[2:]

    def second_cross(self):
        self.own.append(to_yx(self.own[1]))

    def share(self, k):
        self.near.append(self.order.tie(to_core(self.own[k])))

    def done(self):
        last = self.order.tie(self.own[3])
        self.own = self.own[:3] + [last]
        self.near.append(self.order.tie(to_core(last)))
        self.pieces = tuple(self.own + self.near)


def low_sum(*parts):
    total = parts[0].astype(F32)
    for part in parts[1:]:
        total = total + part.astype(F32)
    return total.astype(BF)


def rows_of(parts):
    row = 0
    for k, part in enumerate(parts[::2]):
        yield slice(row, row + part.shape[4]), part, parts[2 * k + 1]
        row += part.shape[4]


def send_block(step, source, target, sems, more):
    def copies():
        for k in range(4):
            yield k, pltpu.make_async_copy(
                source.at[k], target.at[pl.ds(k * source.shape[1], source.shape[1])], sems.at[k]
            )

    last = pltpu.make_async_copy(*more, sems.at[4])
    for k, copy in copies():
        pl.when(step == k)(copy.start)
    pl.when(step == 0)(last.start)

    @pl.when(step == 3)
    def _():
        for unused, copy in copies():
            copy.wait()
        last.wait()


def reduce_first_kernel(norm_own, norm_came, *refs):
    sent, held, norm, sems = refs[-4:]
    step = pl.program_id(0)

    @pl.when(step == 0)
    def _():
        norm[...] = (norm_own[...] + norm_came[...]).astype(BF)

    whole = held.shape[1] // 4
    for rows, own, came in rows_of(refs[:-4]):
        for second in range(2):
            for core in range(2):
                row = (2 * second + core) * whole + rows.start
                held[step, row : row + rows.stop - rows.start] = (
                    own[0, second, 0, core] + came[0, second, 0, core]
                )
    send_block(step, held, sent, sems, (norm, sent.at[pl.ds(16 * whole, 16)]))


def reduce_second_kernel(norm_own, norm_came, came_first, *refs):
    sent, held, norm, sems = refs[-4:]
    step = pl.program_id(0)

    @pl.when(step == 0)
    def _():
        norm[...] = (norm_own[...].astype(F32) + norm_came[...].astype(F32)).astype(BF)

    whole = held.shape[1] // 2
    for rows, own, came in rows_of(refs[:-4]):
        for core in range(2):
            span = slice(core * whole + rows.start, core * whole + rows.stop)
            held[step, span] = low_sum(own[0, 0, 0, core], came[0, 0, 0, core], came_first[span])
    send_block(step, held, sent, sems, (norm, sent.at[pl.ds(8 * whole, 16)]))


def reduce_third_kernel(norm_own, norm_came, place, came_first, came_second, *refs):
    outs = refs[-4:]
    norm = (norm_own[...].astype(F32) + norm_came[...].astype(F32)).astype(BF)
    whole = (outs[0].shape[0] - 16) // 2
    for d in range(4):
        z = (place[0] + d) & 3
        outs[d][2 * whole :] = norm
        for rows, own, came in rows_of(refs[:-4]):
            for core in range(2):
                span = slice(core * whole + rows.start, core * whole + rows.stop)
                size = rows.stop - rows.start
                first = pl.multiple_of(z * 4 * whole + span.start, 16)
                second = pl.multiple_of(z * 2 * whole + span.start, 16)
                outs[d][span] = low_sum(
                    own[0, 0, z, core],
                    came[0, 0, z, core],
                    came_first[pl.ds(first, size)],
                    came_second[pl.ds(second, size)],
                )


def reduce_fourth_kernel(a, b, c, d, out, norm):
    rows = out.shape[1]
    for core in range(2):
        span = slice(core * rows, (core + 1) * rows)
        out[core] = low_sum(a[span], b[span], c[span], d[span])
    total = a[2 * rows :].astype(F32)
    for part in (b, c, d):
        total = total + part[2 * rows :].astype(F32)
    norm[...] = total


class Reduce:
    def __init__(self, order):
        self.order, self.own, self.came = order, [], []

    def add(self, own, other):
        self.own.append(own)
        self.came.append(to_core(self.order.tie(other)))

    def arrive(self):
        self.came[-1] = self.order.tie(self.came[-1])

    def start_norm(self, norm):
        self.norm = self.order.tie(norm)
        self.norm_came = to_core(self.norm)

    def run(self, body, name, dims, operands, in_specs, part_spec, out_specs=None, scratch=(), grid=(4,)):
        parts = [x for both in zip(self.own, self.came) for x in both]
        specs = [pl.BlockSpec(part_spec[0] + (part.shape[4], D), part_spec[1]) for part in parts]
        sent = small(
            self.order,
            body,
            name,
            [(item, BF) for item in dims],
            operands + parts,
            scratch,
            in_specs=in_specs + specs,
            out_specs=out_specs or [HB] * len(dims),
            grid=grid,
        )
        return [self.order.tie(x) for x in sent]

    def first(self):
        rows = self.rows = sum(own.shape[4] for own in self.own)
        norm_spec = pl.BlockSpec((16, D), lambda i: (0, 0))
        (self.first_sent,) = self.run(
            reduce_first_kernel,
            "reduce_first",
            [(16 * rows + 16, D)],
            [self.norm, self.norm_came],
            [norm_spec] * 2,
            ((1, 2, 1, 2), lambda i: (1, 0, i, 0, 0, 0)),
            scratch=buffers([((4, 4 * rows, D), BF), ((16, D), BF)]) + [pltpu.SemaphoreType.DMA((5,))],
        )
        self.first_came = to_yx(self.first_sent)

    def second(self):
        rows = self.rows
        norm_spec = pl.BlockSpec((16, D), lambda i: (rows, 0))
        (self.second_sent,) = self.run(
            reduce_second_kernel,
            "reduce_second",
            [(8 * rows + 16, D)],
            [self.first_sent, self.first_came, self.first_came],
            [norm_spec] * 2 + [pl.BlockSpec((2 * rows, D), lambda i: (2 * i + 1, 0))],
            ((1, 1, 1, 2), lambda i: (0, 1, i, 0, 0, 0)),
            scratch=buffers([((4, 2 * rows, D), BF), ((16, D), BF)]) + [pltpu.SemaphoreType.DMA((5,))],
        )
        self.second_came = to_xy(self.second_sent)

    def third(self, place):
        rows = self.rows
        norm_spec = pl.BlockSpec((16, D), lambda i: (rows // 2, 0))
        parts = self.run(
            reduce_third_kernel,
            "reduce_third",
            [(2 * rows + 16, D)] * 4,
            [self.second_sent, self.second_came, place, self.first_came, self.second_came],
            [norm_spec] * 2
            + [SM]
            + [pl.BlockSpec(x.shape, lambda i: (0, 0)) for x in (self.first_came, self.second_came)],
            ((1, 1, 4, 2), lambda i: (0, 0, 0, 0, 0, 0)),
            [pl.BlockSpec((2 * rows + 16, D), lambda i: (0, 0))] * 4,
            grid=(1,),
        )
        self.lines = [parts[0]] + [to_z(parts[d], d) for d in (1, 2, 3)]

    def fourth(self):
        total, self.norm = small(
            self.order,
            reduce_fourth_kernel,
            "reduce_fourth",
            [((2, self.rows, D), BF), ((16, D), F32)],
            self.lines,
        )
        total = self.order.tie(total)
        self.ends = [total, to_dp(total), to_core(total)]

    def last(self):
        near = self.order.tie(self.ends[2])
        came = self.order.tie(self.ends[1])
        self.ends = [self.ends[0], came, near, to_core(came)]


def quarter_of(place, ends, quarter, rows):
    core = place[3]
    half, which = quarter >> 1, quarter & 1
    first = jnp.where(place[3] == which, ends[0][core, rows], ends[2][core, rows].astype(BF))
    second = jnp.where(place[3] == which, ends[1][core, rows], ends[3][core, rows])
    return jnp.where(place[2] == half, first, second).astype(F32)


def unpack_kernel(layout, place, *refs):
    ends, outs = refs[:4], refs[4:]
    first = 0
    for kind, row in layout:
        for quarter in range(4):
            if kind == "ffn":
                for j in range(2):
                    block = 2 * quarter + j
                    rows = slice(row + j * BLOCK, row + (j + 1) * BLOCK)
                    value = quarter_of(place, ends, quarter, rows)
                    if block < 4:
                        outs[first][:, block * D : (block + 1) * D] = value
                    else:
                        outs[first + 1][(block - 4) * BLOCK : (block - 3) * BLOCK] = value
            else:
                value = quarter_of(place, ends, quarter, slice(row, row + BLOCK))
                if kind == "attn":
                    if quarter < 3:
                        outs[first][:, quarter * D : (quarter + 1) * D] = value
                    else:
                        outs[first + 1][...] = value
                elif quarter in (1, 2):
                    outs[first + 1][:, (quarter - 1) * D : quarter * D] = value
                else:
                    outs[first + (quarter + 1) // 2][...] = value
        first += 3 if kind == "cross" else 2


SHARD_SHAPES = {
    "ffn": [((BLOCK, FF), F32), ((4 * BLOCK, D), F32)],
    "attn": [((BLOCK, 3 * D), F32), ((BLOCK, D), F32)],
    "cross": [((BLOCK, D), F32), ((BLOCK, 2 * D), F32), ((BLOCK, D), F32)],
}


def unpack(order, place, ends, layout):
    return small(
        order,
        functools.partial(unpack_kernel, layout),
        "unpack",
        [item for kind, unused in layout for item in SHARD_SHAPES[kind]],
        (place, *ends),
        in_specs=[SM] + [VM] * 4,
    )


def norm_last_kernel(place, total, *outs):
    total = total[...]
    spot = place[0] * 4 + place[1] * 2 + place[3]
    turned = jnp.zeros((16, BLOCK), F32)
    for k in range(SHARDS):
        turned = jnp.where(spot == k, total[:, k * BLOCK : (k + 1) * BLOCK], turned)
    for first, gain, bias in ((0, outs[0], outs[1]), (4, outs[2], outs[3])):
        for k in range(gain.shape[0]):
            gain[k : k + 1] = turned[first + 2 * k : first + 2 * k + 1]
            bias[k : k + 1] = turned[first + 2 * k + 1 : first + 2 * k + 2]


def norm_last(order, place, total):
    return small(
        order,
        norm_last_kernel,
        "norm_last",
        [((2, BLOCK), F32), ((2, BLOCK), F32), ((3, BLOCK), F32), ((3, BLOCK), F32)],
        (place, total),
        in_specs=[SM, VM],
    )


def spread_kernel(own, came, ffn_in, ffn_out, cross_q, cross_kv, cross_out):
    total = own[...].astype(F32) + came[...].astype(F32)
    for block in range(4):
        ffn_in[:, block * D : (block + 1) * D] = total[block * BLOCK : (block + 1) * BLOCK]
    ffn_out[...] = total[128:256]
    cross_q[...] = total[256:288]
    cross_kv[:, 0:D] = total[288:320]
    cross_kv[:, D : 2 * D] = total[320:352]
    cross_out[...] = total[352:384]


def spread(order, own, came):
    return small(
        order,
        spread_kernel,
        "spread",
        SHARD_SHAPES["ffn"] + SHARD_SHAPES["cross"],
        (own, came),
    )


def gather_plain(weights):
    parts = []
    for weight in weights:
        whole = lax.all_gather(weight, AXIS, axis=0, tiled=True)
        parts.append(jax.vmap(blocks_of)(whole.reshape(SHARDS, -1, whole.shape[1])))
    return jnp.concatenate(parts, axis=1).reshape(4, 4, -1, D)


def reduce_plain(made, columns):
    shards = made.reshape(SHARDS, -1, BLOCK, D)
    grads = []
    for first, last, cols in columns:
        whole = jax.vmap(functools.partial(shard_of, cols=cols))(shards[:, first:last])
        whole = whole.reshape(-1, cols).astype(F32)
        part = lax.psum_scatter(whole, AXIS, scatter_dimension=0, tiled=True)
        grads.append(lax.psum(part.astype(BF), "dp").astype(F32))
    return grads


def norm_rows_of(gain_enc, bias_enc, gain_dec, bias_dec):
    rows = []
    for gain, bias in ((gain_enc, bias_enc), (gain_dec, bias_dec)):
        for k in range(gain.shape[0]):
            rows += [gain[k : k + 1], bias[k : k + 1]]
    return jnp.concatenate(rows, axis=0)


ATTN_COLUMNS = ((0, 3, 3 * D), (3, 4, D))
FFN_COLUMNS = ((0, 4, FF), (4, 8, D))
CROSS_COLUMNS = ((0, 1, D), (1, 3, 2 * D), (3, 4, D))


def step(
    custom,
    source,
    first_in,
    second_in,
    cot_first,
    cot_second,
    src_lengths,
    tgt_lengths,
    enc_attn_in,
    enc_attn_out,
    enc_ffn_in,
    enc_ffn_out,
    enc_gain,
    enc_bias,
    dec_self_in,
    dec_self_out,
    dec_cross_q,
    dec_cross_kv,
    dec_cross_out,
    dec_ffn_in,
    dec_ffn_out,
    dec_gain,
    dec_bias,
):
    spot = lax.axis_index(AXIS)
    order = Order()
    group_self = (dec_self_in, dec_self_out)
    group_enc = (enc_attn_in, enc_attn_out)
    group_enc_ffn = (enc_ffn_in, enc_ffn_out)
    group_cross = (dec_cross_q, dec_cross_kv, dec_cross_out)
    group_ffn = (dec_ffn_in, dec_ffn_out)
    if custom:
        place = jnp.stack([spot >> 2, (spot >> 1) & 1, lax.axis_index("dp"), spot & 1]).astype(jnp.int32)
        weights = group_self + group_enc + group_enc_ffn + group_cross + group_ffn
        mine_one, mine_two, mine_three = pack(
            order, place, weights, (enc_gain, enc_bias, dec_gain, dec_bias)
        )
        mine = (mine_one, mine_three)
        pairs = pair_up(order, place, mine, [to_core(x) for x in mine])
        one, three = (Gather(order, pair) for pair in pairs)
        one.along_z()
        one.parts[3] = order.tie(one.parts[3])
        mine_two = order.tie(mine_two)
        whole = lax.all_gather(mine_two, AXIS, axis=0, tiled=True).reshape(4, 4, -1, D)
        one.lined(place)
        one.first_cross()
        three.along_z()
        one.crossed(three.parts)
        one.second_cross()
        three.lined(place)
        three.first_cross()
        for k in range(3):
            one.share(k)
        one.done()
        gains = norm_table(order, place, one.pieces)
        w_self, w_enc = (Layout(0, 8), one.pieces), (Layout(32, 8), one.pieces)
        w_enc_ffn = (Layout(0, 1), (whole,))
        w_cross = (Layout(256, 1, 1, 256, 384), (whole,))
    else:
        place = jnp.zeros((4,), jnp.int32)
        w_self, w_enc, w_enc_ffn = (
            (Layout(0, 1, 1, 0, rows), (gather_plain(group),))
            for group, rows in ((group_self, 128), (group_enc, 128), (group_enc_ffn, 256))
        )
        w_cross = (Layout(0, 1, 1, 256, 384), (gather_plain(group_cross),))
        w_ffn = (Layout(0, 1, 1, 0, 384), (gather_plain(group_ffn),))
        norm_rows = norm_rows_of(enc_gain, enc_bias, dec_gain, dec_bias)
        gains = lax.all_gather(norm_rows, AXIS, axis=1, tiled=True)
        gains = jnp.pad(gains.astype(F32), ((0, 6), (0, 0)))

    (hidden_one, *kept_self), (hidden_enc, *kept_enc) = self_forward(
        order, place, src_lengths, tgt_lengths, gains, [first_in, second_in, source], w_self, w_enc
    )
    if custom:
        three.crossed()
        three.second_cross()
        for k in range(3):
            three.share(k)
    kept_enc_ffn, kept_cross = second(
        order, place, src_lengths, tgt_lengths, gains, hidden_enc, hidden_one, w_enc_ffn, w_cross
    )
    if custom:
        three.done()
        w_ffn = (Layout(0, 8, 1, 0, 384), three.pieces)
    norm_ffn, norm_cross, first_out, second_out, grad_memory, grad_one, made = middle(
        order, place, gains, hidden_one, kept_cross, (cot_first, cot_second), w_cross, w_ffn
    )
    if custom:
        scattered = lax.psum_scatter(
            made.reshape(-1, D), AXIS, scatter_dimension=0, tiled=True
        )
    grad_enc, norm_enc_ffn, *made_enc_ffn = ffn_back(
        order, 2, place, gains, hidden_enc, grad_memory, kept_enc_ffn, w_enc_ffn
    )
    if custom:
        red = Reduce(order)
        red.add(*made_enc_ffn)
    grad_first, norm_self, *made_self = self_back(
        order, 4, place, gains, [first_in, second_in], grad_one, kept_self, w_self
    )
    if custom:
        red.arrive()
        red.add(*made_self)
    grad_source, norm_total, *made_enc = self_back(
        order,
        0,
        place,
        gains,
        [source],
        grad_enc,
        kept_enc,
        w_enc,
        (norm_enc_ffn, norm_self, norm_cross, norm_ffn),
    )
    if custom:
        red.arrive()
        red.add(*made_enc)
        red.start_norm(norm_total)
        red.first()
        red.second()
        red.third(place)
        scattered = order.tie(scattered)
        scattered_came = order.tie(to_dp(scattered))
        red.fourth()
        grads_ffn_cross = spread(order, scattered, scattered_came)
        norm_grads = norm_last(order, place, red.norm)
        red.last()
        grads_ffn, grads_cross = grads_ffn_cross[:2], grads_ffn_cross[2:]
        g = unpack(order, place, red.ends, (("ffn", 0), ("attn", 64), ("attn", 96)))
        grads_enc_ffn, grads_self, grads_enc = g[:2], g[2:4], g[4:6]
    else:
        grads_ffn = reduce_plain(made[:, :, 0:256], FFN_COLUMNS)
        grads_cross = reduce_plain(made[:, :, 256:384], CROSS_COLUMNS)
        grads_enc_ffn = reduce_plain(*made_enc_ffn, FFN_COLUMNS)
        grads_self = reduce_plain(*made_self, ATTN_COLUMNS)
        grads_enc = reduce_plain(*made_enc, ATTN_COLUMNS)
        norm_shard = lax.psum_scatter(norm_total, AXIS, scatter_dimension=1, tiled=True)
        norm_shard = lax.psum(norm_shard.astype(BF), "dp").astype(F32)
        norm_grads = (norm_shard[0:4:2], norm_shard[1:4:2], norm_shard[4:10:2], norm_shard[5:10:2])
    return (
        first_out,
        second_out,
        grad_source,
        grad_first,
        *grads_enc,
        *grads_enc_ffn,
        *norm_grads[:2],
        *grads_self,
        *grads_cross,
        *grads_ffn,
        *norm_grads[2:],
    )


def solution(mesh):
    blocked = P(("dp", "fsdp"), None)
    rows = P("fsdp", None)
    columns = P(None, "fsdp")
    custom = mesh.shape["fsdp"] == SHARDS and mesh.shape["dp"] == 2
    return jax.shard_map(
        functools.partial(step, custom),
        mesh=mesh,
        in_specs=(blocked,) * 7 + (rows,) * 4 + (columns,) * 2 + (rows,) * 7 + (columns,) * 2,
        out_specs=(blocked,) * 4 + (rows,) * 4 + (columns,) * 2 + (rows,) * 7 + (columns,) * 2,
        check_vma=False,
    )
```

```python
import functools
import typing

import jax
import jax.numpy as jnp
from jax import lax
from jax.experimental import pallas as pl
from jax.experimental.pallas import tpu as pltpu
from jax.sharding import PartitionSpec as P

D = 512
HEADS = 8
HEAD = 64
TOK = 256
FF = 2048
QUAD = 256
BLOCK = 32
EPSILON = 1e-05
MASKED = -1000000000.0
BF = jnp.bfloat16
F32 = jnp.float32
VMEM_LIMIT = 64 * 1024 * 1024
COST = 1.1e9


class Layout(typing.NamedTuple):
    offset: int
    pieces: int
    made: int = 2
    made_offset: int = 0
    made_rows: int = 0


def dot(left, right):
    return lax.dot_general(left, right, (((1,), (0,)), ((), ())), preferred_element_type=F32)


def dot_nt(left, right):
    return lax.dot_general(left, right, (((1,), (1,)), ((), ())), preferred_element_type=F32)


def dot_tn(left, right):
    return lax.dot_general(left, right, (((0,), (0,)), ((), ())), preferred_element_type=F32)


def wait_all(copies):
    for copy in copies:
        copy.wait()


def column_block(held, index):
    return held[:, :, index * BLOCK : (index + 1) * BLOCK].reshape(D, D)


def row_block(held, index):
    return held[index, :, 4 * BLOCK : 8 * BLOCK].reshape(D, D)


def normed_of(values):
    centre = values - jnp.mean(values, axis=-1, keepdims=True)
    spread = jnp.mean(centre * centre, axis=-1, keepdims=True)
    inverse = lax.rsqrt(spread + EPSILON)
    return centre * inverse, inverse


def norm_back(unit, inverse, gain, grad_normed, norm_ref):
    norm_ref[0:1] = jnp.sum(grad_normed * unit, axis=0, keepdims=True)
    norm_ref[1:2] = jnp.sum(grad_normed, axis=0, keepdims=True)
    grad_unit = grad_normed * gain
    return (
        grad_unit
        - jnp.mean(grad_unit, axis=-1, keepdims=True)
        - unit * jnp.mean(grad_unit * unit, axis=-1, keepdims=True)
    ) * inverse


def mask_bias(key_lengths, query_lengths):
    key_place = lax.broadcasted_iota(jnp.int32, (TOK, 1), 0)
    query_place = lax.broadcasted_iota(jnp.int32, (1, TOK), 1)
    key_ids = jnp.zeros((TOK, 1), jnp.int32)
    query_ids = jnp.zeros((1, TOK), jnp.int32)
    key_end = jnp.int32(0)
    query_end = jnp.int32(0)
    for k in range(key_lengths.shape[1]):
        key_end = key_end + key_lengths[0, k]
        query_end = query_end + query_lengths[0, k]
        key_ids = key_ids + jnp.where(key_place >= key_end, 1, 0)
        query_ids = query_ids + jnp.where(query_place >= query_end, 1, 0)
    return jnp.where(key_ids == query_ids, 0.0, MASKED).astype(F32)


def lane_masks():
    head_of = lax.broadcasted_iota(jnp.int32, (1, QUAD), 1) // HEAD
    return [jnp.where(head_of == h, 1.0, 0.0).astype(BF) for h in range(QUAD // HEAD)]


def attend(queries, keys, values, bias, probs_ref, first):
    masks = lane_masks()
    outs = []
    for g in range(D // QUAD):
        cols = slice(g * QUAD, (g + 1) * QUAD)
        q, k, v = queries[:, cols], keys[:, cols], values[:, cols]
        total = None
        for h in range(QUAD // HEAD):
            scores = dot_nt(k * (masks[h] * (HEAD**-0.5)), q) + bias
            top = jnp.max(scores, axis=0, keepdims=True)
            grown = jnp.exp(scores - top)
            probs = (grown * (1.0 / jnp.sum(grown, axis=0, keepdims=True))).astype(BF)
            probs_ref[first + g * (QUAD // HEAD) + h] = probs
            part = dot_tn(probs, v * masks[h])
            total = part if total is None else total + part
        outs.append(total.astype(BF))
    return jnp.concatenate(outs, axis=1)


def attend_back(queries, keys, values, probs_ref, first, grad_mixed):
    masks = lane_masks()
    grads = []
    for g in range(D // QUAD):
        cols = slice(g * QUAD, (g + 1) * QUAD)
        q, k, v, go = queries[:, cols], keys[:, cols], values[:, cols], grad_mixed[:, cols]
        gq = gk = gv = None
        for h in range(QUAD // HEAD):
            probs_low = probs_ref[first + g * (QUAD // HEAD) + h]
            probs = probs_low.astype(F32)
            grad_probs = dot_nt(v * masks[h], go)
            both = probs * grad_probs
            grad_scores = (both - probs * jnp.sum(both, axis=0, keepdims=True)).astype(BF)
            part_v = dot(probs_low, go * masks[h])
            part_k = dot(grad_scores, q * masks[h])
            part_q = dot_tn(grad_scores, k * masks[h])
            gv = part_v if gv is None else gv + part_v
            gk = part_k if gk is None else gk + part_k
            gq = part_q if gq is None else gq + part_q
        grads.append((gq * (HEAD**-0.5), gk * (HEAD**-0.5), gv))
    return tuple(jnp.concatenate(parts, axis=1) for parts in zip(*grads))


def put_block(held, index, product):
    held[:, :, index * BLOCK : (index + 1) * BLOCK] = product.astype(BF).reshape(4, 4, BLOCK, D)


class Copies:
    def __init__(self, sems):
        self.sems, self.count, self.out = sems, 0, []

    def start(self, source, target):
        copy = pltpu.make_async_copy(source, target, self.sems.at[self.count])
        self.count += 1
        copy.start()
        return copy

    def load(self, source, target):
        return Loaded(target, [self.start(source, target)])

    def store(self, source, target):
        self.out.append(self.start(source, target))

    def finish(self):
        wait_all(self.out)

    def fetch(self, place, pieces, layout, held):
        rows = held.shape[2] // 4
        if layout.pieces == 1:
            loads = []
            for half in range(2):
                part = pieces[0].at[:, :, pl.ds(layout.offset + 2 * half * rows, 2 * rows)]
                loads.append(self.load(part, held.at[:, :, pl.ds(2 * half * rows, 2 * rows)]))
            return loads
        copies = []
        for turn in range(2):
            for first in range(2):
                for second in range(2):
                    y, half, which = place[1] ^ first, place[2] ^ second, place[3] ^ turn
                    quarter = pl.multiple_of((2 * half + which) * rows, rows)
                    piece = pieces[4 * turn + 2 * first + second]
                    copies.append(
                        self.start(
                            piece.at[:, :, pl.ds(layout.offset, rows)],
                            held.at[:, pl.ds(2 * y, 2), pl.ds(quarter, rows)],
                        )
                    )
        return [Loaded(held, copies)] * 2

    def deliver(self, place, held, layout, outs, *quarters):
        rows = held.shape[2] // 4
        if layout.made == 1:
            for quarter in (q for q in quarters if q < 4):
                part = pl.ds(layout.made_offset + quarter * rows, rows)
                self.store(held.at[:, :, pl.ds(quarter * rows, rows)], outs[0].at[:, :, part])
        elif 4 in quarters:
            for turn in range(2):
                for first in range(2):
                    for second in range(2):
                        y, half, which = place_of(place, turn, first, second)
                        quarter = pl.multiple_of((2 * half + which) * rows, rows)
                        self.store(
                            held.at[:, pl.ds(2 * y, 2), pl.ds(quarter, rows)],
                            outs[turn].at[first, second],
                        )


def place_of(place, turn, first, second):
    which = place[3] ^ turn
    y = place[1] ^ jnp.where(which == 0, first, second)
    half = place[2] ^ jnp.where(which == 0, second, first)
    return y, half, which


class Loaded:
    def __init__(self, target, copies):
        self.target, self.copies = target, copies

    def arrive(self):
        wait_all(self.copies)
        self.copies.clear()
        return self.target

    def __getitem__(self, index):
        return self.arrive()[index]


def self_forward_part(copies, row, gains, bias, inputs, loads, held, scratch, outs):
    out, normed, joined, probs, mixed = scratch
    out_ref, normed_ref, joined_ref, probs_ref, mixed_ref = outs
    passes = len(inputs)
    for p in range(passes):
        rows = slice(p * TOK, (p + 1) * TOK)
        unit, unused = normed_of(inputs[p][...].astype(F32))
        normed[rows] = (unit * gains[row : row + 1] + gains[row + 1 : row + 2]).astype(BF)
    copies.store(normed, normed_ref)
    for b in range(3):
        loads[b // 2].arrive()
        joined[:, b * D : (b + 1) * D] = dot(normed[...], column_block(held, b)).astype(BF)
    copies.store(joined, joined_ref)
    for p in range(passes):
        rows = slice(p * TOK, (p + 1) * TOK)
        mixed_part = attend(
            joined[rows, 0:D], joined[rows, D : 2 * D], joined[rows, 2 * D : 3 * D], bias, probs, p * HEADS
        )
        heads = pl.ds(p * HEADS, HEADS)
        copies.store(probs.at[heads], probs_ref.at[heads])
        mixed[rows] = mixed_part
        out[rows] = inputs[p][...].astype(F32) + dot(mixed_part, column_block(held, 3))
    copies.store(out, out_ref)
    copies.store(mixed, mixed_ref)


def norm_table(copies, place, pieces, gains, held):
    loads = [
        copies.load(pieces[2 * k].at[:, :, pl.ds(64, 16)], held.at[k]) for k in range(2)
    ]

    def compute():
        for load in loads:
            load.arrive()
        for y in range(2):
            where = jnp.where(place[1] == y, 0, 1)
            for z in range(4):
                for core in range(2):
                    spot = 4 * z + 2 * y + core
                    row = held[where, z, core]
                    gains[:, spot * BLOCK : (spot + 1) * BLOCK] = row[:, 0:BLOCK].astype(F32)

    return compute


def self_forward_kernel(decoder, encoder, me_ref, src_lengths, tgt_lengths, given, *refs):
    taken, refs = refs[:3], refs[3:]
    pieces, refs = refs[: decoder.pieces], refs[decoder.pieces :]
    more, refs = refs[: encoder.pieces], refs[encoder.pieces :]
    outs, gains, scratch, (held, held_enc, held_norm, *come, sems) = refs[:10], refs[10], refs[11:21], refs[21:]
    copies = Copies(sems)
    table = norm_table(copies, me_ref, pieces, gains, held_norm) if decoder.pieces > 1 else None
    inputs = [copies.load(taken[p], come[p]) for p in range(3)]
    loads = copies.fetch(me_ref, pieces, decoder, held)
    loads_enc = copies.fetch(me_ref, more, encoder, held_enc)
    bias = mask_bias(tgt_lengths, tgt_lengths)
    if table:
        table()
    else:
        gains[...] = given[...]
    self_forward_part(copies, 4, gains, bias, inputs[:2], loads, held, scratch[:5], outs[:5])
    bias = mask_bias(src_lengths, src_lengths)
    self_forward_part(copies, 0, gains, bias, inputs[2:], loads_enc, held_enc, scratch[5:], outs[5:])
    copies.finish()


def self_back_kernel(passes, row, more, layout, me_ref, gains, *refs):
    others, refs = refs[:more], refs[more:]
    inputs, refs = refs[:passes], refs[passes:]
    taken, refs = refs[:5], refs[5:]
    pieces, refs = refs[: layout.pieces], refs[layout.pieces :]
    grad_in_ref, norm_ref, *refs = refs
    outs, refs = refs[: layout.made], refs[layout.made :]
    grad_in, held, made, back, grad_out, normed, joined, probs, mixed, *come, sems = refs
    copies = Copies(sems)
    grad_out = copies.load(taken[0], grad_out)
    mixed = copies.load(taken[4], mixed)
    loads = copies.fetch(me_ref, pieces, layout, held)
    probs = [
        copies.load(taken[3].at[pl.ds(p * HEADS, HEADS)], probs.at[pl.ds(p * HEADS, HEADS)])
        for p in range(passes)
    ]
    joined = copies.load(taken[2], joined)
    normed = copies.load(taken[1], normed)
    inputs = [copies.load(inputs[p], come[p]) for p in range(passes)]
    grad_low = grad_out[...].astype(BF)
    put_block(made, 3, dot_tn(mixed[...], grad_low))
    copies.deliver(me_ref, made, layout, outs, 3)
    loads[1].arrive()
    grad_mixed = dot_nt(grad_low, column_block(held, 3)).astype(BF)
    for p in range(passes):
        rows = slice(p * TOK, (p + 1) * TOK)
        grads = attend_back(
            joined[rows, 0:D],
            joined[rows, D : 2 * D],
            joined[rows, 2 * D : 3 * D],
            probs[p].arrive(),
            0,
            grad_mixed[rows],
        )
        for b in range(3):
            back[rows, b * D : (b + 1) * D] = grads[b].astype(BF)
    loads[0].arrive()
    for b in range(3):
        part = back[:, b * D : (b + 1) * D]
        put_block(made, b, dot_tn(normed[...], part))
        copies.deliver(me_ref, made, layout, outs, b)
    copies.deliver(me_ref, made, layout, outs, 4)
    grad_normed = None
    for b in range(3):
        step = dot_nt(back[:, b * D : (b + 1) * D], column_block(held, b))
        grad_normed = step if grad_normed is None else grad_normed + step
    units = [normed_of(inputs[p][...].astype(F32)) for p in range(passes)]
    unit = jnp.concatenate([u[0] for u in units], axis=0)
    inverse = jnp.concatenate([u[1] for u in units], axis=0)
    if more:
        norm_ref[...] = jnp.zeros(norm_ref.shape, F32)
        for k, other in enumerate(others):
            norm_ref[2 * k + 2 : 2 * k + 4] = other[...]
    grad = norm_back(unit, inverse, gains[row : row + 1], grad_normed, norm_ref)
    grad_in[...] = grad_out[0:TOK] + grad[0:TOK]
    copies.store(grad_in, grad_in_ref)
    copies.finish()


GELU_SCALE = 0.7978845608028654
GELU_CUBE = 0.044715


def gelu_both(up):
    square = up * up
    bent = jnp.tanh(GELU_SCALE * up * (1.0 + GELU_CUBE * square))
    half = 0.5 * (1.0 + bent)
    slope = half + 0.5 * up * (1.0 - bent * bent) * (
        GELU_SCALE * (1.0 + (3.0 * GELU_CUBE) * square)
    )
    return up * half, slope


def ffn_grads(copies, place, layout, outs, gain, hidden, grad_low, normed, active, slope, norm_ref, held, made):
    for z in range(4):
        product = dot_tn(active[:, z * D : (z + 1) * D], grad_low)
        made[z, :, 4 * BLOCK : 8 * BLOCK] = product.astype(BF).reshape(4, 4 * BLOCK, D)
    copies.deliver(place, made, layout, outs, 2)
    copies.deliver(place, made, layout, outs, 3)
    grad_normed = None
    for b in range(4):
        cols = slice(b * D, (b + 1) * D)
        grad_active = dot_nt(grad_low, row_block(held, b))
        grad_up = (slope[:, cols].astype(F32) * grad_active).astype(BF)
        put_block(made, b, dot_tn(normed[...], grad_up))
        if b % 2 == 1:
            copies.deliver(place, made, layout, outs, b // 2)
        step = dot_nt(grad_up, column_block(held, b))
        grad_normed = step if grad_normed is None else grad_normed + step
    copies.deliver(place, made, layout, outs, 4)
    unit, inverse = normed_of(hidden)
    return norm_back(unit, inverse, gain, grad_normed, norm_ref)


def ffn_back_kernel(row, layout, me_ref, gains, *refs):
    taken, refs = refs[:5], refs[5:]
    pieces, refs = refs[: layout.pieces], refs[layout.pieces :]
    grad_in_ref, norm_ref, *refs = refs
    outs, refs = refs[: layout.made], refs[layout.made :]
    grad_in, held, made, hidden, grad_out, normed, active, slope, sems = refs
    copies = Copies(sems)
    grad_out = copies.load(taken[1], grad_out)
    active = copies.load(taken[3], active)
    loads = copies.fetch(me_ref, pieces, layout, held)
    slope = copies.load(taken[4], slope)
    normed = copies.load(taken[2], normed)
    hidden = copies.load(taken[0], hidden)
    grad_low = grad_out[...].astype(BF)
    active = active.arrive()
    for load in loads:
        load.arrive()
    hidden.arrive()
    grad = ffn_grads(
        copies, me_ref, layout, outs, gains[row : row + 1], hidden[...], grad_low, normed, active, slope, norm_ref, held, made
    )
    grad_in[...] = grad_out[...] + grad
    copies.store(grad_in, grad_in_ref)
    copies.finish()


def second_kernel(encoder, cross, me_ref, src_lengths, tgt_lengths, gains, *refs):
    taken, whole, refs = refs[:2], refs[2:4], refs[4:]
    sent, made, (held_enc, held_cross, hidden_enc, hidden_one, sems) = refs[:10], refs[10:20], refs[20:]
    normed_enc, active_enc, slope_enc, memory, normed, query, pair, probs, mixed, hidden = made
    copies = Copies(sems)
    hidden_enc = copies.load(taken[0], hidden_enc)
    loads_enc = copies.fetch(me_ref, whole[:1], encoder, held_enc)
    hidden_one = copies.load(taken[1], hidden_one)
    loads_cross = copies.fetch(me_ref, whole[1:], cross, held_cross)

    unit, unused = normed_of(hidden_enc[...])
    normed_enc[...] = (unit * gains[2:3] + gains[3:4]).astype(BF)
    copies.store(normed_enc, sent[0])
    unit, unused = normed_of(hidden_one[...])
    normed[...] = (unit * gains[6:7] + gains[7:8]).astype(BF)
    copies.store(normed, sent[4])
    loads_enc[0].arrive()
    for b in range(4):
        cols = slice(b * D, (b + 1) * D)
        grown, bent = gelu_both(dot(normed_enc[...], column_block(held_enc, b)))
        active_enc[:, cols] = grown.astype(BF)
        slope_enc[:, cols] = bent.astype(BF)
    copies.store(active_enc, sent[1])
    copies.store(slope_enc, sent[2])
    loads_enc[1].arrive()
    total = hidden_enc[...]
    for z in range(4):
        total = total + dot(active_enc[:, z * D : (z + 1) * D], row_block(held_enc, z))
    memory[...] = total.astype(BF)
    copies.store(memory, sent[3])

    loads_cross[0].arrive()
    query[...] = dot(normed[...], column_block(held_cross, 0)).astype(BF)
    copies.store(query, sent[5])
    pair[:, 0:D] = dot(memory[...], column_block(held_cross, 1)).astype(BF)
    loads_cross[1].arrive()
    pair[:, D : 2 * D] = dot(memory[...], column_block(held_cross, 2)).astype(BF)
    copies.store(pair, sent[6])
    bias = mask_bias(src_lengths, tgt_lengths)
    for p in range(2):
        rows = slice(p * TOK, (p + 1) * TOK)
        part = attend(query[rows], pair[:, 0:D], pair[:, D : 2 * D], bias, probs, p * HEADS)
        heads = pl.ds(p * HEADS, HEADS)
        copies.store(probs.at[heads], sent[7].at[heads])
        mixed[rows] = part
        hidden[rows] = hidden_one[rows] + dot(part, column_block(held_cross, 3))
    copies.store(mixed, sent[8])
    copies.store(hidden, sent[9])
    copies.finish()


def middle_kernel(cross, decoder, me_ref, gains, *refs):
    taken, whole, refs = refs[:10], refs[10:11], refs[11:]
    pieces, refs = refs[: decoder.pieces], refs[decoder.pieces :]
    norm_ffn, norm_cross, *refs = refs
    sent, refs = refs[:5], refs[5:]
    come, refs = refs[:10], refs[10:]
    held_cross, held, made_cross, made, first_out, second_out, grad_memory, grad_one, *refs = refs
    normed_two, active, slope, grad_two, back, sems = refs
    copies = Copies(sems)
    hidden = copies.load(taken[0], come[0])
    loads = copies.fetch(me_ref, pieces, decoder, held)
    cots = [copies.load(taken[k], come[k]) for k in (1, 2)]
    loads_cross = copies.fetch(me_ref, whole, cross, held_cross)
    mixed, probs, query, pair, normed, memory, hidden_one = (
        copies.load(taken[k], come[k]) for k in range(3, 10)
    )

    unit, unused = normed_of(hidden[...])
    normed_two[...] = (unit * gains[8:9] + gains[9:10]).astype(BF)
    loads[0].arrive()
    for b in range(4):
        cols = slice(b * D, (b + 1) * D)
        grown, bent = gelu_both(dot(normed_two[...], column_block(held, b)))
        active[:, cols] = grown.astype(BF)
        slope[:, cols] = bent.astype(BF)
    loads[1].arrive()
    total = hidden[...]
    for z in range(4):
        total = total + dot(active[:, z * D : (z + 1) * D], row_block(held, z))
    first_out[...] = total[0:TOK].astype(BF)
    second_out[...] = total[TOK:].astype(BF)
    copies.store(first_out, sent[0])
    copies.store(second_out, sent[1])
    grad_low = jnp.concatenate([cots[0][...], cots[1][...]], axis=0)
    grad = ffn_grads(
        copies, me_ref, decoder, sent[4:], gains[8:9], hidden[...], grad_low, normed_two, active, slope, norm_ffn, held, made
    )
    grad_two[...] = grad_low.astype(F32) + grad

    grad_low = grad_two[...].astype(BF)
    put_block(made_cross, 3, dot_tn(mixed[...], grad_low))
    copies.deliver(me_ref, made_cross, cross, sent[4:], 3)
    loads_cross[1].arrive()
    grad_mixed = dot_nt(grad_low, column_block(held_cross, 3)).astype(BF)
    grad_key = grad_value = None
    probs = probs.arrive()
    for p in range(2):
        rows = slice(p * TOK, (p + 1) * TOK)
        grads = attend_back(
            query[rows], pair[:, 0:D], pair[:, D : 2 * D], probs, p * HEADS, grad_mixed[rows]
        )
        back[rows] = grads[0].astype(BF)
        grad_key = grads[1] if grad_key is None else grad_key + grads[1]
        grad_value = grads[2] if grad_value is None else grad_value + grads[2]
    grad_key = grad_key.astype(BF)
    grad_value = grad_value.astype(BF)
    for b, (left, right) in enumerate(
        ((normed[...], back[...]), (memory[...], grad_key), (memory[...], grad_value))
    ):
        put_block(made_cross, b, dot_tn(left, right))
        copies.deliver(me_ref, made_cross, cross, sent[4:], b)
    loads_cross[0].arrive()
    grad_memory[...] = dot_nt(grad_key, column_block(held_cross, 1)) + dot_nt(
        grad_value, column_block(held_cross, 2)
    )
    copies.store(grad_memory, sent[2])
    grad_normed = dot_nt(back[...], column_block(held_cross, 0))
    unit, inverse = normed_of(hidden_one[...])
    grad = norm_back(unit, inverse, gains[6:7], grad_normed, norm_cross)
    grad_one[...] = grad_two[...] + grad
    copies.store(grad_one, sent[3])
    copies.finish()


ANY = pl.BlockSpec(memory_space=pl.ANY)
HB = pl.BlockSpec(memory_space=pltpu.HBM)
VM = pl.BlockSpec(memory_space=pltpu.VMEM)
SM = pl.BlockSpec(memory_space=pltpu.SMEM)


def held_of(blocks):
    return pltpu.VMEM((4, 4, blocks * BLOCK, D), BF)


def made_of(layout, blocks):
    if layout.made == 1:
        return [jax.ShapeDtypeStruct((4, 4, layout.made_rows, D), BF)]
    return [jax.ShapeDtypeStruct((2, 2, 4, 2, blocks * BLOCK // 4, D), BF)] * 2


def shape(rows, cols, dtype):
    return jax.ShapeDtypeStruct((rows, cols), dtype)


class Order:
    def __init__(self):
        self.token = jnp.zeros((8, 128), F32)

    def tie(self, value):
        return self.tie_all([value])[0]

    def tie_all(self, values):
        arrays = list(values) + [self.token]
        *values, self.token = pl.pallas_call(
            nothing_kernel,
            name="tie",
            out_shape=[jax.ShapeDtypeStruct(x.shape, x.dtype) for x in arrays],
            in_specs=[HB] * len(arrays),
            out_specs=[HB] * len(arrays),
            input_output_aliases={k: k for k in range(len(arrays))},
            compiler_params=pltpu.CompilerParams(vmem_limit_bytes=VMEM_LIMIT),
        )(*arrays)
        return values


def nothing_kernel(*refs):
    pass


def call(order, body, name, in_specs, out_shape, out_specs, scratch, operands, micros, grid=None, inplace=()):
    count, more, outs = len(operands), len(inplace) + 1, len(out_shape)

    def ordered(*refs):
        body(*refs[:count], *refs[count + more : count + more + outs], *refs[count + more + outs + 1 :])

    aliases = {count + k: out for k, (unused, out) in enumerate(inplace)}
    aliases[count + len(inplace)] = outs
    *results, order.token = pl.pallas_call(
        ordered,
        name=name,
        out_shape=out_shape + [jax.ShapeDtypeStruct(order.token.shape, order.token.dtype)],
        in_specs=in_specs + [HB] * more,
        out_specs=out_specs + [HB],
        input_output_aliases=aliases,
        scratch_shapes=scratch,
        compiler_params=pltpu.CompilerParams(vmem_limit_bytes=VMEM_LIMIT),
        cost_estimate=pl.CostEstimate(
            flops=int((micros + 0.01) * COST), bytes_accessed=0, transcendentals=0
        ),
        **({} if grid is None else {"grid": grid}),
    )(*operands, *(array for array, unused in inplace), order.token)
    return results


def vmem(rows, cols, dtype):
    return pltpu.VMEM((rows, cols), dtype)


def probs_of(count, scratch=False):
    dims = (count * HEADS, TOK, TOK)
    return pltpu.VMEM(dims, BF) if scratch else jax.ShapeDtypeStruct(dims, BF)


SEMS = pltpu.SemaphoreType.DMA((64,))


def arrays(items):
    return [jax.ShapeDtypeStruct(dims, dtype) for dims, dtype in items]


def buffers(items):
    return [pltpu.VMEM(dims, dtype) for dims, dtype in items]


def self_kept(count):
    rows = count * TOK
    return [
        ((rows, D), F32),
        ((rows, D), BF),
        ((rows, 3 * D), BF),
        ((count * HEADS, TOK, TOK), BF),
        ((rows, D), BF),
    ]


def self_forward(order, me, src_lengths, tgt_lengths, gains, inputs, decoder, encoder):
    kept = self_kept(2) + self_kept(1)
    results = call(
        order,
        functools.partial(self_forward_kernel, decoder[0], encoder[0]),
        "self_forward",
        [SM, SM, SM, ANY if decoder[0].pieces > 1 else VM] + [HB] * 3 + [ANY] * (decoder[0].pieces + encoder[0].pieces),
        arrays(kept) + [shape(16, D, F32)],
        [HB] * 10 + [VM],
        buffers(kept)
        + [held_of(4), held_of(4), pltpu.VMEM((2, 4, 2, 16, D), BF)]
        + [vmem(TOK, D, BF)] * 3
        + [SEMS],
        (me, src_lengths, tgt_lengths, gains, *inputs, *decoder[1], *encoder[1]),
        12,
    )
    return results[:5], results[5:10], results[10]


def second(order, me, src_lengths, tgt_lengths, gains, hidden_enc, hidden_one, encoder, cross):
    rows = 2 * TOK
    kept = [
        ((TOK, D), BF),
        ((TOK, FF), BF),
        ((TOK, FF), BF),
        ((TOK, D), BF),
        ((rows, D), BF),
        ((rows, D), BF),
        ((TOK, 2 * D), BF),
        ((2 * HEADS, TOK, TOK), BF),
        ((rows, D), BF),
        ((rows, D), F32),
    ]
    results = call(
        order,
        functools.partial(second_kernel, encoder[0], cross[0]),
        "second",
        [SM, SM, SM, VM] + [HB] * 2 + [ANY] * 2,
        arrays(kept),
        [HB] * 10,
        buffers(kept) + [held_of(8), held_of(4), vmem(TOK, D, F32), vmem(rows, D, F32), SEMS],
        (me, src_lengths, tgt_lengths, gains, hidden_enc, hidden_one, encoder[1][0], cross[1][0]),
        13,
    )
    return results[:3], results[3:]


def self_back(order, row, me, gains, inputs, grad_out, kept, pieces, others=()):
    count = len(inputs)
    rows = count * TOK
    return call(
        order,
        functools.partial(self_back_kernel, count, row, len(others), pieces[0]),
        "self_back",
        [SM, VM] + [VM] * len(others) + [HB] * count + [HB] * 5 + [ANY] * pieces[0].pieces,
        [shape(TOK, D, F32), shape(16 if others else 2, D, F32)] + made_of(pieces[0], 4),
        [HB, VM] + [HB] * pieces[0].made,
        [
            vmem(TOK, D, F32),
            held_of(4),
            held_of(4),
            vmem(rows, 3 * D, BF),
            vmem(rows, D, F32),
            vmem(rows, D, BF),
            vmem(rows, 3 * D, BF),
            probs_of(count, True),
            vmem(rows, D, BF),
        ]
        + [vmem(TOK, D, BF)] * count
        + [SEMS],
        (me, gains, *others, *inputs, grad_out, *kept, *pieces[1]),
        5.8 + 3.4 * count,
    )


def ffn_back(order, row, me, gains, hidden, grad_out, kept, pieces):
    return call(
        order,
        functools.partial(ffn_back_kernel, row, pieces[0]),
        "ffn_back",
        [SM, VM] + [HB] * 5 + [ANY] * pieces[0].pieces,
        [shape(TOK, D, F32), shape(2, D, F32)] + made_of(pieces[0], 8),
        [HB, VM] + [HB] * pieces[0].made,
        [
            vmem(TOK, D, F32),
            held_of(8),
            held_of(8),
            vmem(TOK, D, F32),
            vmem(TOK, D, F32),
            vmem(TOK, D, BF),
            vmem(TOK, FF, BF),
            vmem(TOK, FF, BF),
            SEMS,
        ],
        (me, gains, hidden, grad_out, *kept, *pieces[1]),
        10.2,
    )


def middle(order, me, gains, hidden_one, kept, cots, cross, decoder):
    rows = 2 * TOK
    memory, normed, query, pair, probs, mixed, hidden = kept
    taken = [hidden, *cots, mixed, probs, query, pair, normed, memory, hidden_one]
    sent = [((TOK, D), BF), ((TOK, D), BF), ((TOK, D), F32), ((rows, D), F32)]
    return call(
        order,
        functools.partial(middle_kernel, cross[0], decoder[0]),
        "middle",
        [SM, VM] + [HB] * 10 + [ANY] * (1 + decoder[0].pieces),
        [shape(2, D, F32)] * 2 + arrays(sent + [((4, 4, 384, D), BF)]),
        [VM] * 2 + [HB] * 5,
        buffers([(x.shape, x.dtype) for x in taken])
        + [held_of(4), held_of(8), held_of(4), held_of(8)]
        + buffers(sent)
        + [
            vmem(rows, D, BF),
            vmem(rows, FF, BF),
            vmem(rows, FF, BF),
            vmem(rows, D, F32),
            vmem(rows, D, BF),
            SEMS,
        ],
        (me, gains, *taken, cross[1][0], *decoder[1]),
        25,
    )


AXIS = "fsdp"
BOTH = ("dp", "fsdp")
SHARDS = 16


def route(target):
    pairs = []
    for i in range(2 * SHARDS):
        dp, z, y, core = target(i // 16, (i // 4) % 4, (i // 2) % 2, i % 2)
        pairs.append((i, dp * 16 + (z % 4) * 4 + y * 2 + core))
    return pairs


def to_core(x):
    return lax.ppermute(x, BOTH, route(lambda dp, z, y, core: (dp, z, y, 1 - core)))


def to_z(x, step):
    return lax.ppermute(x, BOTH, route(lambda dp, z, y, core: (dp, z + step, y, core)))


def to_z_pair(x, step):
    return lax.ppermute(x, BOTH, route(lambda dp, z, y, core: (dp, z ^ step, y, core)))


def to_y(x):
    return lax.ppermute(x, BOTH, route(lambda dp, z, y, core: (dp, z, 1 - y, core)))


def to_dp(x):
    return lax.ppermute(x, BOTH, route(lambda dp, z, y, core: (1 - dp, z, y, core)))


def to_yx(x):
    return lax.ppermute(
        x, BOTH, route(lambda dp, z, y, core: (dp, z, y ^ 1, core) if core == 0 else (dp ^ 1, z, y, core))
    )


def to_xy(x):
    return lax.ppermute(
        x, BOTH, route(lambda dp, z, y, core: (dp ^ 1, z, y, core) if core == 0 else (dp, z, y ^ 1, core))
    )


def blocks_of(shard):
    rows, cols = shard.shape
    split = shard.reshape(rows // BLOCK, BLOCK, cols // D, D)
    return split.transpose(2, 0, 1, 3).reshape(-1, BLOCK, D)


def shard_of(blocks, cols):
    wide = blocks.reshape(cols // D, -1, D)
    return wide.transpose(1, 0, 2).reshape(-1, cols)


def small(order, body, name, out, operands, scratch=(), in_specs=None, out_specs=None, micros=0, grid=None):
    return call(
        order,
        body,
        name,
        in_specs if in_specs is not None else [VM] * len(operands),
        [jax.ShapeDtypeStruct(dims, dtype) for dims, dtype in out],
        out_specs if out_specs is not None else [VM] * len(out),
        list(scratch),
        operands,
        micros,
        grid,
    )


def pack_kernel(place, *refs):
    weights, (one, two, three, norms) = refs[:15], refs[15:]
    self_in, self_out, enc_in, enc_out, enc_ffn_in, enc_ffn_out = weights[:6]
    cross_q, cross_kv, cross_out, ffn_in, ffn_out = weights[6:11]
    for half in range(2):

        @pl.when(place[2] == half)
        def _():
            for k in range(2):
                quarter = 2 * half + k
                cols = slice(quarter * D, (quarter + 1) * D)
                one[k, 0:32] = self_out[...] if quarter == 3 else self_in[:, cols]
                one[k, 32:64] = enc_out[...] if quarter == 3 else enc_in[:, cols]
                for j in range(2):
                    block = 2 * quarter + j
                    rows = slice(j * BLOCK, (j + 1) * BLOCK)
                    cols = slice(block * D, (block + 1) * D)
                    part = slice((block - 4) * BLOCK, (block - 3) * BLOCK)
                    three[k, rows] = ffn_in[:, cols] if block < 4 else ffn_out[part]

    for block in range(4):
        rows = slice(block * BLOCK, (block + 1) * BLOCK)
        two[rows] = enc_ffn_in[:, block * D : (block + 1) * D]
    two[128:256] = enc_ffn_out[...]
    two[256:288] = cross_q[...]
    two[288:320] = cross_kv[:, 0:D]
    two[320:352] = cross_kv[:, D : 2 * D]
    two[352:384] = cross_out[...]
    norms[...] = jnp.zeros(norms.shape, F32)
    row = 0
    for gain, bias in (weights[11:13], weights[13:15]):
        for k in range(gain.shape[0]):
            norms[row : row + 1, 0:BLOCK] = gain[k : k + 1].astype(F32)
            norms[row + 1 : row + 2, 0:BLOCK] = bias[k : k + 1].astype(F32)
            row += 2
    for k in range(2):
        one[k, 64:80] = norms[...].astype(BF)


def pack(order, place, weights, norms):
    return small(
        order,
        pack_kernel,
        "pack",
        [((2, 80, D), BF), ((384, D), BF), ((2, 64, D), BF)],
        (place, *weights, *norms),
        [pltpu.VMEM((16, D), F32)],
        in_specs=[SM] + [VM] * 15,
    )


def pair_kernel(place, *refs):
    core = place[3]
    for k in range(2):
        mine, near, pair = refs[2 * k], refs[2 * k + 1], refs[4 + k]
        pair[core] = mine[core]
        pair[1 - core] = near[core]


def pair_up(order, place, mine, near):
    operands = [x for both in zip(mine, near) for x in both]
    return small(
        order,
        pair_kernel,
        "pair_up",
        [(x.shape, x.dtype) for x in mine],
        (place, *operands),
        in_specs=[SM] + [VM] * 4,
    )


def stack_kernel(place, *refs):
    parts, (out, held, sems) = refs[:-3], refs[-3:]
    count = len(parts)
    loads = [pltpu.make_async_copy(parts[d], held.at[d], sems.at[d]) for d in range(count)]
    stores = [
        pltpu.make_async_copy(held.at[d], out.at[(place[0] + (4 - d)) & 3], sems.at[count + d])
        for d in range(count)
    ]
    for copy in loads:
        copy.start()
    for d in range(count):
        loads[d].wait()
        stores[d].start()
    wait_all(stores)


def stack(order, place, parts):
    dims = (len(parts),) + parts[0].shape
    dtype = parts[0].dtype
    return small(
        order,
        stack_kernel,
        "stack",
        [(dims, dtype)],
        (place, *parts),
        [pltpu.VMEM(dims, dtype), pltpu.SemaphoreType.DMA((2 * len(parts),))],
        [SM] + [ANY] * len(parts),
        [ANY],
    )[0]


class Gather:
    def __init__(self, order, pair):
        self.order, self.pair = order, pair

    def along_z(self):
        pair = self.order.tie(self.pair)
        self.parts = [pair] + [to_z(pair, d) for d in (1, 2, 3)]

    def lined(self, place):
        self.line = stack(self.order, place, self.parts)

    def first_cross(self):
        line = self.order.tie(self.line)
        self.own = [line, to_dp(line), to_y(line)]
        self.near = []

    def crossed(self, others=()):
        arrived = self.order.tie_all(self.own[1:3] + list(others[1:]))
        self.own[1:3] = arrived[:2]
        if others:
            others[1:] = arrived[2:]

    def second_cross(self):
        self.own.append(to_dp(self.own[2]))

    def share(self, k):
        self.near.append(self.order.tie(to_core(self.own[k])))

    def done(self):
        last = self.order.tie(self.own[3])
        self.own = self.own[:3] + [last]
        self.near.append(self.order.tie(to_core(last)))
        self.pieces = tuple(self.own + self.near)


def low_sum(*parts):
    total = parts[0].astype(F32)
    for part in parts[1:]:
        total = total + part.astype(F32)
    return total.astype(BF)


def rows_of(parts):
    row = 0
    for k, part in enumerate(parts[::2]):
        yield slice(row, row + part.shape[4]), part, parts[2 * k + 1]
        row += part.shape[4]


def send_block(step, source, target, sems, more):
    def copies():
        for k in range(4):
            yield k, pltpu.make_async_copy(
                source.at[k], target.at[pl.ds(k * source.shape[1], source.shape[1])], sems.at[k]
            )

    last = pltpu.make_async_copy(*more, sems.at[4])
    for k, copy in copies():
        pl.when(step == k)(copy.start)
    pl.when(step == 0)(last.start)

    @pl.when(step == 3)
    def _():
        for unused, copy in copies():
            copy.wait()
        last.wait()


def reduce_first_kernel(norm_own, norm_came, *refs):
    sent, held, norm, sems = refs[-4:]
    step = pl.program_id(0)

    @pl.when(step == 0)
    def _():
        norm[...] = (norm_own[...] + norm_came[...]).astype(BF)

    whole = held.shape[1] // 4
    for rows, own, came in rows_of(refs[:-4]):
        for second in range(2):
            for core in range(2):
                row = (2 * second + core) * whole + rows.start
                held[step, row : row + rows.stop - rows.start] = (
                    own[0, second, 0, core] + came[0, second, 0, core]
                )
    send_block(step, held, sent, sems, (norm, sent.at[pl.ds(16 * whole, 16)]))


def reduce_second_kernel(norm_own, norm_came, came_first, *refs):
    sent, held, norm, sems = refs[-4:]
    step = pl.program_id(0)

    @pl.when(step == 0)
    def _():
        norm[...] = (norm_own[...].astype(F32) + norm_came[...].astype(F32)).astype(BF)

    whole = held.shape[1] // 2
    for rows, own, came in rows_of(refs[:-4]):
        for core in range(2):
            span = slice(core * whole + rows.start, core * whole + rows.stop)
            held[step, span] = low_sum(own[0, 0, 0, core], came[0, 0, 0, core], came_first[span])
    send_block(step, held, sent, sems, (norm, sent.at[pl.ds(8 * whole, 16)]))


def reduce_third_kernel(norm_own, norm_came, place, came_first, came_second, *refs):
    outs = refs[-4:]
    norm = (norm_own[...].astype(F32) + norm_came[...].astype(F32)).astype(BF)
    whole = (outs[0].shape[0] - 16) // 2
    for d in range(4):
        z = (place[0] + d) & 3
        outs[d][2 * whole :] = norm
        for rows, own, came in rows_of(refs[:-4]):
            for core in range(2):
                span = slice(core * whole + rows.start, core * whole + rows.stop)
                size = rows.stop - rows.start
                first = pl.multiple_of(z * 4 * whole + span.start, 16)
                second = pl.multiple_of(z * 2 * whole + span.start, 16)
                outs[d][span] = low_sum(
                    own[0, 0, z, core],
                    came[0, 0, z, core],
                    came_first[pl.ds(first, size)],
                    came_second[pl.ds(second, size)],
                )


def reduce_fourth_kernel(a, b, c, d, out, norm):
    rows = out.shape[1]
    for core in range(2):
        span = slice(core * rows, (core + 1) * rows)
        out[core] = low_sum(a[span], b[span], c[span], d[span])
    total = a[2 * rows :].astype(F32)
    for part in (b, c, d):
        total = total + part[2 * rows :].astype(F32)
    norm[...] = total


class Reduce:
    def __init__(self, order):
        self.order, self.own, self.came = order, [], []

    def add(self, own, other):
        self.own.append(own)
        self.came.append(to_core(self.order.tie(other)))

    def arrive(self):
        self.came[-1] = self.order.tie(self.came[-1])

    def start_norm(self, norm):
        self.norm = self.order.tie(norm)
        self.norm_came = to_core(self.norm)

    def run(self, body, name, dims, operands, in_specs, part_spec, out_specs=None, scratch=(), grid=(4,)):
        parts = [x for both in zip(self.own, self.came) for x in both]
        specs = [pl.BlockSpec(part_spec[0] + (part.shape[4], D), part_spec[1]) for part in parts]
        sent = small(
            self.order,
            body,
            name,
            [(item, BF) for item in dims],
            operands + parts,
            scratch,
            in_specs=in_specs + specs,
            out_specs=out_specs or [HB] * len(dims),
            grid=grid,
        )
        return [self.order.tie(x) for x in sent]

    def first(self):
        rows = self.rows = sum(own.shape[4] for own in self.own)
        norm_spec = pl.BlockSpec((16, D), lambda i: (0, 0))
        (self.first_sent,) = self.run(
            reduce_first_kernel,
            "reduce_first",
            [(16 * rows + 16, D)],
            [self.norm, self.norm_came],
            [norm_spec] * 2,
            ((1, 2, 1, 2), lambda i: (1, 0, i, 0, 0, 0)),
            scratch=buffers([((4, 4 * rows, D), BF), ((16, D), BF)]) + [pltpu.SemaphoreType.DMA((5,))],
        )
        self.first_came = to_yx(self.first_sent)

    def second(self):
        rows = self.rows
        norm_spec = pl.BlockSpec((16, D), lambda i: (rows, 0))
        (self.second_sent,) = self.run(
            reduce_second_kernel,
            "reduce_second",
            [(8 * rows + 16, D)],
            [self.first_sent, self.first_came, self.first_came],
            [norm_spec] * 2 + [pl.BlockSpec((2 * rows, D), lambda i: (2 * i + 1, 0))],
            ((1, 1, 1, 2), lambda i: (0, 1, i, 0, 0, 0)),
            scratch=buffers([((4, 2 * rows, D), BF), ((16, D), BF)]) + [pltpu.SemaphoreType.DMA((5,))],
        )
        self.second_came = to_xy(self.second_sent)

    def third(self, place):
        rows = self.rows
        norm_spec = pl.BlockSpec((16, D), lambda i: (rows // 2, 0))
        parts = self.run(
            reduce_third_kernel,
            "reduce_third",
            [(2 * rows + 16, D)] * 4,
            [self.second_sent, self.second_came, place, self.first_came, self.second_came],
            [norm_spec] * 2
            + [SM]
            + [pl.BlockSpec(x.shape, lambda i: (0, 0)) for x in (self.first_came, self.second_came)],
            ((1, 1, 4, 2), lambda i: (0, 0, 0, 0, 0, 0)),
            [pl.BlockSpec((2 * rows + 16, D), lambda i: (0, 0))] * 4,
            grid=(1,),
        )
        self.lines = [parts[0]] + [to_z(parts[d], d) for d in (1, 2, 3)]

    def fourth(self):
        total, self.norm = small(
            self.order,
            reduce_fourth_kernel,
            "reduce_fourth",
            [((2, self.rows, D), BF), ((16, D), F32)],
            self.lines,
        )
        total = self.order.tie(total)
        self.ends = [total, to_dp(total), to_core(total)]

    def last(self):
        near = self.order.tie(self.ends[2])
        came = self.order.tie(self.ends[1])
        self.ends = [self.ends[0], came, near, to_core(came)]


def quarter_of(place, ends, quarter, rows):
    core = place[3]
    half, which = quarter >> 1, quarter & 1
    first = jnp.where(place[3] == which, ends[0][core, rows], ends[2][core, rows].astype(BF))
    second = jnp.where(place[3] == which, ends[1][core, rows], ends[3][core, rows])
    return jnp.where(place[2] == half, first, second).astype(F32)


def unpack_kernel(layout, place, *refs):
    ends, outs = refs[:4], refs[4:]
    first = 0
    for kind, row in layout:
        for quarter in range(4):
            if kind == "ffn":
                for j in range(2):
                    block = 2 * quarter + j
                    rows = slice(row + j * BLOCK, row + (j + 1) * BLOCK)
                    value = quarter_of(place, ends, quarter, rows)
                    if block < 4:
                        outs[first][:, block * D : (block + 1) * D] = value
                    else:
                        outs[first + 1][(block - 4) * BLOCK : (block - 3) * BLOCK] = value
            else:
                value = quarter_of(place, ends, quarter, slice(row, row + BLOCK))
                if kind == "attn":
                    if quarter < 3:
                        outs[first][:, quarter * D : (quarter + 1) * D] = value
                    else:
                        outs[first + 1][...] = value
                elif quarter in (1, 2):
                    outs[first + 1][:, (quarter - 1) * D : quarter * D] = value
                else:
                    outs[first + (quarter + 1) // 2][...] = value
        first += 3 if kind == "cross" else 2


SHARD_SHAPES = {
    "ffn": [((BLOCK, FF), F32), ((4 * BLOCK, D), F32)],
    "attn": [((BLOCK, 3 * D), F32), ((BLOCK, D), F32)],
    "cross": [((BLOCK, D), F32), ((BLOCK, 2 * D), F32), ((BLOCK, D), F32)],
}


def unpack(order, place, ends, layout):
    return small(
        order,
        functools.partial(unpack_kernel, layout),
        "unpack",
        [item for kind, unused in layout for item in SHARD_SHAPES[kind]],
        (place, *ends),
        in_specs=[SM] + [VM] * 4,
    )


def norm_last_kernel(place, total, *outs):
    total = total[...]
    spot = place[0] * 4 + place[1] * 2 + place[3]
    turned = jnp.zeros((16, BLOCK), F32)
    for k in range(SHARDS):
        turned = jnp.where(spot == k, total[:, k * BLOCK : (k + 1) * BLOCK], turned)
    for first, gain, bias in ((0, outs[0], outs[1]), (4, outs[2], outs[3])):
        for k in range(gain.shape[0]):
            gain[k : k + 1] = turned[first + 2 * k : first + 2 * k + 1]
            bias[k : k + 1] = turned[first + 2 * k + 1 : first + 2 * k + 2]


def norm_last(order, place, total):
    return small(
        order,
        norm_last_kernel,
        "norm_last",
        [((2, BLOCK), F32), ((2, BLOCK), F32), ((3, BLOCK), F32), ((3, BLOCK), F32)],
        (place, total),
        in_specs=[SM, VM],
    )


def spread_kernel(own, came, ffn_in, ffn_out, cross_q, cross_kv, cross_out):
    total = own[...].astype(F32) + came[...].astype(F32)
    for block in range(4):
        ffn_in[:, block * D : (block + 1) * D] = total[block * BLOCK : (block + 1) * BLOCK]
    ffn_out[...] = total[128:256]
    cross_q[...] = total[256:288]
    cross_kv[:, 0:D] = total[288:320]
    cross_kv[:, D : 2 * D] = total[320:352]
    cross_out[...] = total[352:384]


def spread(order, own, came):
    return small(
        order,
        spread_kernel,
        "spread",
        SHARD_SHAPES["ffn"] + SHARD_SHAPES["cross"],
        (own, came),
    )


def gather_plain(weights):
    parts = []
    for weight in weights:
        whole = lax.all_gather(weight, AXIS, axis=0, tiled=True)
        parts.append(jax.vmap(blocks_of)(whole.reshape(SHARDS, -1, whole.shape[1])))
    return jnp.concatenate(parts, axis=1).reshape(4, 4, -1, D)


def reduce_plain(made, columns):
    shards = made.reshape(SHARDS, -1, BLOCK, D)
    grads = []
    for first, last, cols in columns:
        whole = jax.vmap(functools.partial(shard_of, cols=cols))(shards[:, first:last])
        whole = whole.reshape(-1, cols).astype(F32)
        part = lax.psum_scatter(whole, AXIS, scatter_dimension=0, tiled=True)
        grads.append(lax.psum(part.astype(BF), "dp").astype(F32))
    return grads


def norm_rows_of(gain_enc, bias_enc, gain_dec, bias_dec):
    rows = []
    for gain, bias in ((gain_enc, bias_enc), (gain_dec, bias_dec)):
        for k in range(gain.shape[0]):
            rows += [gain[k : k + 1], bias[k : k + 1]]
    return jnp.concatenate(rows, axis=0)


ATTN_COLUMNS = ((0, 3, 3 * D), (3, 4, D))
FFN_COLUMNS = ((0, 4, FF), (4, 8, D))
CROSS_COLUMNS = ((0, 1, D), (1, 3, 2 * D), (3, 4, D))


def step(
    custom,
    source,
    first_in,
    second_in,
    cot_first,
    cot_second,
    src_lengths,
    tgt_lengths,
    enc_attn_in,
    enc_attn_out,
    enc_ffn_in,
    enc_ffn_out,
    enc_gain,
    enc_bias,
    dec_self_in,
    dec_self_out,
    dec_cross_q,
    dec_cross_kv,
    dec_cross_out,
    dec_ffn_in,
    dec_ffn_out,
    dec_gain,
    dec_bias,
):
    spot = lax.axis_index(AXIS)
    order = Order()
    group_self = (dec_self_in, dec_self_out)
    group_enc = (enc_attn_in, enc_attn_out)
    group_enc_ffn = (enc_ffn_in, enc_ffn_out)
    group_cross = (dec_cross_q, dec_cross_kv, dec_cross_out)
    group_ffn = (dec_ffn_in, dec_ffn_out)
    if custom:
        place = jnp.stack([spot >> 2, (spot >> 1) & 1, lax.axis_index("dp"), spot & 1]).astype(jnp.int32)
        weights = group_self + group_enc + group_enc_ffn + group_cross + group_ffn
        mine_one, mine_two, mine_three = pack(
            order, place, weights, (enc_gain, enc_bias, dec_gain, dec_bias)
        )
        mine = (mine_one, mine_three)
        pairs = pair_up(order, place, mine, [to_core(x) for x in mine])
        one, three = (Gather(order, pair) for pair in pairs)
        one.along_z()
        one.parts[3] = order.tie(one.parts[3])
        mine_two = order.tie(mine_two)
        whole = lax.all_gather(mine_two, AXIS, axis=0, tiled=True).reshape(4, 4, -1, D)
        one.lined(place)
        one.first_cross()
        three.along_z()
        one.crossed(three.parts)
        one.second_cross()
        three.lined(place)
        three.first_cross()
        for k in range(3):
            one.share(k)
        one.done()
        gains = first_in
        w_self, w_enc = (Layout(0, 8), one.pieces), (Layout(32, 8), one.pieces)
        w_enc_ffn = (Layout(0, 1), (whole,))
        w_cross = (Layout(256, 1, 1, 256, 384), (whole,))
    else:
        place = jnp.zeros((4,), jnp.int32)
        w_self, w_enc, w_enc_ffn = (
            (Layout(0, 1, 1, 0, rows), (gather_plain(group),))
            for group, rows in ((group_self, 128), (group_enc, 128), (group_enc_ffn, 256))
        )
        w_cross = (Layout(0, 1, 1, 256, 384), (gather_plain(group_cross),))
        w_ffn = (Layout(0, 1, 1, 0, 384), (gather_plain(group_ffn),))
        norm_rows = norm_rows_of(enc_gain, enc_bias, dec_gain, dec_bias)
        gains = lax.all_gather(norm_rows, AXIS, axis=1, tiled=True)
        gains = jnp.pad(gains.astype(F32), ((0, 6), (0, 0)))

    (hidden_one, *kept_self), (hidden_enc, *kept_enc), gains = self_forward(
        order, place, src_lengths, tgt_lengths, gains, [first_in, second_in, source], w_self, w_enc
    )
    if custom:
        three.crossed()
        three.second_cross()
        for k in range(3):
            three.share(k)
    kept_enc_ffn, kept_cross = second(
        order, place, src_lengths, tgt_lengths, gains, hidden_enc, hidden_one, w_enc_ffn, w_cross
    )
    if custom:
        three.done()
        w_ffn = (Layout(0, 8, 1, 0, 384), three.pieces)
    norm_ffn, norm_cross, first_out, second_out, grad_memory, grad_one, made = middle(
        order, place, gains, hidden_one, kept_cross, (cot_first, cot_second), w_cross, w_ffn
    )
    if custom:
        scattered = lax.psum_scatter(
            made.reshape(-1, D), AXIS, scatter_dimension=0, tiled=True
        )
    grad_enc, norm_enc_ffn, *made_enc_ffn = ffn_back(
        order, 2, place, gains, hidden_enc, grad_memory, kept_enc_ffn, w_enc_ffn
    )
    if custom:
        red = Reduce(order)
        red.add(*made_enc_ffn)
    grad_first, norm_self, *made_self = self_back(
        order, 4, place, gains, [first_in, second_in], grad_one, kept_self, w_self
    )
    if custom:
        red.arrive()
        red.add(*made_self)
    grad_source, norm_total, *made_enc = self_back(
        order,
        0,
        place,
        gains,
        [source],
        grad_enc,
        kept_enc,
        w_enc,
        (norm_enc_ffn, norm_self, norm_cross, norm_ffn),
    )
    if custom:
        red.arrive()
        red.add(*made_enc)
        red.start_norm(norm_total)
        red.first()
        red.second()
        red.third(place)
        scattered = order.tie(scattered)
        scattered_came = order.tie(to_dp(scattered))
        red.fourth()
        grads_ffn_cross = spread(order, scattered, scattered_came)
        norm_grads = norm_last(order, place, red.norm)
        red.last()
        grads_ffn, grads_cross = grads_ffn_cross[:2], grads_ffn_cross[2:]
        g = unpack(order, place, red.ends, (("ffn", 0), ("attn", 64), ("attn", 96)))
        grads_enc_ffn, grads_self, grads_enc = g[:2], g[2:4], g[4:6]
    else:
        grads_ffn = reduce_plain(made[:, :, 0:256], FFN_COLUMNS)
        grads_cross = reduce_plain(made[:, :, 256:384], CROSS_COLUMNS)
        grads_enc_ffn = reduce_plain(*made_enc_ffn, FFN_COLUMNS)
        grads_self = reduce_plain(*made_self, ATTN_COLUMNS)
        grads_enc = reduce_plain(*made_enc, ATTN_COLUMNS)
        norm_shard = lax.psum_scatter(norm_total, AXIS, scatter_dimension=1, tiled=True)
        norm_shard = lax.psum(norm_shard.astype(BF), "dp").astype(F32)
        norm_grads = (norm_shard[0:4:2], norm_shard[1:4:2], norm_shard[4:10:2], norm_shard[5:10:2])
    return (
        first_out,
        second_out,
        grad_source,
        grad_first,
        *grads_enc,
        *grads_enc_ffn,
        *norm_grads[:2],
        *grads_self,
        *grads_cross,
        *grads_ffn,
        *norm_grads[2:],
    )


def solution(mesh):
    blocked = P(("dp", "fsdp"), None)
    rows = P("fsdp", None)
    columns = P(None, "fsdp")
    custom = mesh.shape["fsdp"] == SHARDS and mesh.shape["dp"] == 2
    return jax.shard_map(
        functools.partial(step, custom),
        mesh=mesh,
        in_specs=(blocked,) * 7 + (rows,) * 4 + (columns,) * 2 + (rows,) * 7 + (columns,) * 2,
        out_specs=(blocked,) * 4 + (rows,) * 4 + (columns,) * 2 + (rows,) * 7 + (columns,) * 2,
        check_vma=False,
    )
```

```python
import functools
import typing

import jax
import jax.numpy as jnp
from jax import lax
from jax.experimental import pallas as pl
from jax.experimental.pallas import tpu as pltpu
from jax.sharding import PartitionSpec as P

D = 512
HEADS = 8
HEAD = 64
TOK = 256
FF = 2048
QUAD = 256
BLOCK = 32
EPSILON = 1e-05
MASKED = -1000000000.0
BF = jnp.bfloat16
F32 = jnp.float32
VMEM_LIMIT = 64 * 1024 * 1024
COST = 1.1e9


class Layout(typing.NamedTuple):
    offset: int
    pieces: int
    made: int = 2
    made_offset: int = 0
    made_rows: int = 0


def dot(left, right):
    return lax.dot_general(left, right, (((1,), (0,)), ((), ())), preferred_element_type=F32)


def dot_nt(left, right):
    return lax.dot_general(left, right, (((1,), (1,)), ((), ())), preferred_element_type=F32)


def dot_tn(left, right):
    return lax.dot_general(left, right, (((0,), (0,)), ((), ())), preferred_element_type=F32)


def wait_all(copies):
    for copy in copies:
        copy.wait()


def column_block(held, index):
    return held[:, :, index * BLOCK : (index + 1) * BLOCK].reshape(D, D)


def row_block(held, index):
    return held[index, :, 4 * BLOCK : 8 * BLOCK].reshape(D, D)


def normed_of(values):
    centre = values - jnp.mean(values, axis=-1, keepdims=True)
    spread = jnp.mean(centre * centre, axis=-1, keepdims=True)
    inverse = lax.rsqrt(spread + EPSILON)
    return centre * inverse, inverse


def norm_back(unit, inverse, gain, grad_normed, norm_ref):
    norm_ref[0:1] = jnp.sum(grad_normed * unit, axis=0, keepdims=True)
    norm_ref[1:2] = jnp.sum(grad_normed, axis=0, keepdims=True)
    grad_unit = grad_normed * gain
    return (
        grad_unit
        - jnp.mean(grad_unit, axis=-1, keepdims=True)
        - unit * jnp.mean(grad_unit * unit, axis=-1, keepdims=True)
    ) * inverse


def mask_bias(key_lengths, query_lengths):
    key_place = lax.broadcasted_iota(jnp.int32, (TOK, 1), 0)
    query_place = lax.broadcasted_iota(jnp.int32, (1, TOK), 1)
    key_ids = jnp.zeros((TOK, 1), jnp.int32)
    query_ids = jnp.zeros((1, TOK), jnp.int32)
    key_end = jnp.int32(0)
    query_end = jnp.int32(0)
    for k in range(key_lengths.shape[1]):
        key_end = key_end + key_lengths[0, k]
        query_end = query_end + query_lengths[0, k]
        key_ids = key_ids + jnp.where(key_place >= key_end, 1, 0)
        query_ids = query_ids + jnp.where(query_place >= query_end, 1, 0)
    return jnp.where(key_ids == query_ids, 0.0, MASKED).astype(F32)


def lane_masks():
    head_of = lax.broadcasted_iota(jnp.int32, (1, QUAD), 1) // HEAD
    return [jnp.where(head_of == h, 1.0, 0.0).astype(BF) for h in range(QUAD // HEAD)]


def attend(queries, keys, values, bias, probs_ref, first):
    masks = lane_masks()
    outs = []
    for g in range(D // QUAD):
        cols = slice(g * QUAD, (g + 1) * QUAD)
        q, k, v = queries[:, cols], keys[:, cols], values[:, cols]
        total = None
        for h in range(QUAD // HEAD):
            scores = dot_nt(k * (masks[h] * (HEAD**-0.5)), q) + bias
            top = jnp.max(scores, axis=0, keepdims=True)
            grown = jnp.exp(scores - top)
            probs = (grown * (1.0 / jnp.sum(grown, axis=0, keepdims=True))).astype(BF)
            probs_ref[first + g * (QUAD // HEAD) + h] = probs
            part = dot_tn(probs, v * masks[h])
            total = part if total is None else total + part
        outs.append(total.astype(BF))
    return jnp.concatenate(outs, axis=1)


def attend_back(queries, keys, values, probs_ref, first, grad_mixed):
    masks = lane_masks()
    grads = []
    for g in range(D // QUAD):
        cols = slice(g * QUAD, (g + 1) * QUAD)
        q, k, v, go = queries[:, cols], keys[:, cols], values[:, cols], grad_mixed[:, cols]
        gq = gk = gv = None
        for h in range(QUAD // HEAD):
            probs_low = probs_ref[first + g * (QUAD // HEAD) + h]
            probs = probs_low.astype(F32)
            grad_probs = dot_nt(v * masks[h], go)
            both = probs * grad_probs
            grad_scores = (both - probs * jnp.sum(both, axis=0, keepdims=True)).astype(BF)
            part_v = dot(probs_low, go * masks[h])
            part_k = dot(grad_scores, q * masks[h])
            part_q = dot_tn(grad_scores, k * masks[h])
            gv = part_v if gv is None else gv + part_v
            gk = part_k if gk is None else gk + part_k
            gq = part_q if gq is None else gq + part_q
        grads.append((gq * (HEAD**-0.5), gk * (HEAD**-0.5), gv))
    return tuple(jnp.concatenate(parts, axis=1) for parts in zip(*grads))


def put_block(held, index, product):
    held[:, :, index * BLOCK : (index + 1) * BLOCK] = product.astype(BF).reshape(4, 4, BLOCK, D)


class Copies:
    def __init__(self, sems):
        self.sems, self.count, self.out = sems, 0, []

    def start(self, source, target):
        copy = pltpu.make_async_copy(source, target, self.sems.at[self.count])
        self.count += 1
        copy.start()
        return copy

    def load(self, source, target):
        return Loaded(target, [self.start(source, target)])

    def store(self, source, target):
        self.out.append(self.start(source, target))

    def finish(self):
        wait_all(self.out)

    def fetch(self, place, pieces, layout, held):
        rows = held.shape[2] // 4
        if layout.pieces == 1:
            loads = []
            for half in range(2):
                part = pieces[0].at[:, :, pl.ds(layout.offset + 2 * half * rows, 2 * rows)]
                loads.append(self.load(part, held.at[:, :, pl.ds(2 * half * rows, 2 * rows)]))
            return loads
        start = self.count
        self.count += 8
        for dp in range(2):

            @pl.when(place[2] == dp)
            def _():
                for copy in self.piece_copies(place, pieces, layout, held, dp, start):
                    copy.start()

        copies = list(self.piece_copies(place, pieces, layout, held, 0, start))
        return [Loaded(held, copies[:4]), Loaded(held, copies[4:])]

    def piece_copies(self, place, pieces, layout, held, dp, sem):
        rows = held.shape[2] // 4
        for half in range(2):
            for turn in range(2):
                for first in range(2):
                    y, which = place[1] ^ first, place[3] ^ turn
                    quarter = pl.multiple_of((2 * half + which) * rows, rows)
                    piece = pieces[4 * turn + 2 * first + (half ^ dp)]
                    yield pltpu.make_async_copy(
                        piece.at[:, :, pl.ds(layout.offset, rows)],
                        held.at[:, pl.ds(2 * y, 2), pl.ds(quarter, rows)],
                        self.sems.at[sem],
                    )
                    sem += 1

    def deliver(self, place, held, layout, outs, *quarters):
        rows = held.shape[2] // 4
        if layout.made == 1:
            for quarter in (q for q in quarters if q < 4):
                part = pl.ds(layout.made_offset + quarter * rows, rows)
                self.store(held.at[:, :, pl.ds(quarter * rows, rows)], outs[0].at[:, :, part])
        elif 4 in quarters:
            for turn in range(2):
                for first in range(2):
                    for second in range(2):
                        y, half, which = place_of(place, turn, first, second)
                        quarter = pl.multiple_of((2 * half + which) * rows, rows)
                        self.store(
                            held.at[:, pl.ds(2 * y, 2), pl.ds(quarter, rows)],
                            outs[turn].at[first, second],
                        )


def place_of(place, turn, first, second):
    which = place[3] ^ turn
    y = place[1] ^ jnp.where(which == 0, first, second)
    half = place[2] ^ jnp.where(which == 0, second, first)
    return y, half, which


class Loaded:
    def __init__(self, target, copies):
        self.target, self.copies = target, copies

    def arrive(self):
        wait_all(self.copies)
        self.copies.clear()
        return self.target

    def __getitem__(self, index):
        return self.arrive()[index]


def self_forward_part(copies, row, gains, bias, inputs, loads, held, scratch, outs):
    out, normed, joined, probs, mixed = scratch
    out_ref, normed_ref, joined_ref, probs_ref, mixed_ref = outs
    passes = len(inputs)
    for p in range(passes):
        rows = slice(p * TOK, (p + 1) * TOK)
        unit, unused = normed_of(inputs[p][...].astype(F32))
        normed[rows] = (unit * gains[row : row + 1] + gains[row + 1 : row + 2]).astype(BF)
    copies.store(normed, normed_ref)
    for b in range(3):
        loads[b // 2].arrive()
        joined[:, b * D : (b + 1) * D] = dot(normed[...], column_block(held, b)).astype(BF)
    copies.store(joined, joined_ref)
    for p in range(passes):
        rows = slice(p * TOK, (p + 1) * TOK)
        mixed_part = attend(
            joined[rows, 0:D], joined[rows, D : 2 * D], joined[rows, 2 * D : 3 * D], bias, probs, p * HEADS
        )
        heads = pl.ds(p * HEADS, HEADS)
        copies.store(probs.at[heads], probs_ref.at[heads])
        mixed[rows] = mixed_part
        out[rows] = inputs[p][...].astype(F32) + dot(mixed_part, column_block(held, 3))
    copies.store(out, out_ref)
    copies.store(mixed, mixed_ref)


def norm_table(copies, place, pieces, gains, held):
    loads = [
        copies.load(pieces[2 * k].at[:, :, pl.ds(64, 16)], held.at[k]) for k in range(2)
    ]

    def compute():
        for load in loads:
            load.arrive()
        for y in range(2):
            where = jnp.where(place[1] == y, 0, 1)
            for z in range(4):
                for core in range(2):
                    spot = 4 * z + 2 * y + core
                    row = held[where, z, core]
                    gains[:, spot * BLOCK : (spot + 1) * BLOCK] = row[:, 0:BLOCK].astype(F32)

    return compute


def self_forward_kernel(decoder, encoder, me_ref, src_lengths, tgt_lengths, given, *refs):
    taken, refs = refs[:3], refs[3:]
    pieces, refs = refs[: decoder.pieces], refs[decoder.pieces :]
    more, refs = refs[: encoder.pieces], refs[encoder.pieces :]
    outs, gains, scratch, (held, held_enc, held_norm, *come, sems) = refs[:10], refs[10], refs[11:21], refs[21:]
    copies = Copies(sems)
    table = norm_table(copies, me_ref, pieces, gains, held_norm) if decoder.pieces > 1 else None
    inputs = [copies.load(taken[p], come[p]) for p in range(3)]
    loads = copies.fetch(me_ref, pieces, decoder, held)
    loads_enc = copies.fetch(me_ref, more, encoder, held_enc)
    bias = mask_bias(tgt_lengths, tgt_lengths)
    if table:
        table()
    else:
        gains[...] = given[...]
    self_forward_part(copies, 4, gains, bias, inputs[:2], loads, held, scratch[:5], outs[:5])
    bias = mask_bias(src_lengths, src_lengths)
    self_forward_part(copies, 0, gains, bias, inputs[2:], loads_enc, held_enc, scratch[5:], outs[5:])
    copies.finish()


def self_back_kernel(passes, row, more, layout, me_ref, gains, *refs):
    others, refs = refs[:more], refs[more:]
    inputs, refs = refs[:passes], refs[passes:]
    taken, refs = refs[:5], refs[5:]
    pieces, refs = refs[: layout.pieces], refs[layout.pieces :]
    grad_in_ref, norm_ref, *refs = refs
    outs, refs = refs[: layout.made], refs[layout.made :]
    grad_in, held, made, back, grad_out, normed, joined, probs, mixed, *come, sems = refs
    copies = Copies(sems)
    grad_out = copies.load(taken[0], grad_out)
    mixed = copies.load(taken[4], mixed)
    loads = copies.fetch(me_ref, pieces, layout, held)
    probs = [
        copies.load(taken[3].at[pl.ds(p * HEADS, HEADS)], probs.at[pl.ds(p * HEADS, HEADS)])
        for p in range(passes)
    ]
    joined = copies.load(taken[2], joined)
    normed = copies.load(taken[1], normed)
    inputs = [copies.load(inputs[p], come[p]) for p in range(passes)]
    grad_low = grad_out[...].astype(BF)
    put_block(made, 3, dot_tn(mixed[...], grad_low))
    copies.deliver(me_ref, made, layout, outs, 3)
    loads[1].arrive()
    grad_mixed = dot_nt(grad_low, column_block(held, 3)).astype(BF)
    for p in range(passes):
        rows = slice(p * TOK, (p + 1) * TOK)
        grads = attend_back(
            joined[rows, 0:D],
            joined[rows, D : 2 * D],
            joined[rows, 2 * D : 3 * D],
            probs[p].arrive(),
            0,
            grad_mixed[rows],
        )
        for b in range(3):
            back[rows, b * D : (b + 1) * D] = grads[b].astype(BF)
    loads[0].arrive()
    for b in range(3):
        part = back[:, b * D : (b + 1) * D]
        put_block(made, b, dot_tn(normed[...], part))
        copies.deliver(me_ref, made, layout, outs, b)
    copies.deliver(me_ref, made, layout, outs, 4)
    grad_normed = None
    for b in range(3):
        step = dot_nt(back[:, b * D : (b + 1) * D], column_block(held, b))
        grad_normed = step if grad_normed is None else grad_normed + step
    units = [normed_of(inputs[p][...].astype(F32)) for p in range(passes)]
    unit = jnp.concatenate([u[0] for u in units], axis=0)
    inverse = jnp.concatenate([u[1] for u in units], axis=0)
    if more:
        norm_ref[...] = jnp.zeros(norm_ref.shape, F32)
        for k, other in enumerate(others):
            norm_ref[2 * k + 2 : 2 * k + 4] = other[...]
    grad = norm_back(unit, inverse, gains[row : row + 1], grad_normed, norm_ref)
    grad_in[...] = grad_out[0:TOK] + grad[0:TOK]
    copies.store(grad_in, grad_in_ref)
    copies.finish()


GELU_SCALE = 0.7978845608028654
GELU_CUBE = 0.044715


def gelu_both(up):
    square = up * up
    bent = jnp.tanh(up * (GELU_SCALE + (GELU_SCALE * GELU_CUBE) * square))
    half = 0.5 + 0.5 * bent
    inner = 2.0 * GELU_SCALE + (6.0 * GELU_SCALE * GELU_CUBE) * square
    return up * half, half + up * (half - half * half) * inner


def ffn_grads(copies, place, layout, outs, gain, hidden, grad_low, normed, active, slope, norm_ref, held, made):
    for z in range(4):
        product = dot_tn(active[:, z * D : (z + 1) * D], grad_low)
        made[z, :, 4 * BLOCK : 8 * BLOCK] = product.astype(BF).reshape(4, 4 * BLOCK, D)
    copies.deliver(place, made, layout, outs, 2)
    copies.deliver(place, made, layout, outs, 3)
    grad_normed = None
    for b in range(4):
        cols = slice(b * D, (b + 1) * D)
        grad_active = dot_nt(grad_low, row_block(held, b))
        grad_up = (slope[:, cols].astype(F32) * grad_active).astype(BF)
        put_block(made, b, dot_tn(normed[...], grad_up))
        if b % 2 == 1:
            copies.deliver(place, made, layout, outs, b // 2)
        step = dot_nt(grad_up, column_block(held, b))
        grad_normed = step if grad_normed is None else grad_normed + step
    copies.deliver(place, made, layout, outs, 4)
    unit, inverse = normed_of(hidden)
    return norm_back(unit, inverse, gain, grad_normed, norm_ref)


def ffn_back_kernel(row, layout, me_ref, gains, *refs):
    taken, refs = refs[:5], refs[5:]
    pieces, refs = refs[: layout.pieces], refs[layout.pieces :]
    grad_in_ref, norm_ref, *refs = refs
    outs, refs = refs[: layout.made], refs[layout.made :]
    grad_in, held, made, hidden, grad_out, normed, active, slope, sems = refs
    copies = Copies(sems)
    grad_out = copies.load(taken[1], grad_out)
    active = copies.load(taken[3], active)
    loads = copies.fetch(me_ref, pieces, layout, held)
    slope = copies.load(taken[4], slope)
    normed = copies.load(taken[2], normed)
    hidden = copies.load(taken[0], hidden)
    grad_low = grad_out[...].astype(BF)
    active = active.arrive()
    for load in loads:
        load.arrive()
    hidden.arrive()
    grad = ffn_grads(
        copies, me_ref, layout, outs, gains[row : row + 1], hidden[...], grad_low, normed, active, slope, norm_ref, held, made
    )
    grad_in[...] = grad_out[...] + grad
    copies.store(grad_in, grad_in_ref)
    copies.finish()


def second_kernel(encoder, cross, me_ref, src_lengths, tgt_lengths, gains, *refs):
    taken, whole, refs = refs[:2], refs[2:4], refs[4:]
    sent, made, (held_enc, held_cross, hidden_enc, hidden_one, sems) = refs[:10], refs[10:20], refs[20:]
    normed_enc, active_enc, slope_enc, memory, normed, query, pair, probs, mixed, hidden = made
    copies = Copies(sems)
    hidden_enc = copies.load(taken[0], hidden_enc)
    loads_enc = copies.fetch(me_ref, whole[:1], encoder, held_enc)
    hidden_one = copies.load(taken[1], hidden_one)
    loads_cross = copies.fetch(me_ref, whole[1:], cross, held_cross)

    unit, unused = normed_of(hidden_enc[...])
    normed_enc[...] = (unit * gains[2:3] + gains[3:4]).astype(BF)
    copies.store(normed_enc, sent[0])
    unit, unused = normed_of(hidden_one[...])
    normed[...] = (unit * gains[6:7] + gains[7:8]).astype(BF)
    copies.store(normed, sent[4])
    loads_enc[0].arrive()
    for b in range(4):
        cols = slice(b * D, (b + 1) * D)
        grown, bent = gelu_both(dot(normed_enc[...], column_block(held_enc, b)))
        active_enc[:, cols] = grown.astype(BF)
        slope_enc[:, cols] = bent.astype(BF)
    copies.store(active_enc, sent[1])
    copies.store(slope_enc, sent[2])
    loads_enc[1].arrive()
    total = hidden_enc[...]
    for z in range(4):
        total = total + dot(active_enc[:, z * D : (z + 1) * D], row_block(held_enc, z))
    memory[...] = total.astype(BF)
    copies.store(memory, sent[3])

    loads_cross[0].arrive()
    query[...] = dot(normed[...], column_block(held_cross, 0)).astype(BF)
    copies.store(query, sent[5])
    pair[:, 0:D] = dot(memory[...], column_block(held_cross, 1)).astype(BF)
    loads_cross[1].arrive()
    pair[:, D : 2 * D] = dot(memory[...], column_block(held_cross, 2)).astype(BF)
    copies.store(pair, sent[6])
    bias = mask_bias(src_lengths, tgt_lengths)
    for p in range(2):
        rows = slice(p * TOK, (p + 1) * TOK)
        part = attend(query[rows], pair[:, 0:D], pair[:, D : 2 * D], bias, probs, p * HEADS)
        heads = pl.ds(p * HEADS, HEADS)
        copies.store(probs.at[heads], sent[7].at[heads])
        mixed[rows] = part
        hidden[rows] = hidden_one[rows] + dot(part, column_block(held_cross, 3))
    copies.store(mixed, sent[8])
    copies.store(hidden, sent[9])
    copies.finish()


def middle_kernel(cross, decoder, me_ref, gains, *refs):
    taken, whole, refs = refs[:10], refs[10:11], refs[11:]
    pieces, refs = refs[: decoder.pieces], refs[decoder.pieces :]
    norm_ffn, norm_cross, *refs = refs
    sent, refs = refs[:5], refs[5:]
    come, refs = refs[:10], refs[10:]
    held_cross, held, made_cross, made, first_out, second_out, grad_memory, grad_one, *refs = refs
    normed_two, active, slope, grad_two, back, sems = refs
    copies = Copies(sems)
    hidden = copies.load(taken[0], come[0])
    loads = copies.fetch(me_ref, pieces, decoder, held)
    cots = [copies.load(taken[k], come[k]) for k in (1, 2)]
    loads_cross = copies.fetch(me_ref, whole, cross, held_cross)
    mixed, probs, query, pair, normed, memory, hidden_one = (
        copies.load(taken[k], come[k]) for k in range(3, 10)
    )

    unit, unused = normed_of(hidden[...])
    normed_two[...] = (unit * gains[8:9] + gains[9:10]).astype(BF)
    loads[0].arrive()
    for b in range(4):
        cols = slice(b * D, (b + 1) * D)
        grown, bent = gelu_both(dot(normed_two[...], column_block(held, b)))
        active[:, cols] = grown.astype(BF)
        slope[:, cols] = bent.astype(BF)
    loads[1].arrive()
    total = hidden[...]
    for z in range(4):
        total = total + dot(active[:, z * D : (z + 1) * D], row_block(held, z))
    first_out[...] = total[0:TOK].astype(BF)
    second_out[...] = total[TOK:].astype(BF)
    copies.store(first_out, sent[0])
    copies.store(second_out, sent[1])
    grad_low = jnp.concatenate([cots[0][...], cots[1][...]], axis=0)
    grad = ffn_grads(
        copies, me_ref, decoder, sent[4:], gains[8:9], hidden[...], grad_low, normed_two, active, slope, norm_ffn, held, made
    )
    grad_two[...] = grad_low.astype(F32) + grad

    grad_low = grad_two[...].astype(BF)
    put_block(made_cross, 3, dot_tn(mixed[...], grad_low))
    copies.deliver(me_ref, made_cross, cross, sent[4:], 3)
    loads_cross[1].arrive()
    grad_mixed = dot_nt(grad_low, column_block(held_cross, 3)).astype(BF)
    grad_key = grad_value = None
    probs = probs.arrive()
    for p in range(2):
        rows = slice(p * TOK, (p + 1) * TOK)
        grads = attend_back(
            query[rows], pair[:, 0:D], pair[:, D : 2 * D], probs, p * HEADS, grad_mixed[rows]
        )
        back[rows] = grads[0].astype(BF)
        grad_key = grads[1] if grad_key is None else grad_key + grads[1]
        grad_value = grads[2] if grad_value is None else grad_value + grads[2]
    grad_key = grad_key.astype(BF)
    grad_value = grad_value.astype(BF)
    for b, (left, right) in enumerate(
        ((normed[...], back[...]), (memory[...], grad_key), (memory[...], grad_value))
    ):
        put_block(made_cross, b, dot_tn(left, right))
        copies.deliver(me_ref, made_cross, cross, sent[4:], b)
    loads_cross[0].arrive()
    grad_memory[...] = dot_nt(grad_key, column_block(held_cross, 1)) + dot_nt(
        grad_value, column_block(held_cross, 2)
    )
    copies.store(grad_memory, sent[2])
    grad_normed = dot_nt(back[...], column_block(held_cross, 0))
    unit, inverse = normed_of(hidden_one[...])
    grad = norm_back(unit, inverse, gains[6:7], grad_normed, norm_cross)
    grad_one[...] = grad_two[...] + grad
    copies.store(grad_one, sent[3])
    copies.finish()


ANY = pl.BlockSpec(memory_space=pl.ANY)
HB = pl.BlockSpec(memory_space=pltpu.HBM)
VM = pl.BlockSpec(memory_space=pltpu.VMEM)
SM = pl.BlockSpec(memory_space=pltpu.SMEM)


def held_of(blocks):
    return pltpu.VMEM((4, 4, blocks * BLOCK, D), BF)


def made_of(layout, blocks):
    if layout.made == 1:
        return [jax.ShapeDtypeStruct((4, 4, layout.made_rows, D), BF)]
    return [jax.ShapeDtypeStruct((2, 2, 4, 2, blocks * BLOCK // 4, D), BF)] * 2


def shape(rows, cols, dtype):
    return jax.ShapeDtypeStruct((rows, cols), dtype)


class Order:
    def __init__(self):
        self.token = None

    def tie(self, value):
        return self.tie_all([value])[0]

    def tie_all(self, values):
        arrays = list(values) + [self.token]
        *values, self.token = pl.pallas_call(
            nothing_kernel,
            name="tie",
            out_shape=[jax.ShapeDtypeStruct(x.shape, x.dtype) for x in arrays],
            in_specs=[HB] * len(arrays),
            out_specs=[HB] * len(arrays),
            input_output_aliases={k: k for k in range(len(arrays))},
            compiler_params=pltpu.CompilerParams(vmem_limit_bytes=VMEM_LIMIT),
        )(*arrays)
        return values


def nothing_kernel(*refs):
    pass


def call(order, body, name, in_specs, out_shape, out_specs, scratch, operands, micros, grid=None, inplace=()):
    inplace = list(inplace) + ([(order.token, len(out_shape))] if order.token is not None else [])
    count, more, outs = len(operands), len(inplace), len(out_shape)

    def ordered(*refs):
        body(*refs[:count], *refs[count + more : count + more + outs], *refs[count + more + outs + 1 :])

    aliases = {count + k: out for k, (unused, out) in enumerate(inplace)}
    *results, order.token = pl.pallas_call(
        ordered,
        name=name,
        out_shape=out_shape + [jax.ShapeDtypeStruct((8, 128), F32)],
        in_specs=in_specs + [HB] * more,
        out_specs=out_specs + [HB],
        input_output_aliases=aliases,
        scratch_shapes=scratch,
        compiler_params=pltpu.CompilerParams(vmem_limit_bytes=VMEM_LIMIT),
        cost_estimate=pl.CostEstimate(
            flops=int((micros + 0.01) * COST), bytes_accessed=0, transcendentals=0
        ),
        **({} if grid is None else {"grid": grid}),
    )(*operands, *(array for array, unused in inplace))
    return results


def vmem(rows, cols, dtype):
    return pltpu.VMEM((rows, cols), dtype)


def probs_of(count, scratch=False):
    dims = (count * HEADS, TOK, TOK)
    return pltpu.VMEM(dims, BF) if scratch else jax.ShapeDtypeStruct(dims, BF)


SEMS = pltpu.SemaphoreType.DMA((64,))


def arrays(items):
    return [jax.ShapeDtypeStruct(dims, dtype) for dims, dtype in items]


def buffers(items):
    return [pltpu.VMEM(dims, dtype) for dims, dtype in items]


def self_kept(count):
    rows = count * TOK
    return [
        ((rows, D), F32),
        ((rows, D), BF),
        ((rows, 3 * D), BF),
        ((count * HEADS, TOK, TOK), BF),
        ((rows, D), BF),
    ]


def self_forward(order, me, src_lengths, tgt_lengths, gains, inputs, decoder, encoder):
    kept = self_kept(2) + self_kept(1)
    results = call(
        order,
        functools.partial(self_forward_kernel, decoder[0], encoder[0]),
        "self_forward",
        [SM, SM, SM, ANY if decoder[0].pieces > 1 else VM] + [HB] * 3 + [ANY] * (decoder[0].pieces + encoder[0].pieces),
        arrays(kept) + [shape(16, D, F32)],
        [HB] * 10 + [VM],
        buffers(kept)
        + [held_of(4), held_of(4), pltpu.VMEM((2, 4, 2, 16, D), BF)]
        + [vmem(TOK, D, BF)] * 3
        + [SEMS],
        (me, src_lengths, tgt_lengths, gains, *inputs, *decoder[1], *encoder[1]),
        12,
    )
    return results[:5], results[5:10], results[10]


def second(order, me, src_lengths, tgt_lengths, gains, hidden_enc, hidden_one, encoder, cross):
    rows = 2 * TOK
    kept = [
        ((TOK, D), BF),
        ((TOK, FF), BF),
        ((TOK, FF), BF),
        ((TOK, D), BF),
        ((rows, D), BF),
        ((rows, D), BF),
        ((TOK, 2 * D), BF),
        ((2 * HEADS, TOK, TOK), BF),
        ((rows, D), BF),
        ((rows, D), F32),
    ]
    results = call(
        order,
        functools.partial(second_kernel, encoder[0], cross[0]),
        "second",
        [SM, SM, SM, VM] + [HB] * 2 + [ANY] * 2,
        arrays(kept),
        [HB] * 10,
        buffers(kept) + [held_of(8), held_of(4), vmem(TOK, D, F32), vmem(rows, D, F32), SEMS],
        (me, src_lengths, tgt_lengths, gains, hidden_enc, hidden_one, encoder[1][0], cross[1][0]),
        13,
    )
    return results[:3], results[3:]


def self_back(order, row, me, gains, inputs, grad_out, kept, pieces, others=()):
    count = len(inputs)
    rows = count * TOK
    return call(
        order,
        functools.partial(self_back_kernel, count, row, len(others), pieces[0]),
        "self_back",
        [SM, VM] + [VM] * len(others) + [HB] * count + [HB] * 5 + [ANY] * pieces[0].pieces,
        [shape(TOK, D, F32), shape(16 if others else 2, D, F32)] + made_of(pieces[0], 4),
        [HB, VM] + [HB] * pieces[0].made,
        [
            vmem(TOK, D, F32),
            held_of(4),
            held_of(4),
            vmem(rows, 3 * D, BF),
            vmem(rows, D, F32),
            vmem(rows, D, BF),
            vmem(rows, 3 * D, BF),
            probs_of(count, True),
            vmem(rows, D, BF),
        ]
        + [vmem(TOK, D, BF)] * count
        + [SEMS],
        (me, gains, *others, *inputs, grad_out, *kept, *pieces[1]),
        5.8 + 3.4 * count,
    )


def ffn_back(order, row, me, gains, hidden, grad_out, kept, pieces):
    return call(
        order,
        functools.partial(ffn_back_kernel, row, pieces[0]),
        "ffn_back",
        [SM, VM] + [HB] * 5 + [ANY] * pieces[0].pieces,
        [shape(TOK, D, F32), shape(2, D, F32)] + made_of(pieces[0], 8),
        [HB, VM] + [HB] * pieces[0].made,
        [
            vmem(TOK, D, F32),
            held_of(8),
            held_of(8),
            vmem(TOK, D, F32),
            vmem(TOK, D, F32),
            vmem(TOK, D, BF),
            vmem(TOK, FF, BF),
            vmem(TOK, FF, BF),
            SEMS,
        ],
        (me, gains, hidden, grad_out, *kept, *pieces[1]),
        10.2,
    )


def middle(order, me, gains, hidden_one, kept, cots, cross, decoder):
    rows = 2 * TOK
    memory, normed, query, pair, probs, mixed, hidden = kept
    taken = [hidden, *cots, mixed, probs, query, pair, normed, memory, hidden_one]
    sent = [((TOK, D), BF), ((TOK, D), BF), ((TOK, D), F32), ((rows, D), F32)]
    return call(
        order,
        functools.partial(middle_kernel, cross[0], decoder[0]),
        "middle",
        [SM, VM] + [HB] * 10 + [ANY] * (1 + decoder[0].pieces),
        [shape(2, D, F32)] * 2 + arrays(sent + [((4, 4, 384, D), BF)]),
        [VM] * 2 + [HB] * 5,
        buffers([(x.shape, x.dtype) for x in taken])
        + [held_of(4), held_of(8), held_of(4), held_of(8)]
        + buffers(sent)
        + [
            vmem(rows, D, BF),
            vmem(rows, FF, BF),
            vmem(rows, FF, BF),
            vmem(rows, D, F32),
            vmem(rows, D, BF),
            SEMS,
        ],
        (me, gains, *taken, cross[1][0], *decoder[1]),
        25,
    )


AXIS = "fsdp"
BOTH = ("dp", "fsdp")
SHARDS = 16


def route(target):
    pairs = []
    for i in range(2 * SHARDS):
        dp, z, y, core = target(i // 16, (i // 4) % 4, (i // 2) % 2, i % 2)
        pairs.append((i, dp * 16 + (z % 4) * 4 + y * 2 + core))
    return pairs


def to_core(x):
    return lax.ppermute(x, BOTH, route(lambda dp, z, y, core: (dp, z, y, 1 - core)))


def to_z(x, step):
    return lax.ppermute(x, BOTH, route(lambda dp, z, y, core: (dp, z + step, y, core)))


def to_z_pair(x, step):
    return lax.ppermute(x, BOTH, route(lambda dp, z, y, core: (dp, z ^ step, y, core)))


def to_y(x):
    return lax.ppermute(x, BOTH, route(lambda dp, z, y, core: (dp, z, 1 - y, core)))


def to_dp(x):
    return lax.ppermute(x, BOTH, route(lambda dp, z, y, core: (1 - dp, z, y, core)))


def to_yx(x):
    return lax.ppermute(
        x, BOTH, route(lambda dp, z, y, core: (dp, z, y ^ 1, core) if core == 0 else (dp ^ 1, z, y, core))
    )


def to_xy(x):
    return lax.ppermute(
        x, BOTH, route(lambda dp, z, y, core: (dp ^ 1, z, y, core) if core == 0 else (dp, z, y ^ 1, core))
    )


def blocks_of(shard):
    rows, cols = shard.shape
    split = shard.reshape(rows // BLOCK, BLOCK, cols // D, D)
    return split.transpose(2, 0, 1, 3).reshape(-1, BLOCK, D)


def shard_of(blocks, cols):
    wide = blocks.reshape(cols // D, -1, D)
    return wide.transpose(1, 0, 2).reshape(-1, cols)


def small(order, body, name, out, operands, scratch=(), in_specs=None, out_specs=None, micros=0, grid=None):
    return call(
        order,
        body,
        name,
        in_specs if in_specs is not None else [VM] * len(operands),
        [jax.ShapeDtypeStruct(dims, dtype) for dims, dtype in out],
        out_specs if out_specs is not None else [VM] * len(out),
        list(scratch),
        operands,
        micros,
        grid,
    )


def pack_kernel(*refs):
    weights, (one, two, three, place, norms) = refs[:15], refs[15:]
    spot = lax.axis_index(AXIS)
    place[0] = spot >> 2
    place[1] = (spot >> 1) & 1
    place[2] = lax.axis_index("dp")
    place[3] = spot & 1
    self_in, self_out, enc_in, enc_out, enc_ffn_in, enc_ffn_out = weights[:6]
    cross_q, cross_kv, cross_out, ffn_in, ffn_out = weights[6:11]
    for half in range(2):

        @pl.when(place[2] == half)
        def _():
            for k in range(2):
                quarter = 2 * half + k
                cols = slice(quarter * D, (quarter + 1) * D)
                one[k, 0:32] = self_out[...] if quarter == 3 else self_in[:, cols]
                one[k, 32:64] = enc_out[...] if quarter == 3 else enc_in[:, cols]
                for j in range(2):
                    block = 2 * quarter + j
                    rows = slice(j * BLOCK, (j + 1) * BLOCK)
                    cols = slice(block * D, (block + 1) * D)
                    part = slice((block - 4) * BLOCK, (block - 3) * BLOCK)
                    three[k, rows] = ffn_in[:, cols] if block < 4 else ffn_out[part]

    for block in range(4):
        rows = slice(block * BLOCK, (block + 1) * BLOCK)
        two[rows] = enc_ffn_in[:, block * D : (block + 1) * D]
    two[128:256] = enc_ffn_out[...]
    two[256:288] = cross_q[...]
    two[288:320] = cross_kv[:, 0:D]
    two[320:352] = cross_kv[:, D : 2 * D]
    two[352:384] = cross_out[...]
    norms[...] = jnp.zeros(norms.shape, F32)
    row = 0
    for gain, bias in (weights[11:13], weights[13:15]):
        for k in range(gain.shape[0]):
            norms[row : row + 1, 0:BLOCK] = gain[k : k + 1].astype(F32)
            norms[row + 1 : row + 2, 0:BLOCK] = bias[k : k + 1].astype(F32)
            row += 2
    for k in range(2):
        one[k, 64:80] = norms[...].astype(BF)


def pack(order, weights, norms):
    return small(
        order,
        pack_kernel,
        "pack",
        [((2, 80, D), BF), ((384, D), BF), ((2, 64, D), BF), ((4,), jnp.int32)],
        (*weights, *norms),
        [pltpu.VMEM((16, D), F32)],
        in_specs=[VM] * 15,
        out_specs=[VM] * 3 + [SM],
    )


def pair_kernel(place, *refs):
    core = place[3]
    for k in range(2):
        mine, near, pair = refs[2 * k], refs[2 * k + 1], refs[4 + k]
        pair[core] = mine[core]
        pair[1 - core] = near[core]


def pair_up(order, place, mine, near):
    operands = [x for both in zip(mine, near) for x in both]
    return small(
        order,
        pair_kernel,
        "pair_up",
        [(x.shape, x.dtype) for x in mine],
        (place, *operands),
        in_specs=[SM] + [VM] * 4,
    )


def stack_kernel(place, *refs):
    parts, (out, held, sems) = refs[:-3], refs[-3:]
    count = len(parts)
    loads = [pltpu.make_async_copy(parts[d], held.at[d], sems.at[d]) for d in range(count)]
    stores = [
        pltpu.make_async_copy(held.at[d], out.at[(place[0] + (4 - d)) & 3], sems.at[count + d])
        for d in range(count)
    ]
    for copy in loads:
        copy.start()
    for d in range(count):
        loads[d].wait()
        stores[d].start()
    wait_all(stores)


def stack(order, place, parts):
    dims = (len(parts),) + parts[0].shape
    dtype = parts[0].dtype
    return small(
        order,
        stack_kernel,
        "stack",
        [(dims, dtype)],
        (place, *parts),
        [pltpu.VMEM(dims, dtype), pltpu.SemaphoreType.DMA((2 * len(parts),))],
        [SM] + [ANY] * len(parts),
        [ANY],
    )[0]


class Gather:
    def __init__(self, order, pair):
        self.order, self.pair = order, pair

    def along_z(self):
        pair = self.order.tie(self.pair)
        self.parts = [pair] + [to_z(pair, d) for d in (1, 2, 3)]

    def lined(self, place):
        self.line = stack(self.order, place, self.parts)

    def first_cross(self):
        line = self.order.tie(self.line)
        self.own = [line, to_dp(line), to_y(line)]
        self.near = []

    def crossed(self, others=()):
        arrived = self.order.tie_all(self.own[1:3] + list(others[1:]))
        self.own[1:3] = arrived[:2]
        if others:
            others[1:] = arrived[2:]

    def second_cross(self):
        self.own.append(to_dp(self.own[2]))

    def share(self):
        self.near = [to_core(piece) for piece in self.own[:3]]

    def done(self):
        last, *self.near = self.order.tie_all([self.own[3]] + self.near)
        self.own = self.own[:3] + [last]
        self.near.append(self.order.tie(to_core(last)))
        self.pieces = tuple(self.own + self.near)


def low_sum(*parts):
    total = parts[0].astype(F32)
    for part in parts[1:]:
        total = total + part.astype(F32)
    return total.astype(BF)


def rows_of(parts):
    row = 0
    for k, part in enumerate(parts[::2]):
        yield slice(row, row + part.shape[4]), part, parts[2 * k + 1]
        row += part.shape[4]


def send_block(step, source, target, sems, more):
    def copies():
        for k in range(4):
            yield k, pltpu.make_async_copy(
                source.at[k], target.at[pl.ds(k * source.shape[1], source.shape[1])], sems.at[k]
            )

    last = pltpu.make_async_copy(*more, sems.at[4])
    for k, copy in copies():
        pl.when(step == k)(copy.start)
    pl.when(step == 0)(last.start)

    @pl.when(step == 3)
    def _():
        for unused, copy in copies():
            copy.wait()
        last.wait()


def reduce_first_kernel(norm_own, norm_came, *refs):
    sent, held, norm, sems = refs[-4:]
    step = pl.program_id(0)

    @pl.when(step == 0)
    def _():
        norm[...] = (norm_own[...] + norm_came[...]).astype(BF)

    whole = held.shape[1] // 4
    for rows, own, came in rows_of(refs[:-4]):
        for second in range(2):
            for core in range(2):
                row = (2 * second + core) * whole + rows.start
                held[step, row : row + rows.stop - rows.start] = (
                    own[0, second, 0, core] + came[0, second, 0, core]
                )
    send_block(step, held, sent, sems, (norm, sent.at[pl.ds(16 * whole, 16)]))


def reduce_second_kernel(norm_own, norm_came, came_first, *refs):
    sent, held, norm, sems = refs[-4:]
    step = pl.program_id(0)

    @pl.when(step == 0)
    def _():
        norm[...] = (norm_own[...].astype(F32) + norm_came[...].astype(F32)).astype(BF)

    whole = held.shape[1] // 2
    for rows, own, came in rows_of(refs[:-4]):
        for core in range(2):
            span = slice(core * whole + rows.start, core * whole + rows.stop)
            held[step, span] = low_sum(own[0, 0, 0, core], came[0, 0, 0, core], came_first[span])
    send_block(step, held, sent, sems, (norm, sent.at[pl.ds(8 * whole, 16)]))


def reduce_third_kernel(norm_own, norm_came, place, came_first, came_second, *refs):
    outs = refs[-4:]
    norm = (norm_own[...].astype(F32) + norm_came[...].astype(F32)).astype(BF)
    whole = (outs[0].shape[0] - 16) // 2
    for d in range(4):
        z = (place[0] + d) & 3
        outs[d][2 * whole :] = norm
        for rows, own, came in rows_of(refs[:-4]):
            for core in range(2):
                span = slice(core * whole + rows.start, core * whole + rows.stop)
                size = rows.stop - rows.start
                first = pl.multiple_of(z * 4 * whole + span.start, 16)
                second = pl.multiple_of(z * 2 * whole + span.start, 16)
                outs[d][span] = low_sum(
                    own[0, 0, z, core],
                    came[0, 0, z, core],
                    came_first[pl.ds(first, size)],
                    came_second[pl.ds(second, size)],
                )


def reduce_fourth_kernel(a, b, c, d, out, norm):
    rows = out.shape[1]
    for core in range(2):
        span = slice(core * rows, (core + 1) * rows)
        out[core] = low_sum(a[span], b[span], c[span], d[span])
    total = a[2 * rows :].astype(F32)
    for part in (b, c, d):
        total = total + part[2 * rows :].astype(F32)
    norm[...] = total


class Reduce:
    def __init__(self, order):
        self.order, self.own, self.came = order, [], []

    def add(self, own, other):
        self.own.append(own)
        self.came.append(to_core(self.order.tie(other)))

    def arrive(self):
        self.came[-1] = self.order.tie(self.came[-1])

    def start_norm(self, norm):
        self.norm = self.order.tie(norm)
        self.norm_came = to_core(self.norm)

    def run(self, body, name, dims, operands, in_specs, part_spec, out_specs=None, scratch=(), grid=(4,)):
        parts = [x for both in zip(self.own, self.came) for x in both]
        specs = [pl.BlockSpec(part_spec[0] + (part.shape[4], D), part_spec[1]) for part in parts]
        sent = small(
            self.order,
            body,
            name,
            [(item, BF) for item in dims],
            operands + parts,
            scratch,
            in_specs=in_specs + specs,
            out_specs=out_specs or [HB] * len(dims),
            grid=grid,
        )
        return [self.order.tie(x) for x in sent]

    def first(self):
        rows = self.rows = sum(own.shape[4] for own in self.own)
        norm_spec = pl.BlockSpec((16, D), lambda i: (0, 0))
        (self.first_sent,) = self.run(
            reduce_first_kernel,
            "reduce_first",
            [(16 * rows + 16, D)],
            [self.norm, self.norm_came],
            [norm_spec] * 2,
            ((1, 2, 1, 2), lambda i: (1, 0, i, 0, 0, 0)),
            scratch=buffers([((4, 4 * rows, D), BF), ((16, D), BF)]) + [pltpu.SemaphoreType.DMA((5,))],
        )
        self.first_came = to_yx(self.first_sent)

    def second(self):
        rows = self.rows
        norm_spec = pl.BlockSpec((16, D), lambda i: (rows, 0))
        (self.second_sent,) = self.run(
            reduce_second_kernel,
            "reduce_second",
            [(8 * rows + 16, D)],
            [self.first_sent, self.first_came, self.first_came],
            [norm_spec] * 2 + [pl.BlockSpec((2 * rows, D), lambda i: (2 * i + 1, 0))],
            ((1, 1, 1, 2), lambda i: (0, 1, i, 0, 0, 0)),
            scratch=buffers([((4, 2 * rows, D), BF), ((16, D), BF)]) + [pltpu.SemaphoreType.DMA((5,))],
        )
        self.second_came = to_xy(self.second_sent)

    def third(self, place):
        rows = self.rows
        norm_spec = pl.BlockSpec((16, D), lambda i: (rows // 2, 0))
        parts = self.run(
            reduce_third_kernel,
            "reduce_third",
            [(2 * rows + 16, D)] * 4,
            [self.second_sent, self.second_came, place, self.first_came, self.second_came],
            [norm_spec] * 2
            + [SM]
            + [pl.BlockSpec(x.shape, lambda i: (0, 0)) for x in (self.first_came, self.second_came)],
            ((1, 1, 4, 2), lambda i: (0, 0, 0, 0, 0, 0)),
            [pl.BlockSpec((2 * rows + 16, D), lambda i: (0, 0))] * 4,
            grid=(1,),
        )
        self.lines = [parts[0]] + [to_z(parts[d], d) for d in (1, 2, 3)]

    def fourth(self):
        total, self.norm = small(
            self.order,
            reduce_fourth_kernel,
            "reduce_fourth",
            [((2, self.rows, D), BF), ((16, D), F32)],
            self.lines,
        )
        total = self.order.tie(total)
        self.ends = [total, to_dp(total), to_core(total)]

    def last(self):
        near = self.order.tie(self.ends[2])
        came = self.order.tie(self.ends[1])
        self.ends = [self.ends[0], came, near, to_core(came)]


def quarter_of(place, ends, quarter, rows):
    core = place[3]
    half, which = quarter >> 1, quarter & 1
    first = jnp.where(place[3] == which, ends[0][core, rows], ends[2][core, rows].astype(BF))
    second = jnp.where(place[3] == which, ends[1][core, rows], ends[3][core, rows])
    return jnp.where(place[2] == half, first, second).astype(F32)


def unpack_kernel(layout, place, *refs):
    ends, outs = refs[:4], refs[4:]
    first = 0
    for kind, row in layout:
        for quarter in range(4):
            if kind == "ffn":
                for j in range(2):
                    block = 2 * quarter + j
                    rows = slice(row + j * BLOCK, row + (j + 1) * BLOCK)
                    value = quarter_of(place, ends, quarter, rows)
                    if block < 4:
                        outs[first][:, block * D : (block + 1) * D] = value
                    else:
                        outs[first + 1][(block - 4) * BLOCK : (block - 3) * BLOCK] = value
            else:
                value = quarter_of(place, ends, quarter, slice(row, row + BLOCK))
                if kind == "attn":
                    if quarter < 3:
                        outs[first][:, quarter * D : (quarter + 1) * D] = value
                    else:
                        outs[first + 1][...] = value
                elif quarter in (1, 2):
                    outs[first + 1][:, (quarter - 1) * D : quarter * D] = value
                else:
                    outs[first + (quarter + 1) // 2][...] = value
        first += 3 if kind == "cross" else 2


SHARD_SHAPES = {
    "ffn": [((BLOCK, FF), F32), ((4 * BLOCK, D), F32)],
    "attn": [((BLOCK, 3 * D), F32), ((BLOCK, D), F32)],
    "cross": [((BLOCK, D), F32), ((BLOCK, 2 * D), F32), ((BLOCK, D), F32)],
}


def unpack(order, place, ends, layout):
    return small(
        order,
        functools.partial(unpack_kernel, layout),
        "unpack",
        [item for kind, unused in layout for item in SHARD_SHAPES[kind]],
        (place, *ends),
        in_specs=[SM] + [VM] * 4,
    )


def norm_last_kernel(place, total, *outs):
    total = total[...]
    spot = place[0] * 4 + place[1] * 2 + place[3]
    turned = jnp.zeros((16, BLOCK), F32)
    for k in range(SHARDS):
        turned = jnp.where(spot == k, total[:, k * BLOCK : (k + 1) * BLOCK], turned)
    for first, gain, bias in ((0, outs[0], outs[1]), (4, outs[2], outs[3])):
        for k in range(gain.shape[0]):
            gain[k : k + 1] = turned[first + 2 * k : first + 2 * k + 1]
            bias[k : k + 1] = turned[first + 2 * k + 1 : first + 2 * k + 2]


def norm_last(order, place, total):
    return small(
        order,
        norm_last_kernel,
        "norm_last",
        [((2, BLOCK), F32), ((2, BLOCK), F32), ((3, BLOCK), F32), ((3, BLOCK), F32)],
        (place, total),
        in_specs=[SM, VM],
    )


def spread_kernel(own, came, ffn_in, ffn_out, cross_q, cross_kv, cross_out):
    total = own[...].astype(F32) + came[...].astype(F32)
    for block in range(4):
        ffn_in[:, block * D : (block + 1) * D] = total[block * BLOCK : (block + 1) * BLOCK]
    ffn_out[...] = total[128:256]
    cross_q[...] = total[256:288]
    cross_kv[:, 0:D] = total[288:320]
    cross_kv[:, D : 2 * D] = total[320:352]
    cross_out[...] = total[352:384]


def spread(order, own, came):
    return small(
        order,
        spread_kernel,
        "spread",
        SHARD_SHAPES["ffn"] + SHARD_SHAPES["cross"],
        (own, came),
    )


def gather_plain(weights):
    parts = []
    for weight in weights:
        whole = lax.all_gather(weight, AXIS, axis=0, tiled=True)
        parts.append(jax.vmap(blocks_of)(whole.reshape(SHARDS, -1, whole.shape[1])))
    return jnp.concatenate(parts, axis=1).reshape(4, 4, -1, D)


def reduce_plain(made, columns):
    shards = made.reshape(SHARDS, -1, BLOCK, D)
    grads = []
    for first, last, cols in columns:
        whole = jax.vmap(functools.partial(shard_of, cols=cols))(shards[:, first:last])
        whole = whole.reshape(-1, cols).astype(F32)
        part = lax.psum_scatter(whole, AXIS, scatter_dimension=0, tiled=True)
        grads.append(lax.psum(part.astype(BF), "dp").astype(F32))
    return grads


def norm_rows_of(gain_enc, bias_enc, gain_dec, bias_dec):
    rows = []
    for gain, bias in ((gain_enc, bias_enc), (gain_dec, bias_dec)):
        for k in range(gain.shape[0]):
            rows += [gain[k : k + 1], bias[k : k + 1]]
    return jnp.concatenate(rows, axis=0)


ATTN_COLUMNS = ((0, 3, 3 * D), (3, 4, D))
FFN_COLUMNS = ((0, 4, FF), (4, 8, D))
CROSS_COLUMNS = ((0, 1, D), (1, 3, 2 * D), (3, 4, D))


def step(
    custom,
    source,
    first_in,
    second_in,
    cot_first,
    cot_second,
    src_lengths,
    tgt_lengths,
    enc_attn_in,
    enc_attn_out,
    enc_ffn_in,
    enc_ffn_out,
    enc_gain,
    enc_bias,
    dec_self_in,
    dec_self_out,
    dec_cross_q,
    dec_cross_kv,
    dec_cross_out,
    dec_ffn_in,
    dec_ffn_out,
    dec_gain,
    dec_bias,
):
    order = Order()
    group_self = (dec_self_in, dec_self_out)
    group_enc = (enc_attn_in, enc_attn_out)
    group_enc_ffn = (enc_ffn_in, enc_ffn_out)
    group_cross = (dec_cross_q, dec_cross_kv, dec_cross_out)
    group_ffn = (dec_ffn_in, dec_ffn_out)
    if custom:
        weights = group_self + group_enc + group_enc_ffn + group_cross + group_ffn
        mine_one, mine_two, mine_three, place = pack(
            order, weights, (enc_gain, enc_bias, dec_gain, dec_bias)
        )
        mine = (mine_one, mine_three)
        pairs = pair_up(order, place, mine, [to_core(x) for x in mine])
        one, three = (Gather(order, pair) for pair in pairs)
        one.along_z()
        one.parts[3] = order.tie(one.parts[3])
        mine_two = order.tie(mine_two)
        whole = lax.all_gather(mine_two, AXIS, axis=0, tiled=True).reshape(4, 4, -1, D)
        one.lined(place)
        one.first_cross()
        three.along_z()
        one.crossed(three.parts)
        one.second_cross()
        three.lined(place)
        three.first_cross()
        one.share()
        one.done()
        gains = first_in
        w_self, w_enc = (Layout(0, 8), one.pieces), (Layout(32, 8), one.pieces)
        w_enc_ffn = (Layout(0, 1), (whole,))
        w_cross = (Layout(256, 1, 1, 256, 384), (whole,))
    else:
        place = jnp.zeros((4,), jnp.int32)
        w_self, w_enc, w_enc_ffn = (
            (Layout(0, 1, 1, 0, rows), (gather_plain(group),))
            for group, rows in ((group_self, 128), (group_enc, 128), (group_enc_ffn, 256))
        )
        w_cross = (Layout(0, 1, 1, 256, 384), (gather_plain(group_cross),))
        w_ffn = (Layout(0, 1, 1, 0, 384), (gather_plain(group_ffn),))
        norm_rows = norm_rows_of(enc_gain, enc_bias, dec_gain, dec_bias)
        gains = lax.all_gather(norm_rows, AXIS, axis=1, tiled=True)
        gains = jnp.pad(gains.astype(F32), ((0, 6), (0, 0)))

    (hidden_one, *kept_self), (hidden_enc, *kept_enc), gains = self_forward(
        order, place, src_lengths, tgt_lengths, gains, [first_in, second_in, source], w_self, w_enc
    )
    if custom:
        three.crossed()
        three.second_cross()
        three.share()
    kept_enc_ffn, kept_cross = second(
        order, place, src_lengths, tgt_lengths, gains, hidden_enc, hidden_one, w_enc_ffn, w_cross
    )
    if custom:
        three.done()
        w_ffn = (Layout(0, 8, 1, 0, 384), three.pieces)
    norm_ffn, norm_cross, first_out, second_out, grad_memory, grad_one, made = middle(
        order, place, gains, hidden_one, kept_cross, (cot_first, cot_second), w_cross, w_ffn
    )
    if custom:
        scattered = lax.psum_scatter(
            made.reshape(-1, D), AXIS, scatter_dimension=0, tiled=True
        )
    grad_enc, norm_enc_ffn, *made_enc_ffn = ffn_back(
        order, 2, place, gains, hidden_enc, grad_memory, kept_enc_ffn, w_enc_ffn
    )
    if custom:
        red = Reduce(order)
        red.add(*made_enc_ffn)
    grad_first, norm_self, *made_self = self_back(
        order, 4, place, gains, [first_in, second_in], grad_one, kept_self, w_self
    )
    if custom:
        red.arrive()
        red.add(*made_self)
    grad_source, norm_total, *made_enc = self_back(
        order,
        0,
        place,
        gains,
        [source],
        grad_enc,
        kept_enc,
        w_enc,
        (norm_enc_ffn, norm_self, norm_cross, norm_ffn),
    )
    if custom:
        red.arrive()
        red.add(*made_enc)
        red.start_norm(norm_total)
        red.first()
        red.second()
        red.third(place)
        scattered = order.tie(scattered)
        scattered_came = order.tie(to_dp(scattered))
        red.fourth()
        grads_ffn_cross = spread(order, scattered, scattered_came)
        norm_grads = norm_last(order, place, red.norm)
        red.last()
        grads_ffn, grads_cross = grads_ffn_cross[:2], grads_ffn_cross[2:]
        g = unpack(order, place, red.ends, (("ffn", 0), ("attn", 64), ("attn", 96)))
        grads_enc_ffn, grads_self, grads_enc = g[:2], g[2:4], g[4:6]
    else:
        grads_ffn = reduce_plain(made[:, :, 0:256], FFN_COLUMNS)
        grads_cross = reduce_plain(made[:, :, 256:384], CROSS_COLUMNS)
        grads_enc_ffn = reduce_plain(*made_enc_ffn, FFN_COLUMNS)
        grads_self = reduce_plain(*made_self, ATTN_COLUMNS)
        grads_enc = reduce_plain(*made_enc, ATTN_COLUMNS)
        norm_shard = lax.psum_scatter(norm_total, AXIS, scatter_dimension=1, tiled=True)
        norm_shard = lax.psum(norm_shard.astype(BF), "dp").astype(F32)
        norm_grads = (norm_shard[0:4:2], norm_shard[1:4:2], norm_shard[4:10:2], norm_shard[5:10:2])
    return (
        first_out,
        second_out,
        grad_source,
        grad_first,
        *grads_enc,
        *grads_enc_ffn,
        *norm_grads[:2],
        *grads_self,
        *grads_cross,
        *grads_ffn,
        *norm_grads[2:],
    )


def solution(mesh):
    blocked = P(("dp", "fsdp"), None)
    rows = P("fsdp", None)
    columns = P(None, "fsdp")
    custom = mesh.shape["fsdp"] == SHARDS and mesh.shape["dp"] == 2
    return jax.shard_map(
        functools.partial(step, custom),
        mesh=mesh,
        in_specs=(blocked,) * 7 + (rows,) * 4 + (columns,) * 2 + (rows,) * 7 + (columns,) * 2,
        out_specs=(blocked,) * 4 + (rows,) * 4 + (columns,) * 2 + (rows,) * 7 + (columns,) * 2,
        check_vma=False,
    )
```

```python
import functools
import typing

import jax
import jax.numpy as jnp
from jax import lax
from jax.experimental import pallas as pl
from jax.experimental.pallas import tpu as pltpu
from jax.sharding import PartitionSpec as P

D = 512
HEADS = 8
HEAD = 64
TOK = 256
FF = 2048
QUAD = 256
BLOCK = 32
EPSILON = 1e-05
MASKED = -1000000000.0
BF = jnp.bfloat16
F32 = jnp.float32
VMEM_LIMIT = 64 * 1024 * 1024
COST = 1.1e9


class Layout(typing.NamedTuple):
    offset: int
    pieces: int
    made: int = 2
    made_offset: int = 0
    made_rows: int = 0


def dot(left, right):
    return lax.dot_general(left, right, (((1,), (0,)), ((), ())), preferred_element_type=F32)


def dot_nt(left, right):
    return lax.dot_general(left, right, (((1,), (1,)), ((), ())), preferred_element_type=F32)


def dot_tn(left, right):
    return lax.dot_general(left, right, (((0,), (0,)), ((), ())), preferred_element_type=F32)


def wait_all(copies):
    for copy in copies:
        copy.wait()


def column_block(held, index):
    return held[:, :, index * BLOCK : (index + 1) * BLOCK].reshape(D, D)


def row_block(held, index):
    return held[index, :, 4 * BLOCK : 8 * BLOCK].reshape(D, D)


def normed_of(values):
    centre = values - jnp.mean(values, axis=-1, keepdims=True)
    spread = jnp.mean(centre * centre, axis=-1, keepdims=True)
    inverse = lax.rsqrt(spread + EPSILON)
    return centre * inverse, inverse


def norm_back(unit, inverse, gain, grad_normed, norm_ref):
    norm_ref[0:1] = jnp.sum(grad_normed * unit, axis=0, keepdims=True)
    norm_ref[1:2] = jnp.sum(grad_normed, axis=0, keepdims=True)
    grad_unit = grad_normed * gain
    return (
        grad_unit
        - jnp.mean(grad_unit, axis=-1, keepdims=True)
        - unit * jnp.mean(grad_unit * unit, axis=-1, keepdims=True)
    ) * inverse


def mask_bias(key_lengths, query_lengths):
    key_place = lax.broadcasted_iota(jnp.int32, (TOK, 1), 0)
    query_place = lax.broadcasted_iota(jnp.int32, (1, TOK), 1)
    key_ids = jnp.zeros((TOK, 1), jnp.int32)
    query_ids = jnp.zeros((1, TOK), jnp.int32)
    key_end = jnp.int32(0)
    query_end = jnp.int32(0)
    for k in range(key_lengths.shape[1]):
        key_end = key_end + key_lengths[0, k]
        query_end = query_end + query_lengths[0, k]
        key_ids = key_ids + jnp.where(key_place >= key_end, 1, 0)
        query_ids = query_ids + jnp.where(query_place >= query_end, 1, 0)
    return jnp.where(key_ids == query_ids, 0.0, MASKED).astype(F32)


def lane_masks():
    head_of = lax.broadcasted_iota(jnp.int32, (1, QUAD), 1) // HEAD
    return [jnp.where(head_of == h, 1.0, 0.0).astype(BF) for h in range(QUAD // HEAD)]


def attend(queries, keys, values, bias, probs_ref, first):
    masks = lane_masks()
    outs = []
    for g in range(D // QUAD):
        cols = slice(g * QUAD, (g + 1) * QUAD)
        q, k, v = queries[:, cols], keys[:, cols], values[:, cols]
        total = None
        for h in range(QUAD // HEAD):
            scores = dot_nt(k * (masks[h] * (HEAD**-0.5)), q) + bias
            top = jnp.max(scores, axis=0, keepdims=True)
            grown = jnp.exp(scores - top)
            probs = (grown * (1.0 / jnp.sum(grown, axis=0, keepdims=True))).astype(BF)
            probs_ref[first + g * (QUAD // HEAD) + h] = probs
            part = dot_tn(probs, v * masks[h])
            total = part if total is None else total + part
        outs.append(total.astype(BF))
    return jnp.concatenate(outs, axis=1)


def attend_back(queries, keys, values, probs_ref, first, grad_mixed):
    masks = lane_masks()
    grads = []
    for g in range(D // QUAD):
        cols = slice(g * QUAD, (g + 1) * QUAD)
        q, k, v, go = queries[:, cols], keys[:, cols], values[:, cols], grad_mixed[:, cols]
        gq = gk = gv = None
        for h in range(QUAD // HEAD):
            probs_low = probs_ref[first + g * (QUAD // HEAD) + h]
            probs = probs_low.astype(F32)
            grad_probs = dot_nt(v * masks[h], go)
            both = probs * grad_probs
            grad_scores = (both - probs * jnp.sum(both, axis=0, keepdims=True)).astype(BF)
            part_v = dot(probs_low, go * masks[h])
            part_k = dot(grad_scores, q * masks[h])
            part_q = dot_tn(grad_scores, k * masks[h])
            gv = part_v if gv is None else gv + part_v
            gk = part_k if gk is None else gk + part_k
            gq = part_q if gq is None else gq + part_q
        grads.append((gq * (HEAD**-0.5), gk * (HEAD**-0.5), gv))
    return tuple(jnp.concatenate(parts, axis=1) for parts in zip(*grads))


def put_block(held, index, product):
    held[:, :, index * BLOCK : (index + 1) * BLOCK] = product.astype(BF).reshape(4, 4, BLOCK, D)


class Copies:
    def __init__(self, sems):
        self.sems, self.count, self.out = sems, 0, []

    def start(self, source, target):
        copy = pltpu.make_async_copy(source, target, self.sems.at[self.count])
        self.count += 1
        copy.start()
        return copy

    def load(self, source, target):
        return Loaded(target, [self.start(source, target)])

    def store(self, source, target):
        self.out.append(self.start(source, target))

    def finish(self):
        wait_all(self.out)

    def fetch(self, place, pieces, layout, held):
        rows = held.shape[2] // 4
        if layout.pieces == 1:
            loads = []
            for half in range(2):
                part = pieces[0].at[:, :, pl.ds(layout.offset + 2 * half * rows, 2 * rows)]
                loads.append(self.load(part, held.at[:, :, pl.ds(2 * half * rows, 2 * rows)]))
            return loads
        start = self.count
        self.count += 8
        for dp in range(2):

            @pl.when(place[2] == dp)
            def _():
                for copy in self.piece_copies(place, pieces, layout, held, dp, start):
                    copy.start()

        copies = list(self.piece_copies(place, pieces, layout, held, 0, start))
        return [Loaded(held, copies[:4]), Loaded(held, copies[4:])]

    def piece_copies(self, place, pieces, layout, held, dp, sem):
        rows = held.shape[2] // 4
        for half in range(2):
            for turn in range(2):
                for first in range(2):
                    y, which = place[1] ^ first, place[3] ^ turn
                    quarter = pl.multiple_of((2 * half + which) * rows, rows)
                    piece = pieces[4 * turn + 2 * first + (half ^ dp)]
                    yield pltpu.make_async_copy(
                        piece.at[:, :, pl.ds(layout.offset, rows)],
                        held.at[:, pl.ds(2 * y, 2), pl.ds(quarter, rows)],
                        self.sems.at[sem],
                    )
                    sem += 1

    def deliver(self, place, held, layout, outs, *quarters):
        rows = held.shape[2] // 4
        if layout.made == 1:
            for quarter in (q for q in quarters if q < 4):
                part = pl.ds(layout.made_offset + quarter * rows, rows)
                self.store(held.at[:, :, pl.ds(quarter * rows, rows)], outs[0].at[:, :, part])
        elif 4 in quarters and layout.made == 4:
            for part in range(2):
                for turn in range(2):
                    for first in range(2):
                        for second in range(2):
                            y, half, which = place_of(place, turn, first, second)
                            if part == 0:
                                y, half = place[1] ^ second, place[2] ^ first
                            row = pl.multiple_of((2 * half + which) * rows + part * (rows // 2), 16)
                            self.store(
                                held.at[:, pl.ds(2 * y, 2), pl.ds(row, rows // 2)],
                                outs[2 * part + turn].at[first, second],
                            )
        elif 4 in quarters:
            for turn in range(2):
                for first in range(2):
                    for second in range(2):
                        y, half, which = place_of(place, turn, first, second)
                        quarter = pl.multiple_of((2 * half + which) * rows, rows)
                        self.store(
                            held.at[:, pl.ds(2 * y, 2), pl.ds(quarter, rows)],
                            outs[turn].at[first, second],
                        )


def place_of(place, turn, first, second):
    which = place[3] ^ turn
    y = place[1] ^ jnp.where(which == 0, first, second)
    half = place[2] ^ jnp.where(which == 0, second, first)
    return y, half, which


class Loaded:
    def __init__(self, target, copies):
        self.target, self.copies = target, copies

    def arrive(self):
        wait_all(self.copies)
        self.copies.clear()
        return self.target

    def __getitem__(self, index):
        return self.arrive()[index]


def self_forward_part(copies, row, gains, bias, inputs, loads, held, scratch, outs):
    out, normed, joined, probs, mixed = scratch
    out_ref, normed_ref, joined_ref, probs_ref, mixed_ref = outs
    passes = len(inputs)
    for p in range(passes):
        rows = slice(p * TOK, (p + 1) * TOK)
        unit, unused = normed_of(inputs[p][...].astype(F32))
        normed[rows] = (unit * gains[row : row + 1] + gains[row + 1 : row + 2]).astype(BF)
    copies.store(normed, normed_ref)
    for b in range(3):
        loads[b // 2].arrive()
        joined[:, b * D : (b + 1) * D] = dot(normed[...], column_block(held, b)).astype(BF)
    copies.store(joined, joined_ref)
    for p in range(passes):
        rows = slice(p * TOK, (p + 1) * TOK)
        mixed_part = attend(
            joined[rows, 0:D], joined[rows, D : 2 * D], joined[rows, 2 * D : 3 * D], bias, probs, p * HEADS
        )
        heads = pl.ds(p * HEADS, HEADS)
        copies.store(probs.at[heads], probs_ref.at[heads])
        mixed[rows] = mixed_part
        out[rows] = inputs[p][...].astype(F32) + dot(mixed_part, column_block(held, 3))
    copies.store(out, out_ref)
    copies.store(mixed, mixed_ref)


def norm_table(copies, place, pieces, gains, held):
    loads = [
        copies.load(pieces[2 * k].at[:, :, pl.ds(64, 16)], held.at[k]) for k in range(2)
    ]

    def compute():
        for load in loads:
            load.arrive()
        for y in range(2):
            where = jnp.where(place[1] == y, 0, 1)
            for z in range(4):
                for core in range(2):
                    spot = 4 * z + 2 * y + core
                    row = held[where, z, core]
                    gains[:, spot * BLOCK : (spot + 1) * BLOCK] = row[:, 0:BLOCK].astype(F32)

    return compute


def self_forward_kernel(decoder, encoder, me_ref, src_lengths, tgt_lengths, given, *refs):
    taken, refs = refs[:3], refs[3:]
    pieces, refs = refs[: decoder.pieces], refs[decoder.pieces :]
    more, refs = refs[: encoder.pieces], refs[encoder.pieces :]
    outs, gains, scratch, (held, held_enc, held_norm, *come, sems) = refs[:10], refs[10], refs[11:21], refs[21:]
    copies = Copies(sems)
    table = norm_table(copies, me_ref, pieces, gains, held_norm) if decoder.pieces > 1 else None
    inputs = [copies.load(taken[p], come[p]) for p in range(3)]
    loads = copies.fetch(me_ref, pieces, decoder, held)
    loads_enc = copies.fetch(me_ref, more, encoder, held_enc)
    bias = mask_bias(tgt_lengths, tgt_lengths)
    if table:
        table()
    else:
        gains[...] = given[...]
    self_forward_part(copies, 4, gains, bias, inputs[:2], loads, held, scratch[:5], outs[:5])
    bias = mask_bias(src_lengths, src_lengths)
    self_forward_part(copies, 0, gains, bias, inputs[2:], loads_enc, held_enc, scratch[5:], outs[5:])
    copies.finish()


def self_back_kernel(passes, row, more, layout, me_ref, gains, *refs):
    others, refs = refs[:more], refs[more:]
    inputs, refs = refs[:passes], refs[passes:]
    taken, refs = refs[:5], refs[5:]
    pieces, refs = refs[: layout.pieces], refs[layout.pieces :]
    grad_in_ref, norm_ref, *refs = refs
    outs, refs = refs[: layout.made], refs[layout.made :]
    grad_in, held, made, back, grad_out, normed, joined, probs, mixed, *come, sems = refs
    copies = Copies(sems)
    grad_out = copies.load(taken[0], grad_out)
    mixed = copies.load(taken[4], mixed)
    loads = copies.fetch(me_ref, pieces, layout, held)
    probs = [
        copies.load(taken[3].at[pl.ds(p * HEADS, HEADS)], probs.at[pl.ds(p * HEADS, HEADS)])
        for p in range(passes)
    ]
    joined = copies.load(taken[2], joined)
    normed = copies.load(taken[1], normed)
    inputs = [copies.load(inputs[p], come[p]) for p in range(passes)]
    grad_low = grad_out[...].astype(BF)
    put_block(made, 3, dot_tn(mixed[...], grad_low))
    copies.deliver(me_ref, made, layout, outs, 3)
    loads[1].arrive()
    grad_mixed = dot_nt(grad_low, column_block(held, 3)).astype(BF)
    for p in range(passes):
        rows = slice(p * TOK, (p + 1) * TOK)
        grads = attend_back(
            joined[rows, 0:D],
            joined[rows, D : 2 * D],
            joined[rows, 2 * D : 3 * D],
            probs[p].arrive(),
            0,
            grad_mixed[rows],
        )
        for b in range(3):
            back[rows, b * D : (b + 1) * D] = grads[b].astype(BF)
    loads[0].arrive()
    for b in range(3):
        part = back[:, b * D : (b + 1) * D]
        put_block(made, b, dot_tn(normed[...], part))
        copies.deliver(me_ref, made, layout, outs, b)
    copies.deliver(me_ref, made, layout, outs, 4)
    grad_normed = None
    for b in range(3):
        step = dot_nt(back[:, b * D : (b + 1) * D], column_block(held, b))
        grad_normed = step if grad_normed is None else grad_normed + step
    units = [normed_of(inputs[p][...].astype(F32)) for p in range(passes)]
    unit = jnp.concatenate([u[0] for u in units], axis=0)
    inverse = jnp.concatenate([u[1] for u in units], axis=0)
    if more:
        norm_ref[...] = jnp.zeros(norm_ref.shape, F32)
        for k, other in enumerate(others):
            norm_ref[2 * k + 2 : 2 * k + 4] = other[...]
    grad = norm_back(unit, inverse, gains[row : row + 1], grad_normed, norm_ref)
    grad_in[...] = grad_out[0:TOK] + grad[0:TOK]
    copies.store(grad_in, grad_in_ref)
    copies.finish()


GELU_SCALE = 0.7978845608028654
GELU_CUBE = 0.044715


def gelu_both(up):
    square = up * up
    bent = jnp.tanh(up * (GELU_SCALE + (GELU_SCALE * GELU_CUBE) * square))
    half = 0.5 + 0.5 * bent
    inner = 2.0 * GELU_SCALE + (6.0 * GELU_SCALE * GELU_CUBE) * square
    return up * half, half + up * (half - half * half) * inner


def ffn_grads(copies, place, layout, outs, gain, hidden, grad_low, normed, active, slope, norm_ref, held, made):
    for z in range(4):
        product = dot_tn(active[:, z * D : (z + 1) * D], grad_low)
        made[z, :, 4 * BLOCK : 8 * BLOCK] = product.astype(BF).reshape(4, 4 * BLOCK, D)
    copies.deliver(place, made, layout, outs, 2)
    copies.deliver(place, made, layout, outs, 3)
    grad_normed = None
    for b in range(4):
        cols = slice(b * D, (b + 1) * D)
        grad_active = dot_nt(grad_low, row_block(held, b))
        grad_up = (slope[:, cols].astype(F32) * grad_active).astype(BF)
        put_block(made, b, dot_tn(normed[...], grad_up))
        if b % 2 == 1:
            copies.deliver(place, made, layout, outs, b // 2)
        step = dot_nt(grad_up, column_block(held, b))
        grad_normed = step if grad_normed is None else grad_normed + step
    copies.deliver(place, made, layout, outs, 4)
    unit, inverse = normed_of(hidden)
    return norm_back(unit, inverse, gain, grad_normed, norm_ref)


def ffn_back_kernel(row, layout, me_ref, gains, *refs):
    taken, refs = refs[:5], refs[5:]
    pieces, refs = refs[: layout.pieces], refs[layout.pieces :]
    grad_in_ref, norm_ref, *refs = refs
    outs, refs = refs[: layout.made], refs[layout.made :]
    grad_in, held, made, hidden, grad_out, normed, active, slope, sems = refs
    copies = Copies(sems)
    grad_out = copies.load(taken[1], grad_out)
    active = copies.load(taken[3], active)
    loads = copies.fetch(me_ref, pieces, layout, held)
    slope = copies.load(taken[4], slope)
    normed = copies.load(taken[2], normed)
    hidden = copies.load(taken[0], hidden)
    grad_low = grad_out[...].astype(BF)
    active = active.arrive()
    for load in loads:
        load.arrive()
    hidden.arrive()
    grad = ffn_grads(
        copies, me_ref, layout, outs, gains[row : row + 1], hidden[...], grad_low, normed, active, slope, norm_ref, held, made
    )
    grad_in[...] = grad_out[...] + grad
    copies.store(grad_in, grad_in_ref)
    copies.finish()


def second_kernel(encoder, cross, me_ref, src_lengths, tgt_lengths, gains, *refs):
    taken, whole, refs = refs[:2], refs[2:4], refs[4:]
    sent, made, (held_enc, held_cross, hidden_enc, hidden_one, sems) = refs[:10], refs[10:20], refs[20:]
    normed_enc, active_enc, slope_enc, memory, normed, query, pair, probs, mixed, hidden = made
    copies = Copies(sems)
    hidden_enc = copies.load(taken[0], hidden_enc)
    loads_enc = copies.fetch(me_ref, whole[:1], encoder, held_enc)
    hidden_one = copies.load(taken[1], hidden_one)
    loads_cross = copies.fetch(me_ref, whole[1:], cross, held_cross)

    unit, unused = normed_of(hidden_enc[...])
    normed_enc[...] = (unit * gains[2:3] + gains[3:4]).astype(BF)
    copies.store(normed_enc, sent[0])
    unit, unused = normed_of(hidden_one[...])
    normed[...] = (unit * gains[6:7] + gains[7:8]).astype(BF)
    copies.store(normed, sent[4])
    loads_enc[0].arrive()
    for b in range(4):
        cols = slice(b * D, (b + 1) * D)
        grown, bent = gelu_both(dot(normed_enc[...], column_block(held_enc, b)))
        active_enc[:, cols] = grown.astype(BF)
        slope_enc[:, cols] = bent.astype(BF)
    copies.store(active_enc, sent[1])
    copies.store(slope_enc, sent[2])
    loads_enc[1].arrive()
    total = hidden_enc[...]
    for z in range(4):
        total = total + dot(active_enc[:, z * D : (z + 1) * D], row_block(held_enc, z))
    memory[...] = total.astype(BF)
    copies.store(memory, sent[3])

    loads_cross[0].arrive()
    query[...] = dot(normed[...], column_block(held_cross, 0)).astype(BF)
    copies.store(query, sent[5])
    pair[:, 0:D] = dot(memory[...], column_block(held_cross, 1)).astype(BF)
    loads_cross[1].arrive()
    pair[:, D : 2 * D] = dot(memory[...], column_block(held_cross, 2)).astype(BF)
    copies.store(pair, sent[6])
    bias = mask_bias(src_lengths, tgt_lengths)
    for p in range(2):
        rows = slice(p * TOK, (p + 1) * TOK)
        part = attend(query[rows], pair[:, 0:D], pair[:, D : 2 * D], bias, probs, p * HEADS)
        heads = pl.ds(p * HEADS, HEADS)
        copies.store(probs.at[heads], sent[7].at[heads])
        mixed[rows] = part
        hidden[rows] = hidden_one[rows] + dot(part, column_block(held_cross, 3))
    copies.store(mixed, sent[8])
    copies.store(hidden, sent[9])
    copies.finish()


def middle_kernel(cross, decoder, me_ref, gains, *refs):
    taken, whole, refs = refs[:10], refs[10:11], refs[11:]
    pieces, refs = refs[: decoder.pieces], refs[decoder.pieces :]
    norm_ffn, norm_cross, *refs = refs
    sent, refs = refs[:5], refs[5:]
    come, refs = refs[:10], refs[10:]
    held_cross, held, made_cross, made, first_out, second_out, grad_memory, grad_one, *refs = refs
    normed_two, active, slope, grad_two, back, sems = refs
    copies = Copies(sems)
    hidden = copies.load(taken[0], come[0])
    loads = copies.fetch(me_ref, pieces, decoder, held)
    cots = [copies.load(taken[k], come[k]) for k in (1, 2)]
    loads_cross = copies.fetch(me_ref, whole, cross, held_cross)
    mixed, probs, query, pair, normed, memory, hidden_one = (
        copies.load(taken[k], come[k]) for k in range(3, 10)
    )

    unit, unused = normed_of(hidden[...])
    normed_two[...] = (unit * gains[8:9] + gains[9:10]).astype(BF)
    loads[0].arrive()
    for b in range(4):
        cols = slice(b * D, (b + 1) * D)
        grown, bent = gelu_both(dot(normed_two[...], column_block(held, b)))
        active[:, cols] = grown.astype(BF)
        slope[:, cols] = bent.astype(BF)
    loads[1].arrive()
    total = hidden[...]
    for z in range(4):
        total = total + dot(active[:, z * D : (z + 1) * D], row_block(held, z))
    first_out[...] = total[0:TOK].astype(BF)
    second_out[...] = total[TOK:].astype(BF)
    copies.store(first_out, sent[0])
    copies.store(second_out, sent[1])
    grad_low = jnp.concatenate([cots[0][...], cots[1][...]], axis=0)
    grad = ffn_grads(
        copies, me_ref, decoder, sent[4:], gains[8:9], hidden[...], grad_low, normed_two, active, slope, norm_ffn, held, made
    )
    grad_two[...] = grad_low.astype(F32) + grad

    grad_low = grad_two[...].astype(BF)
    put_block(made_cross, 3, dot_tn(mixed[...], grad_low))
    copies.deliver(me_ref, made_cross, cross, sent[4:], 3)
    loads_cross[1].arrive()
    grad_mixed = dot_nt(grad_low, column_block(held_cross, 3)).astype(BF)
    grad_key = grad_value = None
    probs = probs.arrive()
    for p in range(2):
        rows = slice(p * TOK, (p + 1) * TOK)
        grads = attend_back(
            query[rows], pair[:, 0:D], pair[:, D : 2 * D], probs, p * HEADS, grad_mixed[rows]
        )
        back[rows] = grads[0].astype(BF)
        grad_key = grads[1] if grad_key is None else grad_key + grads[1]
        grad_value = grads[2] if grad_value is None else grad_value + grads[2]
    grad_key = grad_key.astype(BF)
    grad_value = grad_value.astype(BF)
    for b, (left, right) in enumerate(
        ((normed[...], back[...]), (memory[...], grad_key), (memory[...], grad_value))
    ):
        put_block(made_cross, b, dot_tn(left, right))
        copies.deliver(me_ref, made_cross, cross, sent[4:], b)
    loads_cross[0].arrive()
    grad_memory[...] = dot_nt(grad_key, column_block(held_cross, 1)) + dot_nt(
        grad_value, column_block(held_cross, 2)
    )
    copies.store(grad_memory, sent[2])
    grad_normed = dot_nt(back[...], column_block(held_cross, 0))
    unit, inverse = normed_of(hidden_one[...])
    grad = norm_back(unit, inverse, gains[6:7], grad_normed, norm_cross)
    grad_one[...] = grad_two[...] + grad
    copies.store(grad_one, sent[3])
    copies.finish()


ANY = pl.BlockSpec(memory_space=pl.ANY)
HB = pl.BlockSpec(memory_space=pltpu.HBM)
VM = pl.BlockSpec(memory_space=pltpu.VMEM)
SM = pl.BlockSpec(memory_space=pltpu.SMEM)


def held_of(blocks):
    return pltpu.VMEM((4, 4, blocks * BLOCK, D), BF)


def made_of(layout, blocks):
    if layout.made == 1:
        return [jax.ShapeDtypeStruct((4, 4, layout.made_rows, D), BF)]
    rows = blocks * BLOCK // (2 * layout.made)
    return [jax.ShapeDtypeStruct((2, 2, 4, 2, rows, D), BF)] * layout.made


def shape(rows, cols, dtype):
    return jax.ShapeDtypeStruct((rows, cols), dtype)


class Order:
    def __init__(self):
        self.token = None

    def tie(self, value):
        return self.tie_all([value])[0]

    def tie_all(self, values):
        arrays = list(values) + [self.token]
        *values, self.token = pl.pallas_call(
            nothing_kernel,
            name="tie",
            out_shape=[jax.ShapeDtypeStruct(x.shape, x.dtype) for x in arrays],
            in_specs=[HB] * len(arrays),
            out_specs=[HB] * len(arrays),
            input_output_aliases={k: k for k in range(len(arrays))},
            compiler_params=pltpu.CompilerParams(vmem_limit_bytes=VMEM_LIMIT),
        )(*arrays)
        return values


def nothing_kernel(*refs):
    pass


def call(order, body, name, in_specs, out_shape, out_specs, scratch, operands, micros, grid=None, inplace=()):
    inplace = list(inplace) + ([(order.token, len(out_shape))] if order.token is not None else [])
    count, more, outs = len(operands), len(inplace), len(out_shape)

    def ordered(*refs):
        body(*refs[:count], *refs[count + more : count + more + outs], *refs[count + more + outs + 1 :])

    aliases = {count + k: out for k, (unused, out) in enumerate(inplace)}
    *results, order.token = pl.pallas_call(
        ordered,
        name=name,
        out_shape=out_shape + [jax.ShapeDtypeStruct((8, 128), F32)],
        in_specs=in_specs + [HB] * more,
        out_specs=out_specs + [HB],
        input_output_aliases=aliases,
        scratch_shapes=scratch,
        compiler_params=pltpu.CompilerParams(vmem_limit_bytes=VMEM_LIMIT),
        cost_estimate=pl.CostEstimate(
            flops=int((micros + 0.01) * COST), bytes_accessed=0, transcendentals=0
        ),
        **({} if grid is None else {"grid": grid}),
    )(*operands, *(array for array, unused in inplace))
    return results


def vmem(rows, cols, dtype):
    return pltpu.VMEM((rows, cols), dtype)


def probs_of(count, scratch=False):
    dims = (count * HEADS, TOK, TOK)
    return pltpu.VMEM(dims, BF) if scratch else jax.ShapeDtypeStruct(dims, BF)


SEMS = pltpu.SemaphoreType.DMA((64,))


def arrays(items):
    return [jax.ShapeDtypeStruct(dims, dtype) for dims, dtype in items]


def buffers(items):
    return [pltpu.VMEM(dims, dtype) for dims, dtype in items]


def self_kept(count):
    rows = count * TOK
    return [
        ((rows, D), F32),
        ((rows, D), BF),
        ((rows, 3 * D), BF),
        ((count * HEADS, TOK, TOK), BF),
        ((rows, D), BF),
    ]


def self_forward(order, me, src_lengths, tgt_lengths, gains, inputs, decoder, encoder):
    kept = self_kept(2) + self_kept(1)
    results = call(
        order,
        functools.partial(self_forward_kernel, decoder[0], encoder[0]),
        "self_forward",
        [SM, SM, SM, ANY if decoder[0].pieces > 1 else VM] + [HB] * 3 + [ANY] * (decoder[0].pieces + encoder[0].pieces),
        arrays(kept) + [shape(16, D, F32)],
        [HB] * 10 + [VM],
        buffers(kept)
        + [held_of(4), held_of(4), pltpu.VMEM((2, 4, 2, 16, D), BF)]
        + [vmem(TOK, D, BF)] * 3
        + [SEMS],
        (me, src_lengths, tgt_lengths, gains, *inputs, *decoder[1], *encoder[1]),
        12,
    )
    return results[:5], results[5:10], results[10]


def second(order, me, src_lengths, tgt_lengths, gains, hidden_enc, hidden_one, encoder, cross):
    rows = 2 * TOK
    kept = [
        ((TOK, D), BF),
        ((TOK, FF), BF),
        ((TOK, FF), BF),
        ((TOK, D), BF),
        ((rows, D), BF),
        ((rows, D), BF),
        ((TOK, 2 * D), BF),
        ((2 * HEADS, TOK, TOK), BF),
        ((rows, D), BF),
        ((rows, D), F32),
    ]
    results = call(
        order,
        functools.partial(second_kernel, encoder[0], cross[0]),
        "second",
        [SM, SM, SM, VM] + [HB] * 2 + [ANY] * 2,
        arrays(kept),
        [HB] * 10,
        buffers(kept) + [held_of(8), held_of(4), vmem(TOK, D, F32), vmem(rows, D, F32), SEMS],
        (me, src_lengths, tgt_lengths, gains, hidden_enc, hidden_one, encoder[1][0], cross[1][0]),
        13,
    )
    return results[:3], results[3:]


def self_back(order, row, me, gains, inputs, grad_out, kept, pieces, others=()):
    count = len(inputs)
    rows = count * TOK
    return call(
        order,
        functools.partial(self_back_kernel, count, row, len(others), pieces[0]),
        "self_back",
        [SM, VM] + [VM] * len(others) + [HB] * count + [HB] * 5 + [ANY] * pieces[0].pieces,
        [shape(TOK, D, F32), shape(16 if others else 2, D, F32)] + made_of(pieces[0], 4),
        [HB, VM] + [HB] * pieces[0].made,
        [
            vmem(TOK, D, F32),
            held_of(4),
            held_of(4),
            vmem(rows, 3 * D, BF),
            vmem(rows, D, F32),
            vmem(rows, D, BF),
            vmem(rows, 3 * D, BF),
            probs_of(count, True),
            vmem(rows, D, BF),
        ]
        + [vmem(TOK, D, BF)] * count
        + [SEMS],
        (me, gains, *others, *inputs, grad_out, *kept, *pieces[1]),
        5.8 + 3.4 * count,
    )


def ffn_back(order, row, me, gains, hidden, grad_out, kept, pieces):
    return call(
        order,
        functools.partial(ffn_back_kernel, row, pieces[0]),
        "ffn_back",
        [SM, VM] + [HB] * 5 + [ANY] * pieces[0].pieces,
        [shape(TOK, D, F32), shape(2, D, F32)] + made_of(pieces[0], 8),
        [HB, VM] + [HB] * pieces[0].made,
        [
            vmem(TOK, D, F32),
            held_of(8),
            held_of(8),
            vmem(TOK, D, F32),
            vmem(TOK, D, F32),
            vmem(TOK, D, BF),
            vmem(TOK, FF, BF),
            vmem(TOK, FF, BF),
            SEMS,
        ],
        (me, gains, hidden, grad_out, *kept, *pieces[1]),
        10.2,
    )


def middle(order, me, gains, hidden_one, kept, cots, cross, decoder):
    rows = 2 * TOK
    memory, normed, query, pair, probs, mixed, hidden = kept
    taken = [hidden, *cots, mixed, probs, query, pair, normed, memory, hidden_one]
    sent = [((TOK, D), BF), ((TOK, D), BF), ((TOK, D), F32), ((rows, D), F32)]
    return call(
        order,
        functools.partial(middle_kernel, cross[0], decoder[0]),
        "middle",
        [SM, VM] + [HB] * 10 + [ANY] * (1 + decoder[0].pieces),
        [shape(2, D, F32)] * 2 + arrays(sent + [((4, 4, 384, D), BF)]),
        [VM] * 2 + [HB] * 5,
        buffers([(x.shape, x.dtype) for x in taken])
        + [held_of(4), held_of(8), held_of(4), held_of(8)]
        + buffers(sent)
        + [
            vmem(rows, D, BF),
            vmem(rows, FF, BF),
            vmem(rows, FF, BF),
            vmem(rows, D, F32),
            vmem(rows, D, BF),
            SEMS,
        ],
        (me, gains, *taken, cross[1][0], *decoder[1]),
        25,
    )


AXIS = "fsdp"
BOTH = ("dp", "fsdp")
SHARDS = 16


def route(target):
    pairs = []
    for i in range(2 * SHARDS):
        dp, z, y, core = target(i // 16, (i // 4) % 4, (i // 2) % 2, i % 2)
        pairs.append((i, dp * 16 + (z % 4) * 4 + y * 2 + core))
    return pairs


def to_core(x):
    return lax.ppermute(x, BOTH, route(lambda dp, z, y, core: (dp, z, y, 1 - core)))


def to_z(x, step):
    return lax.ppermute(x, BOTH, route(lambda dp, z, y, core: (dp, z + step, y, core)))


def to_z_pair(x, step):
    return lax.ppermute(x, BOTH, route(lambda dp, z, y, core: (dp, z ^ step, y, core)))


def to_y(x):
    return lax.ppermute(x, BOTH, route(lambda dp, z, y, core: (dp, z, 1 - y, core)))


def to_dp(x):
    return lax.ppermute(x, BOTH, route(lambda dp, z, y, core: (1 - dp, z, y, core)))


def to_yx(x):
    return lax.ppermute(
        x, BOTH, route(lambda dp, z, y, core: (dp, z, y ^ 1, core) if core == 0 else (dp ^ 1, z, y, core))
    )


def to_xy(x):
    return lax.ppermute(
        x, BOTH, route(lambda dp, z, y, core: (dp ^ 1, z, y, core) if core == 0 else (dp, z, y ^ 1, core))
    )


def blocks_of(shard):
    rows, cols = shard.shape
    split = shard.reshape(rows // BLOCK, BLOCK, cols // D, D)
    return split.transpose(2, 0, 1, 3).reshape(-1, BLOCK, D)


def shard_of(blocks, cols):
    wide = blocks.reshape(cols // D, -1, D)
    return wide.transpose(1, 0, 2).reshape(-1, cols)


def small(order, body, name, out, operands, scratch=(), in_specs=None, out_specs=None, micros=0, grid=None):
    return call(
        order,
        body,
        name,
        in_specs if in_specs is not None else [VM] * len(operands),
        [jax.ShapeDtypeStruct(dims, dtype) for dims, dtype in out],
        out_specs if out_specs is not None else [VM] * len(out),
        list(scratch),
        operands,
        micros,
        grid,
    )


def pack_kernel(*refs):
    weights, (one, two, three, place, norms) = refs[:15], refs[15:]
    spot = lax.axis_index(AXIS)
    place[0] = spot >> 2
    place[1] = (spot >> 1) & 1
    place[2] = lax.axis_index("dp")
    place[3] = spot & 1
    self_in, self_out, enc_in, enc_out, enc_ffn_in, enc_ffn_out = weights[:6]
    cross_q, cross_kv, cross_out, ffn_in, ffn_out = weights[6:11]
    for half in range(2):

        @pl.when(place[2] == half)
        def _():
            for k in range(2):
                quarter = 2 * half + k
                cols = slice(quarter * D, (quarter + 1) * D)
                one[k, 0:32] = self_out[...] if quarter == 3 else self_in[:, cols]
                one[k, 32:64] = enc_out[...] if quarter == 3 else enc_in[:, cols]
                for j in range(2):
                    block = 2 * quarter + j
                    rows = slice(j * BLOCK, (j + 1) * BLOCK)
                    cols = slice(block * D, (block + 1) * D)
                    part = slice((block - 4) * BLOCK, (block - 3) * BLOCK)
                    three[k, rows] = ffn_in[:, cols] if block < 4 else ffn_out[part]

    for block in range(4):
        rows = slice(block * BLOCK, (block + 1) * BLOCK)
        two[rows] = enc_ffn_in[:, block * D : (block + 1) * D]
    two[128:256] = enc_ffn_out[...]
    two[256:288] = cross_q[...]
    two[288:320] = cross_kv[:, 0:D]
    two[320:352] = cross_kv[:, D : 2 * D]
    two[352:384] = cross_out[...]
    norms[...] = jnp.zeros(norms.shape, F32)
    row = 0
    for gain, bias in (weights[11:13], weights[13:15]):
        for k in range(gain.shape[0]):
            norms[row : row + 1, 0:BLOCK] = gain[k : k + 1].astype(F32)
            norms[row + 1 : row + 2, 0:BLOCK] = bias[k : k + 1].astype(F32)
            row += 2
    for k in range(2):
        one[k, 64:80] = norms[...].astype(BF)


def pack(order, weights, norms):
    return small(
        order,
        pack_kernel,
        "pack",
        [((2, 80, D), BF), ((384, D), BF), ((2, 64, D), BF), ((4,), jnp.int32)],
        (*weights, *norms),
        [pltpu.VMEM((16, D), F32)],
        in_specs=[VM] * 15,
        out_specs=[VM] * 3 + [SM],
    )


def pair_kernel(place, *refs):
    core = place[3]
    for k in range(2):
        mine, near, pair = refs[2 * k], refs[2 * k + 1], refs[4 + k]
        pair[core] = mine[core]
        pair[1 - core] = near[core]


def pair_up(order, place, mine, near):
    operands = [x for both in zip(mine, near) for x in both]
    return small(
        order,
        pair_kernel,
        "pair_up",
        [(x.shape, x.dtype) for x in mine],
        (place, *operands),
        in_specs=[SM] + [VM] * 4,
    )


def stack_kernel(place, *refs):
    parts, (out, held, sems) = refs[:-3], refs[-3:]
    count = len(parts)
    loads = [pltpu.make_async_copy(parts[d], held.at[d], sems.at[d]) for d in range(count)]
    stores = [
        pltpu.make_async_copy(held.at[d], out.at[(place[0] + (4 - d)) & 3], sems.at[count + d])
        for d in range(count)
    ]
    for copy in loads:
        copy.start()
    for d in range(count):
        loads[d].wait()
        stores[d].start()
    wait_all(stores)


def stack(order, place, parts):
    dims = (len(parts),) + parts[0].shape
    dtype = parts[0].dtype
    return small(
        order,
        stack_kernel,
        "stack",
        [(dims, dtype)],
        (place, *parts),
        [pltpu.VMEM(dims, dtype), pltpu.SemaphoreType.DMA((2 * len(parts),))],
        [SM] + [ANY] * len(parts),
        [ANY],
    )[0]


class Gather:
    def __init__(self, order, pair):
        self.order, self.pair = order, pair

    def along_z(self):
        pair = self.order.tie(self.pair)
        self.parts = [pair] + [to_z(pair, d) for d in (1, 2, 3)]

    def lined(self, place):
        self.line = stack(self.order, place, self.parts)

    def first_cross(self):
        line = self.order.tie(self.line)
        self.own = [line, to_dp(line), to_y(line)]
        self.near = []

    def crossed(self, others=()):
        arrived = self.order.tie_all(self.own[1:3] + list(others[1:]))
        self.own[1:3] = arrived[:2]
        if others:
            others[1:] = arrived[2:]

    def second_cross(self):
        self.own.append(to_dp(self.own[2]))

    def share(self):
        self.near = [to_core(piece) for piece in self.own[:3]]

    def done(self):
        last, *self.near = self.order.tie_all([self.own[3]] + self.near)
        self.own = self.own[:3] + [last]
        self.near.append(self.order.tie(to_core(last)))
        self.pieces = tuple(self.own + self.near)


def low_sum(*parts):
    total = parts[0].astype(F32)
    for part in parts[1:]:
        total = total + part.astype(F32)
    return total.astype(BF)


class Span(typing.NamedTuple):
    group: int
    start: int
    size: int
    of: int
    place: int

    def within(self, block):
        return slice(block * self.of + self.start, block * self.of + self.start + self.size)

    def overall(self, block, rows):
        return slice(block * rows + self.place, block * rows + self.place + self.size)


def send_block(step, source, target, sems, more):
    def copies():
        for k in range(4):
            yield k, pltpu.make_async_copy(
                source.at[k], target.at[pl.ds(k * source.shape[1], source.shape[1])], sems.at[k]
            )

    last = pltpu.make_async_copy(*more, sems.at[4]) if more else None
    for k, copy in copies():
        pl.when(step == k)(copy.start)
    if last:
        pl.when(step == 0)(last.start)

    @pl.when(step == 3)
    def _():
        for unused, copy in copies():
            copy.wait()
        if last:
            last.wait()


def reduce_first_kernel(spans, norms, *refs):
    norm_parts, parts = refs[:norms], refs[norms : norms + 2 * len(spans)]
    sent, held, norm, sems = refs[-4:]
    step = pl.program_id(0)
    if norms:

        @pl.when(step == 0)
        def _():
            norm[...] = (norm_parts[0][...] + norm_parts[1][...]).astype(BF)

    for k, span in enumerate(spans):
        own, came = parts[2 * k], parts[2 * k + 1]
        for second in range(2):
            for core in range(2):
                held[step, span.within(2 * second + core)] = (
                    own[0, second, 0, core] + came[0, second, 0, core]
                )
    more = (norm, sent.at[pl.ds(16 * spans[0].of, 16)]) if norms else None
    send_block(step, held, sent, sems, more)


def reduce_second_kernel(spans, groups, norm_own, norm_came, *refs):
    came_first, refs = refs[:groups], refs[groups:]
    parts, refs = refs[: 2 * len(spans)], refs[2 * len(spans) :]
    sent, held, (norm, *sems) = refs[:groups], refs[groups : 2 * groups], refs[2 * groups :]
    step = pl.program_id(0)

    @pl.when(step == 0)
    def _():
        norm[...] = (norm_own[...].astype(F32) + norm_came[...].astype(F32)).astype(BF)

    for k, span in enumerate(spans):
        own, came = parts[2 * k], parts[2 * k + 1]
        for core in range(2):
            rows = span.within(core)
            held[span.group][step, rows] = low_sum(
                own[0, 0, 0, core], came[0, 0, 0, core], came_first[span.group][rows]
            )
    for k in range(groups):
        size = 4 * held[k].shape[1]
        more = (norm, sent[k].at[pl.ds(size, 16)]) if k == groups - 1 else None
        send_block(step, held[k], sent[k], sems[k], more)


def reduce_third_kernel(spans, groups, norm_own, norm_came, place, *refs):
    came_first, came_second, refs = refs[:groups], refs[groups : 2 * groups], refs[2 * groups :]
    parts, outs = refs[:-4], refs[-4:]
    norm = (norm_own[...].astype(F32) + norm_came[...].astype(F32)).astype(BF)
    rows = (outs[0].shape[0] - 16) // 2
    for d in range(4):
        z = (place[0] + d) & 3
        outs[d][2 * rows :] = norm
        for k, span in enumerate(spans):
            own, came = parts[2 * k], parts[2 * k + 1]
            for core in range(2):
                start = span.within(core).start
                first = pl.multiple_of(z * 4 * span.of + start, 16)
                second = pl.multiple_of(z * 2 * span.of + start, 16)
                outs[d][span.overall(core, rows)] = low_sum(
                    own[0, 0, z, core],
                    came[0, 0, z, core],
                    came_first[span.group][pl.ds(first, span.size)],
                    came_second[span.group][pl.ds(second, span.size)],
                )


def reduce_fourth_kernel(a, b, c, d, out, norm):
    rows = out.shape[1]
    for core in range(2):
        span = slice(core * rows, (core + 1) * rows)
        out[core] = low_sum(a[span], b[span], c[span], d[span])
    total = a[2 * rows :].astype(F32)
    for part in (b, c, d):
        total = total + part[2 * rows :].astype(F32)
    norm[...] = total


class Reduce:
    def __init__(self, order):
        self.order, self.own, self.came = order, [], []
        self.spans, self.sent, self.first_came, self.rows = [], [], [], 0

    def add(self, own, other):
        self.own.append(own)
        self.came.append(to_core(self.order.tie(other)))

    def arrive(self):
        self.came[-1] = self.order.tie(self.came[-1])

    def start_norm(self, norm):
        self.norm = self.order.tie(norm)
        self.norm_came = to_core(self.norm)

    def run(self, body, name, dims, operands, in_specs, part_spec, out_specs=None, scratch=(), grid=(4,), start=0):
        parts = [x for both in zip(self.own[start:], self.came[start:]) for x in both]
        specs = [pl.BlockSpec(part_spec[0] + (part.shape[4], D), part_spec[1]) for part in parts]
        sent = small(
            self.order,
            body,
            name,
            [(item, BF) for item in dims],
            operands + parts,
            scratch,
            in_specs=in_specs + specs,
            out_specs=out_specs or [HB] * len(dims),
            grid=grid,
        )
        return [self.order.tie(x) for x in sent]

    def held(self, dims):
        return buffers([(dims, BF), ((16, D), BF)]) + [pltpu.SemaphoreType.DMA((5,))]

    def first(self, norms=(), route=None):
        start = len(self.spans)
        sizes = [own.shape[4] for own in self.own[start:]]
        rows, row, spans = sum(sizes), 0, []
        for size in sizes:
            spans.append(Span(len(self.sent), row, size, rows, self.rows + row))
            row += size
        self.spans += spans
        self.rows += rows
        (sent,) = self.run(
            functools.partial(reduce_first_kernel, spans, len(norms)),
            "reduce_first",
            [(16 * rows + (16 if norms else 0), D)],
            list(norms),
            [pl.BlockSpec((16, D), lambda i: (0, 0))] * len(norms),
            ((1, 2, 1, 2), lambda i: (1, 0, i, 0, 0, 0)),
            scratch=self.held((4, 4 * rows, D)),
            start=start,
        )
        self.sent.append(sent)
        self.first_came.append((route or to_yx)(sent))

    def last_rows(self, array):
        block = array.shape[0] // 16 - 1
        return pl.BlockSpec((16, D), lambda i: (block, 0))

    def second(self, *routes):
        groups = len(self.sent)
        sizes = [self.spans[[span.group for span in self.spans].index(k)].of for k in range(groups)]
        scratch = buffers([((4, 2 * size, D), BF) for size in sizes] + [((16, D), BF)])
        self.second_sent = self.run(
            functools.partial(reduce_second_kernel, self.spans, groups),
            "reduce_second",
            [(8 * size + (16 if k == groups - 1 else 0), D) for k, size in enumerate(sizes)],
            [self.sent[-1], self.first_came[-1]] + self.first_came,
            [self.last_rows(self.sent[-1])] * 2
            + [pl.BlockSpec((2 * size, D), lambda i: (2 * i + 1, 0)) for size in sizes],
            ((1, 1, 1, 2), lambda i: (0, 1, i, 0, 0, 0)),
            scratch=scratch + [pltpu.SemaphoreType.DMA((5,))] * groups,
        )
        self.second_came = [route(sent) for route, sent in zip(routes, self.second_sent)]

    def third(self, place):
        rows = self.rows
        came = self.first_came + self.second_came
        parts = self.run(
            functools.partial(reduce_third_kernel, self.spans, len(self.sent)),
            "reduce_third",
            [(2 * rows + 16, D)] * 4,
            [self.second_sent[-1], self.second_came[-1], place] + came,
            [self.last_rows(self.second_sent[-1])] * 2
            + [SM]
            + [pl.BlockSpec(x.shape, lambda i: (0, 0)) for x in came],
            ((1, 1, 4, 2), lambda i: (0, 0, 0, 0, 0, 0)),
            [pl.BlockSpec((2 * rows + 16, D), lambda i: (0, 0))] * 4,
            grid=(1,),
        )
        self.lines = [parts[0]] + [to_z(parts[d], d) for d in (1, 2, 3)]

    def fourth(self):
        total, self.norm = small(
            self.order,
            reduce_fourth_kernel,
            "reduce_fourth",
            [((2, self.rows, D), BF), ((16, D), F32)],
            self.lines,
        )
        total = self.order.tie(total)
        self.ends = [total, to_dp(total), to_core(total)]

    def last(self):
        near = self.order.tie(self.ends[2])
        came = self.order.tie(self.ends[1])
        self.ends = [self.ends[0], came, near, to_core(came)]


def quarter_of(place, ends, quarter, rows):
    core = place[3]
    half, which = quarter >> 1, quarter & 1
    first = jnp.where(place[3] == which, ends[0][core, rows], ends[2][core, rows].astype(BF))
    second = jnp.where(place[3] == which, ends[1][core, rows], ends[3][core, rows])
    return jnp.where(place[2] == half, first, second).astype(F32)


def unpack_kernel(layout, place, *refs):
    ends, outs = refs[:4], refs[4:]
    first = 0
    for kind, row in layout:
        for quarter in range(4):
            if kind == "ffn":
                for j in range(2):
                    block = 2 * quarter + j
                    rows = slice(row + j * BLOCK, row + (j + 1) * BLOCK)
                    value = quarter_of(place, ends, quarter, rows)
                    if block < 4:
                        outs[first][:, block * D : (block + 1) * D] = value
                    else:
                        outs[first + 1][(block - 4) * BLOCK : (block - 3) * BLOCK] = value
            else:
                value = quarter_of(place, ends, quarter, slice(row, row + BLOCK))
                if kind == "attn":
                    if quarter < 3:
                        outs[first][:, quarter * D : (quarter + 1) * D] = value
                    else:
                        outs[first + 1][...] = value
                elif quarter in (1, 2):
                    outs[first + 1][:, (quarter - 1) * D : quarter * D] = value
                else:
                    outs[first + (quarter + 1) // 2][...] = value
        first += 3 if kind == "cross" else 2


SHARD_SHAPES = {
    "ffn": [((BLOCK, FF), F32), ((4 * BLOCK, D), F32)],
    "attn": [((BLOCK, 3 * D), F32), ((BLOCK, D), F32)],
    "cross": [((BLOCK, D), F32), ((BLOCK, 2 * D), F32), ((BLOCK, D), F32)],
}


def unpack(order, place, ends, layout):
    return small(
        order,
        functools.partial(unpack_kernel, layout),
        "unpack",
        [item for kind, unused in layout for item in SHARD_SHAPES[kind]],
        (place, *ends),
        in_specs=[SM] + [VM] * 4,
    )


def norm_last_kernel(place, total, *outs):
    total = total[...]
    spot = place[0] * 4 + place[1] * 2 + place[3]
    turned = jnp.zeros((16, BLOCK), F32)
    for k in range(SHARDS):
        turned = jnp.where(spot == k, total[:, k * BLOCK : (k + 1) * BLOCK], turned)
    for first, gain, bias in ((0, outs[0], outs[1]), (4, outs[2], outs[3])):
        for k in range(gain.shape[0]):
            gain[k : k + 1] = turned[first + 2 * k : first + 2 * k + 1]
            bias[k : k + 1] = turned[first + 2 * k + 1 : first + 2 * k + 2]


def norm_last(order, place, total):
    return small(
        order,
        norm_last_kernel,
        "norm_last",
        [((2, BLOCK), F32), ((2, BLOCK), F32), ((3, BLOCK), F32), ((3, BLOCK), F32)],
        (place, total),
        in_specs=[SM, VM],
    )


def spread_kernel(own, came, ffn_in, ffn_out, cross_q, cross_kv, cross_out):
    total = own[...].astype(F32) + came[...].astype(F32)
    for block in range(4):
        ffn_in[:, block * D : (block + 1) * D] = total[block * BLOCK : (block + 1) * BLOCK]
    ffn_out[...] = total[128:256]
    cross_q[...] = total[256:288]
    cross_kv[:, 0:D] = total[288:320]
    cross_kv[:, D : 2 * D] = total[320:352]
    cross_out[...] = total[352:384]


def spread(order, own, came):
    return small(
        order,
        spread_kernel,
        "spread",
        SHARD_SHAPES["ffn"] + SHARD_SHAPES["cross"],
        (own, came),
    )


def gather_plain(weights):
    parts = []
    for weight in weights:
        whole = lax.all_gather(weight, AXIS, axis=0, tiled=True)
        parts.append(jax.vmap(blocks_of)(whole.reshape(SHARDS, -1, whole.shape[1])))
    return jnp.concatenate(parts, axis=1).reshape(4, 4, -1, D)


def reduce_plain(made, columns):
    shards = made.reshape(SHARDS, -1, BLOCK, D)
    grads = []
    for first, last, cols in columns:
        whole = jax.vmap(functools.partial(shard_of, cols=cols))(shards[:, first:last])
        whole = whole.reshape(-1, cols).astype(F32)
        part = lax.psum_scatter(whole, AXIS, scatter_dimension=0, tiled=True)
        grads.append(lax.psum(part.astype(BF), "dp").astype(F32))
    return grads


def norm_rows_of(gain_enc, bias_enc, gain_dec, bias_dec):
    rows = []
    for gain, bias in ((gain_enc, bias_enc), (gain_dec, bias_dec)):
        for k in range(gain.shape[0]):
            rows += [gain[k : k + 1], bias[k : k + 1]]
    return jnp.concatenate(rows, axis=0)


ATTN_COLUMNS = ((0, 3, 3 * D), (3, 4, D))
FFN_COLUMNS = ((0, 4, FF), (4, 8, D))
CROSS_COLUMNS = ((0, 1, D), (1, 3, 2 * D), (3, 4, D))


def step(
    custom,
    source,
    first_in,
    second_in,
    cot_first,
    cot_second,
    src_lengths,
    tgt_lengths,
    enc_attn_in,
    enc_attn_out,
    enc_ffn_in,
    enc_ffn_out,
    enc_gain,
    enc_bias,
    dec_self_in,
    dec_self_out,
    dec_cross_q,
    dec_cross_kv,
    dec_cross_out,
    dec_ffn_in,
    dec_ffn_out,
    dec_gain,
    dec_bias,
):
    order = Order()
    group_self = (dec_self_in, dec_self_out)
    group_enc = (enc_attn_in, enc_attn_out)
    group_enc_ffn = (enc_ffn_in, enc_ffn_out)
    group_cross = (dec_cross_q, dec_cross_kv, dec_cross_out)
    group_ffn = (dec_ffn_in, dec_ffn_out)
    if custom:
        weights = group_self + group_enc + group_enc_ffn + group_cross + group_ffn
        mine_one, mine_two, mine_three, place = pack(
            order, weights, (enc_gain, enc_bias, dec_gain, dec_bias)
        )
        mine = (mine_one, mine_three)
        pairs = pair_up(order, place, mine, [to_core(x) for x in mine])
        one, three = (Gather(order, pair) for pair in pairs)
        one.along_z()
        one.parts[3] = order.tie(one.parts[3])
        mine_two = order.tie(mine_two)
        whole = lax.all_gather(mine_two, AXIS, axis=0, tiled=True).reshape(4, 4, -1, D)
        one.lined(place)
        one.first_cross()
        three.along_z()
        one.crossed(three.parts)
        one.second_cross()
        three.lined(place)
        three.first_cross()
        one.share()
        one.done()
        gains = first_in
        w_self, w_enc = (Layout(0, 8), one.pieces), (Layout(32, 8), one.pieces)
        w_enc_ffn = (Layout(0, 1, 4), (whole,))
        w_cross = (Layout(256, 1, 1, 256, 384), (whole,))
    else:
        place = jnp.zeros((4,), jnp.int32)
        w_self, w_enc, w_enc_ffn = (
            (Layout(0, 1, 1, 0, rows), (gather_plain(group),))
            for group, rows in ((group_self, 128), (group_enc, 128), (group_enc_ffn, 256))
        )
        w_cross = (Layout(0, 1, 1, 256, 384), (gather_plain(group_cross),))
        w_ffn = (Layout(0, 1, 1, 0, 384), (gather_plain(group_ffn),))
        norm_rows = norm_rows_of(enc_gain, enc_bias, dec_gain, dec_bias)
        gains = lax.all_gather(norm_rows, AXIS, axis=1, tiled=True)
        gains = jnp.pad(gains.astype(F32), ((0, 6), (0, 0)))

    (hidden_one, *kept_self), (hidden_enc, *kept_enc), gains = self_forward(
        order, place, src_lengths, tgt_lengths, gains, [first_in, second_in, source], w_self, w_enc
    )
    if custom:
        three.crossed()
        three.second_cross()
        three.share()
    kept_enc_ffn, kept_cross = second(
        order, place, src_lengths, tgt_lengths, gains, hidden_enc, hidden_one, w_enc_ffn, w_cross
    )
    if custom:
        three.done()
        w_ffn = (Layout(0, 8, 1, 0, 384), three.pieces)
    norm_ffn, norm_cross, first_out, second_out, grad_memory, grad_one, made = middle(
        order, place, gains, hidden_one, kept_cross, (cot_first, cot_second), w_cross, w_ffn
    )
    if custom:
        scattered = lax.psum_scatter(
            made.reshape(-1, D), AXIS, scatter_dimension=0, tiled=True
        )
    grad_enc, norm_enc_ffn, *made_enc_ffn = ffn_back(
        order, 2, place, gains, hidden_enc, grad_memory, kept_enc_ffn, w_enc_ffn
    )
    if custom:
        red = Reduce(order)
        red.add(*made_enc_ffn[:2])
        came = to_core(order.tie(made_enc_ffn[3]))
    grad_first, norm_self, *made_self = self_back(
        order, 4, place, gains, [first_in, second_in], grad_one, kept_self, w_self
    )
    if custom:
        red.arrive()
        red.first((), to_dp)
        red.own.append(made_enc_ffn[2])
        red.came.append(order.tie(came))
        red.add(*made_self)
    grad_source, norm_total, *made_enc = self_back(
        order,
        0,
        place,
        gains,
        [source],
        grad_enc,
        kept_enc,
        w_enc,
        (norm_enc_ffn, norm_self, norm_cross, norm_ffn),
    )
    if custom:
        red.first_came[0] = order.tie(red.first_came[0])
        red.arrive()
        red.add(*made_enc)
        red.start_norm(norm_total)
        red.first((red.norm, red.norm_came))
        red.second(to_y, to_xy)
        red.third(place)
        scattered = order.tie(scattered)
        scattered_came = order.tie(to_dp(scattered))
        red.fourth()
        grads_ffn_cross = spread(order, scattered, scattered_came)
        norm_grads = norm_last(order, place, red.norm)
        red.last()
        grads_ffn, grads_cross = grads_ffn_cross[:2], grads_ffn_cross[2:]
        g = unpack(order, place, red.ends, (("ffn", 0), ("attn", 64), ("attn", 96)))
        grads_enc_ffn, grads_self, grads_enc = g[:2], g[2:4], g[4:6]
    else:
        grads_ffn = reduce_plain(made[:, :, 0:256], FFN_COLUMNS)
        grads_cross = reduce_plain(made[:, :, 256:384], CROSS_COLUMNS)
        grads_enc_ffn = reduce_plain(*made_enc_ffn, FFN_COLUMNS)
        grads_self = reduce_plain(*made_self, ATTN_COLUMNS)
        grads_enc = reduce_plain(*made_enc, ATTN_COLUMNS)
        norm_shard = lax.psum_scatter(norm_total, AXIS, scatter_dimension=1, tiled=True)
        norm_shard = lax.psum(norm_shard.astype(BF), "dp").astype(F32)
        norm_grads = (norm_shard[0:4:2], norm_shard[1:4:2], norm_shard[4:10:2], norm_shard[5:10:2])
    return (
        first_out,
        second_out,
        grad_source,
        grad_first,
        *grads_enc,
        *grads_enc_ffn,
        *norm_grads[:2],
        *grads_self,
        *grads_cross,
        *grads_ffn,
        *norm_grads[2:],
    )


def solution(mesh):
    blocked = P(("dp", "fsdp"), None)
    rows = P("fsdp", None)
    columns = P(None, "fsdp")
    custom = mesh.shape["fsdp"] == SHARDS and mesh.shape["dp"] == 2
    return jax.shard_map(
        functools.partial(step, custom),
        mesh=mesh,
        in_specs=(blocked,) * 7 + (rows,) * 4 + (columns,) * 2 + (rows,) * 7 + (columns,) * 2,
        out_specs=(blocked,) * 4 + (rows,) * 4 + (columns,) * 2 + (rows,) * 7 + (columns,) * 2,
        check_vma=False,
    )
```
